32 devices in a mesh: lev: 4 (over z), wave: 8 (over y, x, core).
Axes of the slice: x: 2, y: 2, z: 4, core: 2. Of those that a mesh axis runs over, the one named last changes fastest.
Arguments:
- legendre: float32 [320, 16, 641], P('wave'), may hold values from -0.25 to 0.25
- spectral: float32 [320, 8, 2, 641], P('wave', 'lev'), may hold values from -0.12 to 0.12
- pair_low: int32 [320], replicated, may hold values from 0 to 319, each once
- dep_lat: int32 [320], P('wave'), may hold values from 0 to 14, as said below
- dep_col: int32 [320], P('wave'), may hold values from 0 to 1279, as said below
- lon_steps: int32 [320, 128], P('wave'), may hold values from 0 to 24
- tilt_steps: int32 [320, 128], P('wave'), may hold values from 0 to 15
Outputs:
- grid_field: float32 [8, 32, 1280], P('lev', 'wave')
- departed: float32 [8, 32, 1280], P('lev', 'wave')
The draws below stay inside these ranges and needn't reach their ends.
Inputs may be any that keep to these rules, and one draw needn't show every extreme that they name: dep_lat lies between the arrival block's own latitude index in its hemisphere minus 2 and that index plus 1, clipped to the band. dep_col is the arrival block's first column plus -3 to 3, modulo 1280.
All inputs are finite; a program needn't handle non-finite values.
Results may differ from the reference program's by a relative error of at most 0.0003.
Values sent between devices are 32-bit elements; how exact they have to be, the bound alone decides.
No kernel may reach another device: no remote copies, remote signals or barrier semaphores. Data moves between devices by JAX's collectives and lax.ppermute only.
A program may use at most 64 MiB of HBM per device.

```python
import math
import jax
import jax.numpy as jnp
from jax import lax

M = 640
NLON = 1280
WAVENUMBER_PAIRS = 320
PAIR_SLOTS = 641
PAIRS_DEV = 2
BLK = 128
NORTH_LATITUDES = 16
ROWS = 4
NROWS = 32
LEVEL_FIELDS = 8
BLOCKS_ALL = 320
N_WAVE = 8


def draw_dep_lat(key, part):
    block_ids = jnp.arange(BLOCKS_ALL, dtype=jnp.int32)
    arrival_rows = block_ids * BLK // NLON
    own_lat = arrival_rows // ROWS * PAIRS_DEV + arrival_rows % PAIRS_DEV
    lat_step = jax.random.randint(jax.random.fold_in(key, 21), (BLOCKS_ALL,), -2, 2)
    return jnp.clip(own_lat + lat_step, 0, NORTH_LATITUDES - 2).astype(jnp.int32)


def draw_dep_col(key, part):
    block_ids = jnp.arange(BLOCKS_ALL, dtype=jnp.int32)
    first_col = block_ids * BLK % NLON
    col_step = jax.random.randint(jax.random.fold_in(key, 31), (BLOCKS_ALL,), -3, 4)
    return ((first_col + col_step) % NLON).astype(jnp.int32)


def touch_ends(entries, stream_key, smallest, largest):
    dims = entries.shape
    index_at = [jax.random.randint(jax.random.fold_in(stream_key, axis), (), 0, dims[axis]) for axis in range(len(dims))]
    entries = entries.at[tuple(index_at)].set(smallest)
    longest = dims.index(max(dims))
    index_at[longest] = (index_at[longest] + 1) % dims[longest]
    return entries.at[tuple(index_at)].set(largest)


def levels(key, dims, cuts, least, top_value):
    def one(dim, parts):
        heights = jax.random.uniform(jax.random.fold_in(jax.random.fold_in(key, 6), dim), (parts,), jnp.float32, least / len(cuts), top_value / len(cuts))
        return jnp.repeat(jnp.exp(heights), dims[dim] // parts).reshape((-1,) + (1,) * (len(dims) - dim - 1))

    loudness = one(*cuts[0])
    for cut in cuts[1:]:
        loudness = loudness * one(*cut)
    return loudness


def normal_values(own_key, dims, deviation, bound, split=(), kind=jnp.bfloat16):
    array = deviation * jax.random.normal(own_key, dims, jnp.float32)
    if split:
        array = array * levels(own_key, dims, split, -0.22, 0.18)
    return jnp.clip(array, -bound, bound).astype(kind)


def setup_inputs(seed: int = 0) -> dict:
    key_of = jax.random.split(jax.random.key(seed), 8)
    return {
        "legendre": normal_values(key_of[0], (WAVENUMBER_PAIRS, NORTH_LATITUDES, PAIR_SLOTS), PAIR_SLOTS ** -0.5, 0.25, ((0, 8),), jnp.float32),
        "spectral": normal_values(key_of[1], (WAVENUMBER_PAIRS, LEVEL_FIELDS, 2, PAIR_SLOTS), 0.02, 0.12, ((0, 8), (1, 4)), jnp.float32),
        "pair_low": jax.random.permutation(key_of[2], WAVENUMBER_PAIRS).astype(jnp.int32),
        "dep_lat": draw_dep_lat(jax.random.fold_in(key_of[7], 71), 0),
        "dep_col": draw_dep_col(jax.random.fold_in(key_of[7], 71), 0),
        "lon_steps": touch_ends(jax.random.randint(key_of[5], (BLOCKS_ALL, BLK), 0, 25), jax.random.fold_in(key_of[5], 1), 0, 24).astype(jnp.int32),
        "tilt_steps": touch_ends(jax.random.randint(key_of[6], (BLOCKS_ALL, BLK), 0, 16), jax.random.fold_in(key_of[6], 1), 0, 15).astype(jnp.int32),
    }


highest = lax.Precision.HIGHEST


def slot_masks(lower_wave, wavenumber_count, slot_count):
    slot_pos = jnp.arange(slot_count, dtype=jnp.int32)[None, :]
    first_len = wavenumber_count - lower_wave[:, None]
    second = slot_pos >= first_len
    offset = jnp.where(second, slot_pos - first_len, slot_pos)
    parity = offset % 2
    member = second.astype(jnp.int32)
    pieces = []
    for member_id in range(2):
        for parity_split in range(2):
            pieces.append(((member == member_id) & (parity == parity_split)).astype(jnp.float32))
    stacked = jnp.stack(pieces, axis=1)
    return stacked.reshape(lower_wave.shape[0], 2, 2, slot_count)


def fourier_rows(matrix, lower_wave, wavenumber_count):
    lon_count = 2 * wavenumber_count
    wave_table = jnp.stack([lower_wave, wavenumber_count - 1 - lower_wave], axis=0)
    gaussian_weights = jnp.where(wave_table == 0, 1.0, 2.0).astype(jnp.float32)
    lon_block = 512 if lon_count % 512 == 0 else 128

    def one_block(first_lon):
        lon_ids = first_lon + jnp.arange(lon_block, dtype=jnp.int32)
        phases = (wave_table[:, :, None] * lon_ids[None, None, :]) % lon_count
        angles = phases.astype(jnp.float32) * (2.0 * math.pi / lon_count)
        dft_table = jnp.stack([gaussian_weights[:, :, None] * jnp.cos(angles), -gaussian_weights[:, :, None] * jnp.sin(angles)], axis=1)
        dft_table = dft_table.reshape(4 * lower_wave.shape[0], lon_block)
        return jnp.dot(matrix, dft_table, precision=highest, preferred_element_type=jnp.float32)

    block_starts = jnp.arange(lon_count // lon_block, dtype=jnp.int32) * lon_block
    blocks = lax.map(one_block, block_starts)
    return jnp.moveaxis(blocks, 0, 1).reshape(matrix.shape[0], lon_count)


def mix_corners(flat_field, row_lo, row_hi, col_lo, col_hi, lon_frac, lat_frac, lon_count):
    def lookup(row_sel, col_sel):
        return jnp.take(flat_field, row_sel * lon_count + col_sel, axis=-1)

    lower_row = (1.0 - lon_frac) * lookup(row_lo, col_lo) + lon_frac * lookup(row_lo, col_hi)
    upper_row = (1.0 - lon_frac) * lookup(row_hi, col_lo) + lon_frac * lookup(row_hi, col_hi)
    return (1.0 - lat_frac) * lower_row + lat_frac * upper_row


def reference(legendre, spectral, pair_low, dep_lat, dep_col, lon_steps, tilt_steps):
    slot_count = M + 1
    slot_mask = slot_masks(pair_low, M, slot_count)

    def per_pair(pair_items):
        coeffs, table_rows, mask_rows = pair_items
        level_count = coeffs.shape[0]
        masked = coeffs[:, :, None, None, :] * mask_rows[None, None, :, :, :]
        masked = masked.reshape(level_count * 8, slot_count)
        halves = jnp.dot(masked, table_rows.T, precision=highest, preferred_element_type=jnp.float32)
        halves = halves.reshape(level_count, 2, 2, 2, table_rows.shape[0])
        northern = halves[:, :, :, 0] + halves[:, :, :, 1]
        southern = halves[:, :, :, 0] - halves[:, :, :, 1]
        return jnp.stack([northern, southern], axis=3)

    results = lax.map(per_pair, (spectral, legendre, slot_mask))
    arranged = results.transpose(1, 4, 5, 3, 2, 0)
    arranged = arranged.reshape(LEVEL_FIELDS, 2, N_WAVE, PAIRS_DEV, 2, 2, WAVENUMBER_PAIRS)
    arranged = arranged.transpose(0, 2, 1, 3, 4, 5, 6).reshape(LEVEL_FIELDS * NROWS, 4 * WAVENUMBER_PAIRS)
    grid_field = fourier_rows(arranged, pair_low, M).reshape(LEVEL_FIELDS, NROWS, NLON)

    block_ids = jnp.arange(BLOCKS_ALL, dtype=jnp.int32)
    arrival_rows = (block_ids * BLK) // NLON
    hemisphere = (arrival_rows % ROWS) // PAIRS_DEV

    def row_of(lat_ids):
        return (lat_ids // PAIRS_DEV) * ROWS + hemisphere * PAIRS_DEV + lat_ids % PAIRS_DEV

    row_lo = row_of(dep_lat)[:, None]
    row_hi = row_of(dep_lat + 1)[:, None]
    quarters = 4 * (dep_col[:, None] + jnp.arange(BLK, dtype=jnp.int32)[None, :]) + lon_steps - 12
    col_lo = (quarters // 4) % NLON
    col_hi = (col_lo + 1) % NLON
    lon_frac = (quarters % 4).astype(jnp.float32) * 0.25
    lat_frac = (tilt_steps % 4).astype(jnp.float32) * 0.25

    def one_level(level_field):
        flat_field = level_field.reshape(NROWS * NLON)
        return mix_corners(flat_field, row_lo, row_hi, col_lo, col_hi, lon_frac, lat_frac, NLON)

    horizontal = lax.map(one_level, grid_field)
    upper_level = jnp.concatenate([horizontal[1:], horizontal[-1:]], axis=0)
    vertical = (tilt_steps // 4).astype(jnp.float32) * 0.25
    departed = (1.0 - vertical) * horizontal + vertical * upper_level
    return grid_field, departed.reshape(LEVEL_FIELDS, NROWS, NLON)
```

```python
import functools
import math

import jax
import jax.numpy as jnp
import ml_dtypes
import numpy as np
from jax import lax
from jax.experimental import pallas as pl
from jax.experimental.pallas import tpu as pltpu
from jax.sharding import PartitionSpec as P

LANES = 128
GROUP = 8
HALO = 2
NT = (((1,), (1,)), ((), ()))
NN = (((1,), (0,)), ((), ()))


def split(value):
    high = value.astype(jnp.bfloat16)
    low = (value - high.astype(jnp.float32)).astype(jnp.bfloat16)
    return high, low


def legendre_kernel(slot_count, lat_dev, first_ref, spec_ref, leg_ref, out_ref):
    group, lat_all, width = leg_ref.shape
    level_count = spec_ref.shape[1]
    slot_pos = lax.broadcasted_iota(jnp.int32, (group, width), 1)
    inside = slot_pos < slot_count
    first_len = first_ref[:, 0:1]
    second = slot_pos >= first_len
    offset = jnp.where(second, slot_pos - first_len, slot_pos)
    sign = (1 - 2 * (offset & 1)).astype(jnp.float32)
    pieces = []
    for part in range(2):
        for level in range(level_count):
            row = jnp.where(inside, spec_ref[:, level, part, :], 0.0)
            for hemi in range(2):
                signed = row * sign if hemi else row
                pieces.append(jnp.where(second, 0.0, signed))
                pieces.append(jnp.where(second, signed, 0.0))
    columns = jnp.concatenate(split(jnp.concatenate(pieces, axis=0)), axis=0)
    count = group * len(pieces)
    table_pos = lax.broadcasted_iota(jnp.int32, (group * lat_all, width), 1)
    table = jnp.where(table_pos < slot_count, leg_ref[...].reshape(group * lat_all, width), 0.0)
    rows = jnp.concatenate(split(table), axis=0)
    crossed = lax.dot_general(rows, columns, NT, preferred_element_type=jnp.float32)
    half = group * lat_all
    crossed = (crossed[:half, :count] + crossed[:half, count:]) + (
        crossed[half:, :count] + crossed[half:, count:]
    )
    slot_of_lane = lax.broadcasted_iota(jnp.int32, (lat_all, count), 1) % group
    sums = jnp.zeros((lat_all, count), jnp.float32)
    for slot in range(group):
        block = crossed[slot * lat_all : (slot + 1) * lat_all]
        sums = jnp.where(slot_of_lane == slot, block, sums)
    edge = jnp.zeros((HALO, count), jnp.float32)
    tail = jnp.zeros((2 * HALO, count), jnp.float32)
    padded = jnp.concatenate([edge, sums, tail], axis=0)
    for dest in range(out_ref.shape[0]):
        out_ref[dest] = padded[dest * lat_dev : dest * lat_dev + out_ref.shape[1]]


def legendre_sums(spectral, legendre, first_len, slot_count, wave_size):
    slots, level_count = spectral.shape[:2]
    lat_all = legendre.shape[1]
    lat_dev = lat_all // wave_size
    width = pl.cdiv(slot_count, 256) * 256
    count = GROUP * 8 * level_count
    ext = lat_dev + 2 * HALO
    ext_pad = pl.cdiv(ext, 8) * 8
    first = jnp.broadcast_to(first_len[:, None], (slots, LANES))
    return pl.pallas_call(
        functools.partial(legendre_kernel, slot_count, lat_dev),
        grid=(slots // GROUP,),
        in_specs=[
            pl.BlockSpec((GROUP, LANES), lambda g: (g, 0)),
            pl.BlockSpec((GROUP, level_count, 2, width), lambda g: (g, 0, 0, 0)),
            pl.BlockSpec((GROUP, lat_all, width), lambda g: (g, 0, 0)),
        ],
        out_specs=pl.BlockSpec((wave_size, ext_pad, count), lambda g: (0, 0, g)),
        out_shape=jax.ShapeDtypeStruct(
            (wave_size, ext_pad, count * (slots // GROUP)), jnp.float32
        ),
        compiler_params=pltpu.CompilerParams(vmem_limit_bytes=32 * 1024 * 1024),
        name="legendre",
    )(first, spectral, legendre)


def fourier_tables(wavenumber_count):
    lon_count = 2 * wavenumber_count
    half_lon = lon_count // 2
    tables = []
    for parity in range(2):
        wave = np.arange(parity, wavenumber_count, 2)
        phase = wave[:, None] * np.arange(half_lon)[None, :] % lon_count
        angle = phase * (2.0 * math.pi / lon_count)
        weight = np.where(wave == 0, 1.0, 2.0)[:, None]
        parts = [weight * np.cos(angle), -weight * np.sin(angle)]
        tables.append(np.concatenate(parts if parity == 0 else parts[::-1], axis=0))
    exact = np.stack(tables)
    high = exact.astype(ml_dtypes.bfloat16)
    low = (exact - high.astype(np.float64)).astype(ml_dtypes.bfloat16)
    return high, low


def regroup(pieces, lane_bits, piece_lanes):
    pieces = list(pieces)
    for bit in (1, 2, 4):
        upper = (lane_bits & bit) != 0
        for one in range(8):
            if one & bit:
                continue
            two = one | bit
            a, b = pieces[one], pieces[two]
            pieces[one] = jnp.where(upper, pltpu.roll(b, piece_lanes * bit, 1), a)
            pieces[two] = jnp.where(upper, b, pltpu.roll(a, LANES - piece_lanes * bit, 1))
    return pieces


def grid_kernel(
    lat_dev,
    recv_ref,
    wave_ref,
    high_ref,
    low_ref,
    row_ref,
    col_ref,
    lon_ref,
    lat_ref,
    field_ref,
    horizontal_ref,
    rows_ref,
):
    source_count, ext_pad, width = recv_ref.shape
    half = high_ref.shape[2]
    lon_count = 2 * half
    per_source = width // LANES
    lane = lax.broadcasted_iota(jnp.int32, (ext_pad, LANES), 1)
    vectors = [
        recv_ref[source, :, LANES * i : LANES * (i + 1)]
        for source in range(source_count)
        for i in range(per_source)
    ]
    columns = [[] for _ in range(8)]
    for start in range(0, len(vectors), 8):
        for kind, piece in enumerate(regroup(vectors[start : start + 8], lane // 16, 16)):
            columns[kind].append(piece)
    matrix = jnp.concatenate([jnp.concatenate(c, axis=1) for c in columns], axis=0)
    slot_lanes = matrix.shape[1]
    order = lax.broadcasted_iota(jnp.int32, (half, slot_lanes), 0)
    wave_of_row = jnp.where(order < half // 2, 2 * order, 2 * order - half + 1)
    select = jnp.where(wave_ref[0:1, :] == wave_of_row, 1.0, 0.0).astype(jnp.bfloat16)
    high, low = split(matrix)
    count = high.shape[0] // 2
    ordered = lax.dot_general(
        jnp.concatenate([high[:count], low[:count], high[count:], low[count:]], axis=0),
        select,
        NT,
        preferred_element_type=jnp.float32,
    )
    real = ordered[: 2 * count]
    imag = pltpu.roll(ordered[2 * count :], half // 2, 1)
    first_half = lax.broadcasted_iota(jnp.int32, real.shape, 1) < half // 2
    even = jnp.where(first_half, real, imag).astype(jnp.bfloat16)
    odd = jnp.where(first_half, imag, real).astype(jnp.bfloat16)
    sums = []
    for parity, operand in enumerate((even, odd)):
        main = lax.dot_general(
            operand, high_ref[parity], NN, preferred_element_type=jnp.float32
        )
        rest = lax.dot_general(
            operand[:count], low_ref[parity], NN, preferred_element_type=jnp.float32
        )
        sums.append(main[:count] + (main[count:] + rest))
    blocks = lon_count // LANES
    for block in range(blocks // 2):
        here = slice(block * LANES, (block + 1) * LANES)
        rows_ref[block] = sums[0][:, here] + sums[1][:, here]
        rows_ref[block + blocks // 2] = sums[0][:, here] - sums[1][:, here]
    level_count = field_ref.shape[0]
    for block in range(blocks):
        here = slice(block * LANES, (block + 1) * LANES)
        for level in range(level_count):
            for hemi in range(2):
                start = (level * 2 + hemi) * ext_pad + HALO
                field_ref[level, hemi * lat_dev : (hemi + 1) * lat_dev, here] = rows_ref[
                    block, start : start + lat_dev, :
                ]
    groups = 2 * level_count
    near = []
    for block in range(blocks):
        lines = [
            rows_ref[block, pl.ds(j, groups, stride=ext_pad), :]
            for j in range(lat_dev + 2 * HALO)
        ]
        near.append(
            [jnp.concatenate(lines[j : j + lat_dev], axis=0) for j in range(2 * HALO + 1)]
        )
    point = lax.broadcasted_iota(jnp.int32, (groups * lat_dev, LANES), 1)
    for block in range(blocks):
        here = slice(block * LANES, (block + 1) * LANES)
        line = row_ref[:, here]
        step = point + col_ref[:, here]
        values = []
        for upper in range(2):
            picked = []
            for at in (block - 1, block, (block + 1) % blocks):
                choice = near[at][upper]
                for j in range(1, 2 * HALO):
                    choice = jnp.where(line == j, near[at][j + upper], choice)
                picked.append(choice)
            left = jnp.where(point >= LANES - 28, picked[0], picked[1])
            right = jnp.where(point < 28, picked[2], picked[1])
            for shift in range(2):
                place = (step + shift) & (LANES - 1)
                values.append(
                    jnp.where(
                        point < LANES // 2,
                        jnp.take_along_axis(left, place, axis=1),
                        jnp.take_along_axis(right, place, axis=1),
                    )
                )
        f = lon_ref[:, here]
        g = lat_ref[:, here]
        lower = (1.0 - f) * values[0] + f * values[1]
        higher = (1.0 - f) * values[2] + f * values[3]
        horizontal_ref[:, here] = (1.0 - g) * lower + g * higher


def per_device(legendre, spectral, pair_low, dep_lat, dep_col, lon_steps, tilt_steps):
    pair_local, level_count, _, slot_count = spectral.shape
    wavenumber_count = slot_count - 1
    lon_count = 2 * wavenumber_count
    lat_all = legendre.shape[1]
    wave_size = lax.axis_size("wave")
    wave_id = lax.axis_index("wave")
    lat_dev = lat_all // wave_size
    slots = pl.cdiv(pair_local, GROUP) * GROUP
    extra = slots - pair_local
    local_low = lax.dynamic_slice_in_dim(pair_low, wave_id * pair_local, pair_local)
    if extra:
        spectral = jnp.pad(spectral, ((0, extra), (0, 0), (0, 0), (0, 0)))
        legendre = jnp.pad(legendre, ((0, extra), (0, 0), (0, 0)))
        local_low = jnp.pad(local_low, (0, extra))
    sums = legendre_sums(
        spectral, legendre, wavenumber_count - local_low, slot_count, wave_size
    )
    received = lax.all_to_all(sums, "wave", split_axis=0, concat_axis=0, tiled=True)

    all_low = pair_low.reshape(wave_size, pair_local)
    waves = jnp.stack([all_low, wavenumber_count - 1 - all_low], axis=1)
    waves = jnp.pad(waves, ((0, 0), (0, 0), (0, extra)), constant_values=-1)
    waves = waves.reshape(wave_size, 2, slots // GROUP, GROUP).transpose(0, 2, 1, 3)
    waves = jnp.broadcast_to(waves.reshape(1, -1), (8, 2 * wave_size * slots))

    blocks = lon_count // LANES

    def spread(value):
        value = value.reshape(2, lat_dev, blocks, -1)
        value = jnp.broadcast_to(value, (2, lat_dev, blocks, LANES))
        value = value.reshape(2, lat_dev, 1, lon_count).transpose(1, 2, 0, 3)
        value = jnp.broadcast_to(value, (lat_dev, level_count, 2, lon_count))
        return value.reshape(lat_dev * level_count * 2, lon_count)

    own_lat = wave_id * lat_dev + jnp.arange(lat_dev, dtype=jnp.int32)
    row_step = dep_lat.reshape(2, lat_dev, blocks) - own_lat[None, :, None] + HALO
    first_col = LANES * jnp.arange(blocks, dtype=jnp.int32)
    col_step = dep_col.reshape(2, lat_dev, blocks) - first_col
    col_step = (col_step + lon_count // 2) % lon_count - lon_count // 2
    quarters = 4 * col_step.reshape(-1, 1) + lon_steps - 12
    row_step = spread(row_step)
    cells = spread(quarters >> 2)
    lon_frac = spread((quarters & 3).astype(jnp.float32) * 0.25)
    lat_frac = spread((tilt_steps & 3).astype(jnp.float32) * 0.25)

    high, low = fourier_tables(wavenumber_count)
    ext_pad = received.shape[1]
    vmem = pl.BlockSpec(memory_space=pltpu.VMEM)
    grid_field, horizontal = pl.pallas_call(
        functools.partial(grid_kernel, lat_dev),
        in_specs=[vmem] * 8,
        out_specs=[vmem] * 2,
        out_shape=[
            jax.ShapeDtypeStruct((level_count, 2 * lat_dev, lon_count), jnp.float32),
            jax.ShapeDtypeStruct((lat_dev * level_count * 2, lon_count), jnp.float32),
        ],
        scratch_shapes=[pltpu.VMEM((lon_count // LANES, level_count * 2 * ext_pad, LANES), jnp.float32)],
        compiler_params=pltpu.CompilerParams(vmem_limit_bytes=32 * 1024 * 1024),
        name="grid",
    )(received, waves, jnp.asarray(high), jnp.asarray(low), row_step, cells, lon_frac, lat_frac)

    horizontal = horizontal.reshape(lat_dev, level_count, 2, lon_count).transpose(1, 2, 0, 3)
    horizontal = horizontal.reshape(level_count, 2 * lat_dev, lon_count)
    lev_size = lax.axis_size("lev")
    above = lax.ppermute(horizontal[0], "lev", [(i, i - 1) for i in range(1, lev_size)])
    is_last = lax.axis_index("lev") == lev_size - 1
    above = jnp.where(is_last, horizontal[level_count - 1], above)
    upper = jnp.concatenate([horizontal[1:], above[None]], axis=0)
    vertical = (tilt_steps >> 2).astype(jnp.float32).reshape(2 * lat_dev, lon_count) * 0.25
    departed = (1.0 - vertical) * horizontal + vertical * upper
    return grid_field, departed


def solution(mesh):
    return jax.shard_map(
        per_device,
        mesh=mesh,
        in_specs=(
            P("wave", None, None),
            P("wave", "lev", None, None),
            P(),
            P("wave"),
            P("wave"),
            P("wave", None),
            P("wave", None),
        ),
        out_specs=(P("lev", "wave", None), P("lev", "wave", None)),
        check_vma=False,
    )
```

```python
import functools
import math

import jax
import jax.numpy as jnp
import ml_dtypes
import numpy as np
from jax import lax
from jax.experimental import pallas as pl
from jax.experimental.pallas import tpu as pltpu
from jax.sharding import PartitionSpec as P

LANES = 128
GROUP = 8
HALO = 2
MIB = 1024 * 1024
NT = (((1,), (1,)), ((), ()))
NN = (((1,), (0,)), ((), ()))


def split(value):
    high = value.astype(jnp.bfloat16)
    low = (value - high.astype(jnp.float32)).astype(jnp.bfloat16)
    return high, low


def legendre_kernel(slot_count, pair_local, lat_dev, low_ref, spec_ref, leg_ref, out_ref):
    group, lat_all, width = leg_ref.shape
    level_count = spec_ref.shape[1]
    pair_total = low_ref.shape[0]
    base = lax.axis_index("wave") * pair_local + pl.program_id(0) * group
    slot_of_row = lax.broadcasted_iota(jnp.int32, (group, LANES), 0)
    first = jnp.zeros((group, LANES), jnp.int32)
    for slot in range(group):
        low = low_ref[jnp.minimum(base + slot, pair_total - 1)]
        first = jnp.where(slot_of_row == slot, slot_count - 1 - low, first)
    first = jnp.concatenate([first] * (width // LANES), axis=1)
    slot_pos = lax.broadcasted_iota(jnp.int32, (group, width), 1)
    inside = slot_pos < slot_count
    second = slot_pos >= first
    offset = jnp.where(second, slot_pos - first, slot_pos)
    sign = (1 - 2 * (offset & 1)).astype(jnp.float32)
    pieces = []
    for level in range(level_count):
        for part in range(2):
            row = jnp.where(inside, spec_ref[:, level, part, :], 0.0)
            for hemi in range(2):
                signed = row * sign if hemi else row
                pieces.append(jnp.where(second, 0.0, signed))
                pieces.append(jnp.where(second, signed, 0.0))
    columns = jnp.concatenate(split(jnp.concatenate(pieces, axis=0)), axis=0)
    count = group * len(pieces)
    table_pos = lax.broadcasted_iota(jnp.int32, (group * lat_all, width), 1)
    table = jnp.where(table_pos < slot_count, leg_ref[...].reshape(group * lat_all, width), 0.0)
    rows = jnp.concatenate(split(table), axis=0)
    crossed = lax.dot_general(rows, columns, NT, preferred_element_type=jnp.float32)
    half = group * lat_all
    crossed = (crossed[:half, :count] + crossed[:half, count:]) + (
        crossed[half:, :count] + crossed[half:, count:]
    )
    slot_of_lane = lax.broadcasted_iota(jnp.int32, (lat_all, count), 1) % group
    sums = jnp.zeros((lat_all, count), jnp.float32)
    for slot in range(group):
        block = crossed[slot * lat_all : (slot + 1) * lat_all]
        sums = jnp.where(slot_of_lane == slot, block, sums)
    edge = jnp.zeros((HALO, count), jnp.float32)
    tail = jnp.zeros((2 * HALO, count), jnp.float32)
    padded = jnp.concatenate([edge, sums, tail], axis=0)
    for dest in range(out_ref.shape[0]):
        out_ref[dest] = padded[dest * lat_dev : dest * lat_dev + out_ref.shape[1]]


def legendre_sums(pair_low, spectral, legendre, pair_local, slot_count, wave_size):
    slots, level_count = spectral.shape[:2]
    lat_all = legendre.shape[1]
    lat_dev = lat_all // wave_size
    width = pl.cdiv(slot_count, 256) * 256
    count = GROUP * 8 * level_count
    ext_pad = pl.cdiv(lat_dev + 2 * HALO, 8) * 8
    return pl.pallas_call(
        functools.partial(legendre_kernel, slot_count, pair_local, lat_dev),
        grid=(slots // GROUP,),
        in_specs=[
            pl.BlockSpec(memory_space=pltpu.SMEM),
            pl.BlockSpec((GROUP, level_count, 2, width), lambda g: (g, 0, 0, 0)),
            pl.BlockSpec((GROUP, lat_all, width), lambda g: (g, 0, 0)),
        ],
        out_specs=pl.BlockSpec((wave_size, ext_pad, count), lambda g: (0, 0, g)),
        out_shape=jax.ShapeDtypeStruct(
            (wave_size, ext_pad, count * (slots // GROUP)), jnp.float32
        ),
        compiler_params=pltpu.CompilerParams(vmem_limit_bytes=60 * MIB),
        name="legendre",
    )(pair_low, spectral, legendre)


def fourier_tables(wavenumber_count):
    lon_count = 2 * wavenumber_count
    half_lon = lon_count // 2
    tables = []
    for parity in range(2):
        wave = np.arange(parity, wavenumber_count, 2)
        phase = wave[:, None] * np.arange(half_lon)[None, :] % lon_count
        angle = phase * (2.0 * math.pi / lon_count)
        weight = np.where(wave == 0, 1.0, 2.0)[:, None]
        parts = [weight * np.cos(angle), -weight * np.sin(angle)]
        tables.append(np.concatenate(parts if parity == 0 else parts[::-1], axis=0))
    exact = np.stack(tables)
    high = exact.astype(ml_dtypes.bfloat16)
    low = (exact - high.astype(np.float64)).astype(ml_dtypes.bfloat16)
    return high, low


def regroup(pieces, level, lane):
    piece_lanes = LANES // 8
    upper = lane // piece_lanes >= 4
    if level == 0:
        pieces = [
            jnp.where(upper, pltpu.roll(pieces[i + 4], 4 * piece_lanes, 1), pieces[i])
            for i in range(4)
        ]
    else:
        pieces = [
            jnp.where(upper, pieces[i + 4], pltpu.roll(pieces[i], 4 * piece_lanes, 1))
            for i in range(4)
        ]
    for bit in (1, 2):
        upper = (lane // piece_lanes & bit) != 0
        for one in range(4):
            if one & bit:
                continue
            a, b = pieces[one], pieces[one | bit]
            pieces[one] = jnp.where(upper, pltpu.roll(b, piece_lanes * bit, 1), a)
            pieces[one | bit] = jnp.where(
                upper, b, pltpu.roll(a, LANES - piece_lanes * bit, 1)
            )
    return pieces


def level_rows(level, recv_ref, select_ref, high_ref, low_ref):
    source_count, ext_pad, width = recv_ref.shape
    half = high_ref.shape[2]
    lane = lax.broadcasted_iota(jnp.int32, (ext_pad, LANES), 1)
    vectors = [
        recv_ref[source, :, LANES * i : LANES * (i + 1)]
        for source in range(source_count)
        for i in range(width // LANES)
    ]
    columns = [[] for _ in range(4)]
    for start in range(0, len(vectors), 8):
        for kind, piece in enumerate(regroup(vectors[start : start + 8], level, lane)):
            columns[kind].append(piece)
    matrix = jnp.concatenate([jnp.concatenate(c, axis=1) for c in columns], axis=0)
    high, low = split(matrix)
    count = high.shape[0] // 2
    ordered = lax.dot_general(
        jnp.concatenate([high[:count], low[:count], high[count:], low[count:]], axis=0),
        select_ref[...],
        NT,
        preferred_element_type=jnp.float32,
    )
    real = ordered[: 2 * count]
    imag = pltpu.roll(ordered[2 * count :], half // 2, 1)
    first_half = lax.broadcasted_iota(jnp.int32, real.shape, 1) < half // 2
    even = jnp.where(first_half, real, imag).astype(jnp.bfloat16)
    odd = jnp.where(first_half, imag, real).astype(jnp.bfloat16)
    sums = []
    for parity, operand in enumerate((even, odd)):
        main = lax.dot_general(
            operand, high_ref[parity], NN, preferred_element_type=jnp.float32
        )
        rest = lax.dot_general(
            operand[:count], low_ref[parity], NN, preferred_element_type=jnp.float32
        )
        sums.append(main[:count] + (main[count:] + rest))
    return sums


def interpolate(sums, field_ref, level, lat_dev, lon, tilt, row_step, col_step, near_ref):
    half = sums[0].shape[1]
    count = sums[0].shape[0]
    ext_pad = count // 2
    blocks = 2 * half // LANES
    for block in range(blocks // 2):
        here = slice(block * LANES, (block + 1) * LANES)
        for at, rows in (
            (block, sums[0][:, here] + sums[1][:, here]),
            (block + blocks // 2, sums[0][:, here] - sums[1][:, here]),
        ):
            there = slice(at * LANES, (at + 1) * LANES)
            for hemi in range(2):
                start = hemi * ext_pad + HALO
                field_ref[level, hemi * lat_dev : (hemi + 1) * lat_dev, there] = rows[
                    start : start + lat_dev
                ]
            for side in range(3):
                place = (at + 1 - side) % blocks
                near_ref[side, pl.ds(place, count, stride=blocks), :] = rows
    points = 2 * lat_dev * blocks
    point = lax.broadcasted_iota(jnp.int32, (points, LANES), 1)
    quarters = 4 * col_step + lon - 12
    step = point + (quarters >> 2)
    f = (quarters & 3).astype(jnp.float32) * 0.25
    g = (tilt & 3).astype(jnp.float32) * 0.25

    def line(side, j):
        return jnp.concatenate(
            [
                near_ref[side, pl.ds((hemi * ext_pad + j) * blocks, lat_dev * blocks), :]
                for hemi in range(2)
            ],
            axis=0,
        )

    lines = [[line(side, j) for j in range(2 * HALO + 1)] for side in range(3)]
    values = []
    for upper in range(2):
        picked = []
        for side in range(3):
            choice = lines[side][upper]
            for j in range(1, 2 * HALO):
                choice = jnp.where(row_step == j, lines[side][j + upper], choice)
            picked.append(choice)
        left = jnp.where(point >= LANES - 28, picked[0], picked[1])
        right = jnp.where(point < 28, picked[2], picked[1])
        for shift in range(2):
            place = (step + shift) & (LANES - 1)
            values.append(
                jnp.where(
                    point < LANES // 2,
                    jnp.take_along_axis(left, place, axis=1),
                    jnp.take_along_axis(right, place, axis=1),
                )
            )
    lower = (1.0 - f) * values[0] + f * values[1]
    higher = (1.0 - f) * values[2] + f * values[3]
    return (1.0 - g) * lower + g * higher


def first_kernel(
    lat_dev,
    recv_ref,
    select_ref,
    high_ref,
    low_ref,
    row_ref,
    col_ref,
    lon_ref,
    tilt_ref,
    field_ref,
    horizontal_ref,
    near_ref,
):
    sums = level_rows(0, recv_ref, select_ref, high_ref, low_ref)
    horizontal_ref[...] = interpolate(
        sums,
        field_ref,
        0,
        lat_dev,
        lon_ref[...],
        tilt_ref[...],
        row_ref[...],
        col_ref[...],
        near_ref,
    )


def later_kernel(
    lat_dev,
    recv_ref,
    select_ref,
    high_ref,
    low_ref,
    row_ref,
    col_ref,
    lon_ref,
    tilt_ref,
    below_ref,
    field_ref,
    departed_ref,
    horizontal_ref,
    near_ref,
):
    level_count = departed_ref.shape[0] + 1
    tilt = tilt_ref[...]
    vertical = (tilt >> 2).astype(jnp.float32) * 0.25
    below = below_ref[...]
    for level in range(1, level_count):
        sums = level_rows(level, recv_ref, select_ref, high_ref, low_ref)
        horizontal = interpolate(
            sums,
            field_ref,
            level - 1,
            lat_dev,
            lon_ref[...],
            tilt,
            row_ref[...],
            col_ref[...],
            near_ref,
        )
        departed_ref[level - 1] = (1.0 - vertical) * below + vertical * horizontal
        below = horizontal
    horizontal_ref[...] = below


def last_kernel(below_ref, above_ref, tilt_ref, out_ref):
    is_last = lax.axis_index("lev") == lax.axis_size("lev") - 1
    vertical = (tilt_ref[...] >> 2).astype(jnp.float32) * 0.25
    below = below_ref[...]
    above = jnp.where(is_last, below, above_ref[...])
    out_ref[...] = (1.0 - vertical) * below + vertical * above


def per_device(legendre, spectral, pair_low, dep_lat, dep_col, lon_steps, tilt_steps):
    pair_local, level_count, _, slot_count = spectral.shape
    wavenumber_count = slot_count - 1
    lon_count = 2 * wavenumber_count
    lat_all = legendre.shape[1]
    wave_size = lax.axis_size("wave")
    lev_size = lax.axis_size("lev")
    wave_id = lax.axis_index("wave")
    lat_dev = lat_all // wave_size
    slots = pl.cdiv(pair_local, GROUP) * GROUP
    extra = slots - pair_local
    if extra:
        spectral = jnp.pad(spectral, ((0, extra), (0, 0), (0, 0), (0, 0)))
        legendre = jnp.pad(legendre, ((0, extra), (0, 0), (0, 0)))
    sums = legendre_sums(pair_low, spectral, legendre, pair_local, slot_count, wave_size)
    received = lax.all_to_all(sums, "wave", split_axis=0, concat_axis=0, tiled=True)

    all_low = pair_low.reshape(wave_size, pair_local)
    waves = jnp.stack([all_low, wavenumber_count - 1 - all_low], axis=1)
    waves = jnp.pad(waves, ((0, 0), (0, 0), (0, extra)), constant_values=-1)
    waves = waves.reshape(wave_size, 2, slots // GROUP, GROUP).transpose(0, 2, 1, 3)
    order = np.arange(wavenumber_count)
    order = np.concatenate([order[::2], order[1::2]]).astype(np.int32)
    select = (waves.reshape(1, -1) == order[:, None]).astype(jnp.bfloat16)

    blocks = lon_count // LANES
    points = 2 * lat_dev * blocks
    row = jnp.arange(points, dtype=jnp.int32)
    own_lat = wave_id * lat_dev + row // blocks % lat_dev
    row_step = dep_lat - own_lat + HALO
    col_step = dep_col - LANES * (row % blocks)
    col_step = (col_step + lon_count // 2) % lon_count - lon_count // 2
    row_step = jnp.broadcast_to(row_step[:, None], (points, LANES))
    col_step = jnp.broadcast_to(col_step[:, None], (points, LANES))

    high, low = fourier_tables(wavenumber_count)
    ext_pad = received.shape[1]
    vmem = pl.BlockSpec(memory_space=pltpu.VMEM)
    params = pltpu.CompilerParams(vmem_limit_bytes=24 * MIB)
    operands = (
        received,
        select,
        jnp.asarray(high),
        jnp.asarray(low),
        row_step,
        col_step,
        lon_steps,
        tilt_steps,
    )
    near = pltpu.VMEM((3, 2 * ext_pad * blocks, LANES), jnp.float32)
    flat = jax.ShapeDtypeStruct((points, LANES), jnp.float32)
    field_first, horizontal = pl.pallas_call(
        functools.partial(first_kernel, lat_dev),
        in_specs=[vmem] * 8,
        out_specs=[vmem] * 2,
        out_shape=[jax.ShapeDtypeStruct((1, 2 * lat_dev, lon_count), jnp.float32), flat],
        scratch_shapes=[near],
        compiler_params=params,
        name="first_level",
    )(*operands)
    above = lax.ppermute(horizontal, "lev", [(i, i - 1) for i in range(1, lev_size)])
    field_later, departed, top = pl.pallas_call(
        functools.partial(later_kernel, lat_dev),
        in_specs=[vmem] * 9,
        out_specs=[vmem] * 3,
        out_shape=[
            jax.ShapeDtypeStruct((level_count - 1, 2 * lat_dev, lon_count), jnp.float32),
            jax.ShapeDtypeStruct((level_count - 1, points, LANES), jnp.float32),
            flat,
        ],
        scratch_shapes=[near],
        compiler_params=params,
        cost_estimate=pl.CostEstimate(
            flops=10**8, bytes_accessed=4 * 10**6, transcendentals=0
        ),
        name="later_levels",
    )(*operands, horizontal)
    grid_field = jnp.concatenate([field_first, field_later], axis=0)
    final = pl.pallas_call(
        last_kernel,
        in_specs=[vmem] * 3,
        out_specs=vmem,
        out_shape=flat,
        compiler_params=params,
        name="top_level",
    )(top, above, tilt_steps)
    departed = jnp.concatenate([departed, final[None]], axis=0)
    return grid_field, departed.reshape(level_count, 2 * lat_dev, lon_count)


def solution(mesh):
    return jax.shard_map(
        per_device,
        mesh=mesh,
        in_specs=(
            P("wave", None, None),
            P("wave", "lev", None, None),
            P(),
            P("wave"),
            P("wave"),
            P("wave", None),
            P("wave", None),
        ),
        out_specs=(P("lev", "wave", None), P("lev", "wave", None)),
        check_vma=False,
    )
```

```python
import functools
import math

import jax
import jax.numpy as jnp
import ml_dtypes
import numpy as np
from jax import lax
from jax.experimental import pallas as pl
from jax.experimental.pallas import tpu as pltpu
from jax.sharding import PartitionSpec as P

LANES = 128
GROUP = 8
HALO = 2
MIB = 1024 * 1024
NT = (((1,), (1,)), ((), ()))
NN = (((1,), (0,)), ((), ()))


def split(value):
    high = value.astype(jnp.bfloat16)
    low = (value - high.astype(jnp.float32)).astype(jnp.bfloat16)
    return high, low


def widen(value, width):
    lane = lax.broadcasted_iota(jnp.int32, (value.shape[0], LANES), 1)
    full = value.shape[1] // LANES * LANES
    parts = [value[:, :full]]
    for start in range(full, value.shape[1]):
        column = jnp.broadcast_to(value[:, start : start + 1], lane.shape)
        parts.append(jnp.where(lane == start - full, column, 0.0))
    assert len(parts) <= 2 and full + LANES * (len(parts) - 1) == width
    return jnp.concatenate(parts, axis=1)


def legendre_kernel(
    pair_local,
    lat_dev,
    low_hbm,
    spec_hbm,
    leg_hbm,
    *refs,
):
    chip_refs = refs[:-7]
    low_ref, spec_ref, leg_ref, sums_ref, low_sem, spec_sem, leg_sem = refs[-7:]
    slots, lat_all, slot_count = leg_ref.shape
    level_count = spec_ref.shape[1]
    pair_total = low_ref.shape[0]
    ext_pad = sums_ref.shape[1]
    width = pl.cdiv(slot_count, LANES) * LANES
    low_copy = pltpu.make_async_copy(low_hbm, low_ref, low_sem)
    low_copy.start()
    copies = []
    for start in range(0, slots, GROUP):
        part = pl.ds(start, GROUP)
        index = start // GROUP
        pair = (
            pltpu.make_async_copy(spec_hbm.at[part], spec_ref.at[part], spec_sem.at[index]),
            pltpu.make_async_copy(leg_hbm.at[part], leg_ref.at[part], leg_sem.at[index]),
        )
        for copy in pair:
            copy.start()
        copies.append(pair)
    wave = lax.axis_index("wave")
    slot_of_row = lax.broadcasted_iota(jnp.int32, (GROUP, LANES), 0)
    slot_pos = lax.broadcasted_iota(jnp.int32, (GROUP, width), 1)
    low_copy.wait()
    for start in range(0, slots, GROUP):
        base = wave * pair_local + start
        first = jnp.zeros((GROUP, LANES), jnp.int32)
        for slot in range(GROUP):
            low = low_ref[jnp.minimum(base + slot, pair_total - 1)]
            first = jnp.where(slot_of_row == slot, slot_count - 1 - low, first)
        first = jnp.concatenate([first] * (width // LANES), axis=1)
        second = slot_pos >= first
        sign = (1 - 2 * ((slot_pos - jnp.where(second, first, 0)) & 1)).astype(jnp.float32)
        member = [jnp.where(second, 0.0, 1.0), jnp.where(second, 1.0, 0.0)]
        masks = [
            jnp.concatenate(member, axis=0).astype(jnp.bfloat16),
            jnp.concatenate([m * sign for m in member], axis=0).astype(jnp.bfloat16),
        ]
        for copy in copies[start // GROUP]:
            copy.wait()
        highs, lows = [], []
        for level in range(level_count):
            for part in range(2):
                row = widen(spec_ref[pl.ds(start, GROUP), level, part, :], width)
                high, low = split(jnp.concatenate([row, row], axis=0))
                highs += [high * mask for mask in masks]
                lows += [low * mask for mask in masks]
        columns = jnp.concatenate(highs + lows, axis=0)
        count = columns.shape[0] // 2
        half = GROUP * lat_all
        table = leg_ref[pl.ds(start, GROUP)].reshape(half, slot_count)
        rows = jnp.concatenate(split(widen(table, width)), axis=0)
        crossed = lax.dot_general(rows, columns, NT, preferred_element_type=jnp.float32)
        crossed = (crossed[:half, :count] + crossed[:half, count:]) + (
            crossed[half:, :count] + crossed[half:, count:]
        )
        slot_of_lane = lax.broadcasted_iota(jnp.int32, (lat_all, count), 1) % GROUP
        sums = crossed[:lat_all]
        for slot in range(1, GROUP):
            block = crossed[slot * lat_all : (slot + 1) * lat_all]
            sums = jnp.where(slot_of_lane == slot, block, sums)
        edge = jnp.zeros((HALO, count), jnp.float32)
        tail = jnp.zeros((ext_pad, count), jnp.float32)
        padded = jnp.concatenate([edge, sums, tail], axis=0)
        here = slice(start // GROUP * count, (start // GROUP + 1) * count)
        for dest in range(sums_ref.shape[0]):
            sums_ref[dest, :, here] = padded[dest * lat_dev : dest * lat_dev + ext_pad]
    for step, chip_ref in enumerate(chip_refs):
        dest = (wave // 2 ^ step) * 2
        for core in range(2):
            chip_ref[core] = sums_ref[dest + core]


def legendre_sums(pair_low, spectral, legendre, pair_local, wave_size):
    slots, level_count = spectral.shape[:2]
    lat_all, slot_count = legendre.shape[1:]
    lat_dev = lat_all // wave_size
    lanes = 8 * level_count * slots
    ext_pad = pl.cdiv(lat_dev + 2 * HALO, 8) * 8
    chips = wave_size // 2
    out = jax.ShapeDtypeStruct((2, ext_pad, lanes), jnp.float32)
    operands = [
        pltpu.with_memory_space_constraint(x, pltpu.HBM) for x in (pair_low, spectral, legendre)
    ]
    return pl.pallas_call(
        functools.partial(legendre_kernel, pair_local, lat_dev),
        in_specs=[pl.BlockSpec(memory_space=pltpu.HBM)] * 3,
        out_specs=[pl.BlockSpec(memory_space=pltpu.VMEM)] * chips,
        out_shape=[out] * chips,
        scratch_shapes=[
            pltpu.SMEM(pair_low.shape, jnp.int32),
            pltpu.VMEM(spectral.shape, jnp.float32),
            pltpu.VMEM(legendre.shape, jnp.float32),
            pltpu.VMEM((wave_size, ext_pad, lanes), jnp.float32),
            pltpu.SemaphoreType.DMA,
            pltpu.SemaphoreType.DMA((slots // GROUP,)),
            pltpu.SemaphoreType.DMA((slots // GROUP,)),
        ],
        compiler_params=pltpu.CompilerParams(vmem_limit_bytes=24 * MIB),
        name="legendre",
    )(*operands)


def swap(value, by):
    wave_size = lax.axis_size("wave")
    return lax.ppermute(value, "wave", [(i, i ^ by) for i in range(wave_size)])


def plan_kernel(
    pair_local,
    lat_dev,
    after_ref,
    low_hbm,
    lat_hbm,
    col_hbm,
    lon_hbm,
    tilt_hbm,
    table_hbm,
    select_ref,
    row_step_ref,
    place_ref,
    lon_frac_ref,
    lat_frac_ref,
    vertical_ref,
    table_ref,
    low_ref,
    lat_ref,
    col_ref,
    lon_ref,
    tilt_ref,
    sems,
):
    pairs = [
        (low_hbm, low_ref),
        (lat_hbm, lat_ref),
        (col_hbm, col_ref),
        (lon_hbm, lon_ref),
        (tilt_hbm, tilt_ref),
        (table_hbm, table_ref),
    ]
    copies = [
        pltpu.make_async_copy(there, here, sems.at[i]) for i, (there, here) in enumerate(pairs)
    ]
    for copy in copies:
        copy.start()
    for copy in copies[:-1]:
        copy.wait()
    wave = lax.axis_index("wave")
    half, slot_lanes = select_ref.shape
    lon_count = 2 * half
    points = lon_ref.shape[0]
    blocks = points // (2 * lat_dev)
    sources = low_ref.shape[0] // pair_local
    per_source = slot_lanes // (sources * 2 * GROUP)
    lane = lax.broadcasted_iota(jnp.int32, (GROUP, LANES), 1)
    order = lax.broadcasted_iota(jnp.int32, (half, LANES), 0)
    order = jnp.where(order < half // 2, 2 * order, 2 * order - half + 1)
    per_vector = LANES // (2 * GROUP)
    for block in range(slot_lanes // LANES):
        waves = jnp.full((GROUP, LANES), -2 * half, jnp.int32)
        for index in range(per_vector):
            source, group = divmod(block * per_vector + index, per_source)
            base = (wave ^ source) * pair_local + group * GROUP
            for slot in range(min(GROUP, pair_local - group * GROUP)):
                here = (lane & ~GROUP) == index * 2 * GROUP + slot
                waves = jnp.where(here, low_ref[base + slot], waves)
        waves = jnp.where((lane & GROUP) != 0, half - 1 - waves, waves)
        match = jnp.broadcast_to(waves[0:1], order.shape) == order
        select_ref[:, block * LANES : (block + 1) * LANES] = jnp.where(match, 1.0, 0.0).astype(
            jnp.bfloat16
        )
    row = lax.broadcasted_iota(jnp.int32, (points, LANES), 0)
    point = lax.broadcasted_iota(jnp.int32, (points, LANES), 1)
    row_step = jnp.zeros((points, LANES), jnp.int32)
    col_step = jnp.zeros((points, LANES), jnp.int32)
    for index in range(points):
        own = wave * lat_dev + index // blocks % lat_dev - HALO
        row_step = jnp.where(row == index, lat_ref[index] - own, row_step)
        first = LANES * (index % blocks)
        col_step = jnp.where(row == index, col_ref[index] - first, col_step)
    col_step = jnp.where(col_step >= half, col_step - lon_count, col_step)
    col_step = jnp.where(col_step < -half, col_step + lon_count, col_step)
    quarters = 4 * col_step + lon_ref[...] - 12
    row_step_ref[...] = row_step
    place_ref[...] = point + (quarters >> 2)
    lon_frac_ref[...] = (quarters & 3).astype(jnp.float32) * 0.25
    lat_frac_ref[...] = (tilt_ref[...] & 3).astype(jnp.float32) * 0.25
    vertical_ref[...] = (tilt_ref[...] >> 2).astype(jnp.float32) * 0.25
    copies[-1].wait()


def plan(after, tables, pair_low, dep_lat, dep_col, lon_steps, tilt_steps, pair_local, lat_dev, lanes):
    vmem = pl.BlockSpec(memory_space=pltpu.VMEM)
    whole = jax.ShapeDtypeStruct(lon_steps.shape, jnp.int32)
    fraction = jax.ShapeDtypeStruct(lon_steps.shape, jnp.float32)
    half = tables.shape[1]
    operands = [
        pltpu.with_memory_space_constraint(x, pltpu.HBM)
        for x in (pair_low, dep_lat, dep_col, lon_steps, tilt_steps, tables)
    ]
    return pl.pallas_call(
        functools.partial(plan_kernel, pair_local, lat_dev),
        in_specs=[pl.BlockSpec(memory_space=pl.ANY)]
        + [pl.BlockSpec(memory_space=pltpu.HBM)] * len(operands),
        out_specs=[vmem] * 7,
        out_shape=[
            jax.ShapeDtypeStruct((half, lanes), jnp.bfloat16),
            whole,
            whole,
            fraction,
            fraction,
            fraction,
            jax.ShapeDtypeStruct(tables.shape, tables.dtype),
        ],
        scratch_shapes=[
            pltpu.SMEM(pair_low.shape, jnp.int32),
            pltpu.SMEM(dep_lat.shape, jnp.int32),
            pltpu.SMEM(dep_col.shape, jnp.int32),
            pltpu.VMEM(lon_steps.shape, jnp.int32),
            pltpu.VMEM(tilt_steps.shape, jnp.int32),
            pltpu.SemaphoreType.DMA((len(operands),)),
        ],
        compiler_params=pltpu.CompilerParams(vmem_limit_bytes=24 * MIB),
        cost_estimate=pl.CostEstimate(
            flops=10**7, bytes_accessed=4 * 10**6, transcendentals=0
        ),
        name="plan",
    )(after, *operands)


def fourier_tables(wavenumber_count):
    lon_count = 2 * wavenumber_count
    half_lon = lon_count // 2
    tables = []
    for parity in range(2):
        wave = np.arange(parity, wavenumber_count, 2)
        phase = wave[:, None] * np.arange(half_lon)[None, :] % lon_count
        angle = phase * (2.0 * math.pi / lon_count)
        weight = np.where(wave == 0, 1.0, 2.0)[:, None]
        parts = [weight * np.cos(angle), -weight * np.sin(angle)]
        tables.append(np.concatenate(parts if parity == 0 else parts[::-1], axis=0))
    exact = np.stack(tables)
    high = exact.astype(ml_dtypes.bfloat16)
    low = (exact - high.astype(np.float64)).astype(ml_dtypes.bfloat16)
    return np.concatenate([high, low], axis=2)


def regroup(pieces, level, lane):
    piece_lanes = LANES // 8
    upper = lane // piece_lanes >= 4
    if level == 0:
        pieces = [
            jnp.where(upper, pltpu.roll(pieces[i + 4], 4 * piece_lanes, 1), pieces[i])
            for i in range(4)
        ]
    else:
        pieces = [
            jnp.where(upper, pieces[i + 4], pltpu.roll(pieces[i], 4 * piece_lanes, 1))
            for i in range(4)
        ]
    for bit in (1, 2):
        upper = (lane // piece_lanes & bit) != 0
        for one in range(4):
            if one & bit:
                continue
            a, b = pieces[one], pieces[one | bit]
            pieces[one] = jnp.where(upper, pltpu.roll(b, piece_lanes * bit, 1), a)
            pieces[one | bit] = jnp.where(
                upper, b, pltpu.roll(a, LANES - piece_lanes * bit, 1)
            )
    return pieces


def level_rows(level, piece_refs, select_ref, table_ref):
    half = table_ref.shape[2] // 2
    core = lax.axis_index("wave") % 2
    vectors = []
    for ref in piece_refs:
        source = ref[core]
        vectors += [
            source[:, start : start + LANES] for start in range(0, source.shape[1], LANES)
        ]
    lane = lax.broadcasted_iota(jnp.int32, vectors[0].shape, 1)
    columns = [[] for _ in range(4)]
    for start in range(0, len(vectors), 8):
        for kind, piece in enumerate(regroup(vectors[start : start + 8], level, lane)):
            columns[kind].append(piece)
    matrix = jnp.concatenate([jnp.concatenate(c, axis=1) for c in columns], axis=0)
    high, low = split(matrix)
    count = high.shape[0] // 2
    ordered = lax.dot_general(
        jnp.concatenate([high[:count], low[:count], high[count:], low[count:]], axis=0),
        select_ref[...],
        NT,
        preferred_element_type=jnp.float32,
    )
    real = ordered[: 2 * count]
    imag = pltpu.roll(ordered[2 * count :], half // 2, 1)
    first_half = lax.broadcasted_iota(jnp.int32, real.shape, 1) < half // 2
    even = jnp.where(first_half, real, imag).astype(jnp.bfloat16)
    odd = jnp.where(first_half, imag, real).astype(jnp.bfloat16)
    sums = []
    for parity, operand in enumerate((even, odd)):
        main = lax.dot_general(
            operand, table_ref[parity], NN, preferred_element_type=jnp.float32
        )
        sums.append(main[:count, :half] + (main[count:, :half] + main[:count, half:]))
    return sums


def interpolate(sums, field_ref, level, lat_dev, row_step, step, f, g, near_ref):
    half = sums[0].shape[1]
    count = sums[0].shape[0]
    ext_pad = count // 2
    blocks = 2 * half // LANES
    for block in range(blocks // 2):
        here = slice(block * LANES, (block + 1) * LANES)
        for at, rows in (
            (block, sums[0][:, here] + sums[1][:, here]),
            (block + blocks // 2, sums[0][:, here] - sums[1][:, here]),
        ):
            there = slice(at * LANES, (at + 1) * LANES)
            for hemi in range(2):
                start = hemi * ext_pad + HALO
                field_ref[level, hemi * lat_dev : (hemi + 1) * lat_dev, there] = rows[
                    start : start + lat_dev
                ]
            for side in range(3):
                place = (at + 1 - side) % blocks
                near_ref[side, pl.ds(place, count, stride=blocks), :] = rows
    points = 2 * lat_dev * blocks
    point = lax.broadcasted_iota(jnp.int32, (points, LANES), 1)

    def line(side, j):
        return jnp.concatenate(
            [
                near_ref[side, pl.ds((hemi * ext_pad + j) * blocks, lat_dev * blocks), :]
                for hemi in range(2)
            ],
            axis=0,
        )

    lines = [[line(side, j) for j in range(2 * HALO + 1)] for side in range(3)]
    values = []
    for upper in range(2):
        picked = []
        for side in range(3):
            choice = lines[side][upper]
            for j in range(1, 2 * HALO):
                choice = jnp.where(row_step == j, lines[side][j + upper], choice)
            picked.append(choice)
        left = jnp.where(point >= LANES - 28, picked[0], picked[1])
        right = jnp.where(point < 28, picked[2], picked[1])
        for shift in range(2):
            place = (step + shift) & (LANES - 1)
            values.append(
                jnp.where(
                    point < LANES // 2,
                    jnp.take_along_axis(left, place, axis=1),
                    jnp.take_along_axis(right, place, axis=1),
                )
            )
    lower = (1.0 - f) * values[0] + f * values[1]
    higher = (1.0 - f) * values[2] + f * values[3]
    return (1.0 - g) * lower + g * higher


def first_kernel(lat_dev, piece_count, *refs):
    piece_refs, plan_refs = refs[:piece_count], refs[piece_count + 2 : -3]
    select_ref, table_ref = refs[piece_count : piece_count + 2]
    field_ref, horizontal_ref, near_ref = refs[-3:]
    sums = level_rows(0, piece_refs, select_ref, table_ref)
    plans = [ref[...] for ref in plan_refs]
    horizontal_ref[...] = interpolate(sums, field_ref, 0, lat_dev, *plans, near_ref)


def later_kernel(lat_dev, piece_count, *refs):
    piece_refs, plan_refs = refs[:piece_count], refs[piece_count + 2 : -6]
    select_ref, table_ref = refs[piece_count : piece_count + 2]
    vertical_ref, below_ref, field_ref, departed_ref, horizontal_ref, near_ref = refs[-6:]
    vertical = vertical_ref[...]
    below = below_ref[...]
    plans = [ref[...] for ref in plan_refs]
    for level in range(1, departed_ref.shape[0] + 1):
        sums = level_rows(level, piece_refs, select_ref, table_ref)
        horizontal = interpolate(sums, field_ref, level - 1, lat_dev, *plans, near_ref)
        departed_ref[level - 1] = (1.0 - vertical) * below + vertical * horizontal
        below = horizontal
    horizontal_ref[...] = below


def last_kernel(below_ref, above_ref, vertical_ref, out_ref):
    is_last = lax.axis_index("lev") == lax.axis_size("lev") - 1
    vertical = vertical_ref[...]
    below = below_ref[...]
    above = jnp.where(is_last, below, above_ref[...])
    out_ref[...] = (1.0 - vertical) * below + vertical * above


def per_device(legendre, spectral, pair_low, dep_lat, dep_col, lon_steps, tilt_steps):
    pair_local, level_count, _, slot_count = spectral.shape
    wavenumber_count = slot_count - 1
    lon_count = 2 * wavenumber_count
    lat_all = legendre.shape[1]
    wave_size = lax.axis_size("wave")
    lev_size = lax.axis_size("lev")
    lat_dev = lat_all // wave_size
    slots = pl.cdiv(pair_local, GROUP) * GROUP
    extra = slots - pair_local
    if extra:
        spectral = jnp.pad(spectral, ((0, extra), (0, 0), (0, 0), (0, 0)))
        legendre = jnp.pad(legendre, ((0, extra), (0, 0), (0, 0)))
    parts = legendre_sums(pair_low, spectral, legendre, pair_local, wave_size)
    received = [swap(part, 2 * step) if step else part for step, part in enumerate(parts)]
    blocks = lon_count // LANES
    points = 2 * lat_dev * blocks
    ext_pad = parts[0].shape[1]
    select, *plans, vertical, tables = plan(
        parts[0],
        jnp.asarray(fourier_tables(wavenumber_count)),
        pair_low,
        dep_lat,
        dep_col,
        lon_steps,
        tilt_steps,
        pair_local,
        lat_dev,
        2 * wave_size * slots,
    )
    *received, select = lax.optimization_barrier((*received, select))
    pieces = []
    for piece in received:
        pieces += [piece, swap(piece, 1)]
    vmem = pl.BlockSpec(memory_space=pltpu.VMEM)
    params = pltpu.CompilerParams(vmem_limit_bytes=24 * MIB)
    operands = (
        *pieces,
        select,
        tables,
        *plans,
    )
    near = pltpu.VMEM((3, 2 * ext_pad * blocks, LANES), jnp.float32)
    flat = jax.ShapeDtypeStruct((points, LANES), jnp.float32)
    field_first, horizontal = pl.pallas_call(
        functools.partial(first_kernel, lat_dev, len(pieces)),
        in_specs=[vmem] * len(operands),
        out_specs=[vmem] * 2,
        out_shape=[jax.ShapeDtypeStruct((1, 2 * lat_dev, lon_count), jnp.float32), flat],
        scratch_shapes=[near],
        compiler_params=params,
        cost_estimate=pl.CostEstimate(
            flops=10**8, bytes_accessed=4 * 10**6, transcendentals=0
        ),
        name="first_level",
    )(*operands)
    above = lax.ppermute(horizontal, "lev", [(i, i - 1) for i in range(1, lev_size)])
    field_later, departed, top = pl.pallas_call(
        functools.partial(later_kernel, lat_dev, len(pieces)),
        in_specs=[vmem] * (len(operands) + 2),
        out_specs=[vmem] * 3,
        out_shape=[
            jax.ShapeDtypeStruct((level_count - 1, 2 * lat_dev, lon_count), jnp.float32),
            jax.ShapeDtypeStruct((level_count - 1, points, LANES), jnp.float32),
            flat,
        ],
        scratch_shapes=[near],
        compiler_params=params,
        cost_estimate=pl.CostEstimate(
            flops=10**8, bytes_accessed=4 * 10**6, transcendentals=0
        ),
        name="later_levels",
    )(*operands, vertical, horizontal)
    grid_field = jnp.concatenate([field_first, field_later], axis=0)
    final = pl.pallas_call(
        last_kernel,
        in_specs=[vmem] * 3,
        out_specs=vmem,
        out_shape=flat,
        compiler_params=params,
        name="top_level",
    )(top, above, vertical)
    departed = jnp.concatenate([departed, final[None]], axis=0)
    return grid_field, departed.reshape(level_count, 2 * lat_dev, lon_count)


def solution(mesh):
    return jax.shard_map(
        per_device,
        mesh=mesh,
        in_specs=(
            P("wave", None, None),
            P("wave", "lev", None, None),
            P(),
            P("wave"),
            P("wave"),
            P("wave", None),
            P("wave", None),
        ),
        out_specs=(P("lev", "wave", None), P("lev", "wave", None)),
        check_vma=False,
    )
```

```python
import functools
import math

import jax
import jax.numpy as jnp
import ml_dtypes
import numpy as np
from jax import lax
from jax.experimental import pallas as pl
from jax.experimental.pallas import tpu as pltpu
from jax.sharding import PartitionSpec as P

LANES = 128
GROUP = 8
HALO = 2
WAIT_AT = (0, 2)
MIB = 1024 * 1024
NT = (((1,), (1,)), ((), ()))
NN = (((1,), (0,)), ((), ()))


def split(value):
    high = value.astype(jnp.bfloat16)
    low = (value - high.astype(jnp.float32)).astype(jnp.bfloat16)
    return high, low


def widen(value, width):
    lane = lax.broadcasted_iota(jnp.int32, (value.shape[0], LANES), 1)
    full = value.shape[1] // LANES * LANES
    parts = [value[:, :full]]
    for start in range(full, value.shape[1]):
        column = jnp.broadcast_to(value[:, start : start + 1], lane.shape)
        parts.append(jnp.where(lane == start - full, column, 0.0))
    assert len(parts) <= 2 and full + LANES * (len(parts) - 1) == width
    return jnp.concatenate(parts, axis=1)


def legendre_kernel(
    pair_local,
    lat_dev,
    low_hbm,
    spec_hbm,
    leg_hbm,
    *refs,
):
    chip_refs = refs[:-7]
    low_ref, spec_ref, leg_ref, sums_ref, low_sem, spec_sem, leg_sem = refs[-7:]
    slots, lat_all, slot_count = leg_ref.shape
    level_count = spec_ref.shape[1]
    pair_total = low_ref.shape[0]
    ext_pad = sums_ref.shape[1]
    width = pl.cdiv(slot_count, LANES) * LANES
    low_copy = pltpu.make_async_copy(low_hbm, low_ref, low_sem)
    low_copy.start()
    copies = []
    for start in range(0, slots, GROUP):
        part = pl.ds(start, GROUP)
        index = start // GROUP
        pair = (
            pltpu.make_async_copy(spec_hbm.at[part], spec_ref.at[part], spec_sem.at[index]),
            pltpu.make_async_copy(leg_hbm.at[part], leg_ref.at[part], leg_sem.at[index]),
        )
        for copy in pair:
            copy.start()
        copies.append(pair)
    wave = lax.axis_index("wave")
    slot_of_row = lax.broadcasted_iota(jnp.int32, (GROUP, LANES), 0)
    slot_pos = lax.broadcasted_iota(jnp.int32, (GROUP, width), 1)
    low_copy.wait()
    groups = slots // GROUP
    for index in range(groups):
        if index in WAIT_AT:
            later = [at for at in WAIT_AT if at > index]
            for at in range(index, later[0] if later else groups):
                for copy in copies[at]:
                    copy.wait()
        start = index * GROUP
        base = wave * pair_local + start
        first = jnp.zeros((GROUP, LANES), jnp.int32)
        for slot in range(GROUP):
            low = low_ref[jnp.minimum(base + slot, pair_total - 1)]
            first = jnp.where(slot_of_row == slot, slot_count - 1 - low, first)
        first = jnp.concatenate([first] * (width // LANES), axis=1)
        second = slot_pos >= first
        sign = (1 - 2 * ((slot_pos - jnp.where(second, first, 0)) & 1)).astype(jnp.float32)
        member = [jnp.where(second, 0.0, 1.0), jnp.where(second, 1.0, 0.0)]
        masks = [
            jnp.concatenate(member, axis=0).astype(jnp.bfloat16),
            jnp.concatenate([m * sign for m in member], axis=0).astype(jnp.bfloat16),
        ]
        highs, lows = [], []
        for level in range(level_count):
            for part in range(2):
                row = widen(spec_ref[pl.ds(start, GROUP), level, part, :], width)
                high, low = split(jnp.concatenate([row, row], axis=0))
                highs += [high * mask for mask in masks]
                lows += [low * mask for mask in masks]
        columns = jnp.concatenate(highs + lows, axis=0)
        count = columns.shape[0] // 2
        half = GROUP * lat_all
        table = leg_ref[pl.ds(start, GROUP)].reshape(half, slot_count)
        rows = jnp.concatenate(split(widen(table, width)), axis=0)
        crossed = lax.dot_general(rows, columns, NT, preferred_element_type=jnp.float32)
        crossed = (crossed[:half, :count] + crossed[:half, count:]) + (
            crossed[half:, :count] + crossed[half:, count:]
        )
        slot_of_lane = lax.broadcasted_iota(jnp.int32, (lat_all, count), 1) % GROUP
        sums = crossed[:lat_all]
        for slot in range(1, GROUP):
            block = crossed[slot * lat_all : (slot + 1) * lat_all]
            sums = jnp.where(slot_of_lane == slot, block, sums)
        edge = jnp.zeros((HALO, count), jnp.float32)
        tail = jnp.zeros((ext_pad, count), jnp.float32)
        padded = jnp.concatenate([edge, sums, tail], axis=0)
        here = slice(index * count, (index + 1) * count)
        for dest in range(sums_ref.shape[0]):
            sums_ref[dest, :, here] = padded[dest * lat_dev : dest * lat_dev + ext_pad]
    for step, chip_ref in enumerate(chip_refs):
        dest = (wave // 2 ^ step) * 2
        for core in range(2):
            chip_ref[core] = sums_ref[dest + core]


def legendre_sums(pair_low, spectral, legendre, pair_local, wave_size):
    slots, level_count = spectral.shape[:2]
    lat_all, slot_count = legendre.shape[1:]
    lat_dev = lat_all // wave_size
    lanes = 8 * level_count * slots
    ext_pad = pl.cdiv(lat_dev + 2 * HALO, 8) * 8
    chips = wave_size // 2
    out = jax.ShapeDtypeStruct((2, ext_pad, lanes), jnp.float32)
    operands = [
        pltpu.with_memory_space_constraint(x, pltpu.HBM) for x in (pair_low, spectral, legendre)
    ]
    return pl.pallas_call(
        functools.partial(legendre_kernel, pair_local, lat_dev),
        in_specs=[pl.BlockSpec(memory_space=pltpu.HBM)] * 3,
        out_specs=[pl.BlockSpec(memory_space=pltpu.VMEM)] * chips,
        out_shape=[out] * chips,
        scratch_shapes=[
            pltpu.SMEM(pair_low.shape, jnp.int32),
            pltpu.VMEM(spectral.shape, jnp.float32),
            pltpu.VMEM(legendre.shape, jnp.float32),
            pltpu.VMEM((wave_size, ext_pad, lanes), jnp.float32),
            pltpu.SemaphoreType.DMA,
            pltpu.SemaphoreType.DMA((slots // GROUP,)),
            pltpu.SemaphoreType.DMA((slots // GROUP,)),
        ],
        compiler_params=pltpu.CompilerParams(vmem_limit_bytes=24 * MIB),
        name="legendre",
    )(*operands)


def swap(value, by):
    wave_size = lax.axis_size("wave")
    return lax.ppermute(value, "wave", [(i, i ^ by) for i in range(wave_size)])


def trade(value, offset):
    lev_size, wave_size = lax.axis_size("lev"), lax.axis_size("wave")
    pairs = []
    for lev in range(lev_size):
        other = lev + 1 if (lev - offset) % 2 == 0 else lev - 1
        for wave in range(wave_size):
            there = (other, wave) if 0 <= other < lev_size else (lev, wave ^ 1)
            pairs.append((lev * wave_size + wave, there[0] * wave_size + there[1]))
    return lax.ppermute(value, ("lev", "wave"), pairs)


def plan_kernel(
    pair_local,
    lat_dev,
    after_ref,
    low_hbm,
    lat_hbm,
    col_hbm,
    lon_hbm,
    tilt_hbm,
    table_hbm,
    select_ref,
    row_step_ref,
    place_ref,
    lon_frac_ref,
    lat_frac_ref,
    vertical_ref,
    table_ref,
    low_ref,
    lat_ref,
    col_ref,
    lon_ref,
    tilt_ref,
    sems,
):
    pairs = [
        (low_hbm, low_ref),
        (lat_hbm, lat_ref),
        (col_hbm, col_ref),
        (lon_hbm, lon_ref),
        (tilt_hbm, tilt_ref),
        (table_hbm, table_ref),
    ]
    copies = [
        pltpu.make_async_copy(there, here, sems.at[i]) for i, (there, here) in enumerate(pairs)
    ]
    for copy in copies:
        copy.start()
    for copy in copies[:-1]:
        copy.wait()
    wave = lax.axis_index("wave")
    half, slot_lanes = select_ref.shape
    lon_count = 2 * half
    points = lon_ref.shape[0]
    blocks = points // (2 * lat_dev)
    sources = low_ref.shape[0] // pair_local
    per_source = slot_lanes // (sources * 2 * GROUP)
    lane = lax.broadcasted_iota(jnp.int32, (GROUP, LANES), 1)
    order = lax.broadcasted_iota(jnp.int32, (half, LANES), 0)
    order = jnp.where(order < half // 2, 2 * order, 2 * order - half + 1)
    per_vector = LANES // (2 * GROUP)
    for block in range(slot_lanes // LANES):
        waves = jnp.full((GROUP, LANES), -2 * half, jnp.int32)
        for index in range(per_vector):
            source, group = divmod(block * per_vector + index, per_source)
            base = (wave ^ source) * pair_local + group * GROUP
            for slot in range(min(GROUP, pair_local - group * GROUP)):
                here = (lane & ~GROUP) == index * 2 * GROUP + slot
                waves = jnp.where(here, low_ref[base + slot], waves)
        waves = jnp.where((lane & GROUP) != 0, half - 1 - waves, waves)
        match = jnp.broadcast_to(waves[0:1], order.shape) == order
        select_ref[:, block * LANES : (block + 1) * LANES] = jnp.where(match, 1.0, 0.0).astype(
            jnp.bfloat16
        )
    row = lax.broadcasted_iota(jnp.int32, (points, LANES), 0)
    point = lax.broadcasted_iota(jnp.int32, (points, LANES), 1)
    row_step = jnp.zeros((points, LANES), jnp.int32)
    col_step = jnp.zeros((points, LANES), jnp.int32)
    for index in range(points):
        own = wave * lat_dev + index // blocks % lat_dev - HALO
        row_step = jnp.where(row == index, lat_ref[index] - own, row_step)
        first = LANES * (index % blocks)
        col_step = jnp.where(row == index, col_ref[index] - first, col_step)
    col_step = jnp.where(col_step >= half, col_step - lon_count, col_step)
    col_step = jnp.where(col_step < -half, col_step + lon_count, col_step)
    quarters = 4 * col_step + lon_ref[...] - 12
    row_step_ref[...] = row_step
    place_ref[...] = point + (quarters >> 2)
    lon_frac_ref[...] = (quarters & 3).astype(jnp.float32) * 0.25
    lat_frac_ref[...] = (tilt_ref[...] & 3).astype(jnp.float32) * 0.25
    vertical_ref[...] = (tilt_ref[...] >> 2).astype(jnp.float32) * 0.25
    copies[-1].wait()


def plan(after, tables, pair_low, dep_lat, dep_col, lon_steps, tilt_steps, pair_local, lat_dev, lanes):
    vmem = pl.BlockSpec(memory_space=pltpu.VMEM)
    whole = jax.ShapeDtypeStruct(lon_steps.shape, jnp.int32)
    fraction = jax.ShapeDtypeStruct(lon_steps.shape, jnp.float32)
    half = tables.shape[1]
    operands = [
        pltpu.with_memory_space_constraint(x, pltpu.HBM)
        for x in (pair_low, dep_lat, dep_col, lon_steps, tilt_steps, tables)
    ]
    return pl.pallas_call(
        functools.partial(plan_kernel, pair_local, lat_dev),
        in_specs=[pl.BlockSpec(memory_space=pl.ANY)]
        + [pl.BlockSpec(memory_space=pltpu.HBM)] * len(operands),
        out_specs=[vmem] * 7,
        out_shape=[
            jax.ShapeDtypeStruct((half, lanes), jnp.bfloat16),
            whole,
            whole,
            fraction,
            fraction,
            fraction,
            jax.ShapeDtypeStruct(tables.shape, tables.dtype),
        ],
        scratch_shapes=[
            pltpu.SMEM(pair_low.shape, jnp.int32),
            pltpu.SMEM(dep_lat.shape, jnp.int32),
            pltpu.SMEM(dep_col.shape, jnp.int32),
            pltpu.VMEM(lon_steps.shape, jnp.int32),
            pltpu.VMEM(tilt_steps.shape, jnp.int32),
            pltpu.SemaphoreType.DMA((len(operands),)),
        ],
        compiler_params=pltpu.CompilerParams(vmem_limit_bytes=24 * MIB),
        cost_estimate=pl.CostEstimate(
            flops=10**7, bytes_accessed=4 * 10**6, transcendentals=0
        ),
        name="plan",
    )(after, *operands)


def fourier_tables(wavenumber_count):
    lon_count = 2 * wavenumber_count
    half_lon = lon_count // 2
    tables = []
    for parity in range(2):
        wave = np.arange(parity, wavenumber_count, 2)
        phase = wave[:, None] * np.arange(half_lon)[None, :] % lon_count
        angle = phase * (2.0 * math.pi / lon_count)
        weight = np.where(wave == 0, 1.0, 2.0)[:, None]
        parts = [weight * np.cos(angle), -weight * np.sin(angle)]
        tables.append(np.concatenate(parts if parity == 0 else parts[::-1], axis=0))
    exact = np.stack(tables)
    high = exact.astype(ml_dtypes.bfloat16)
    low = (exact - high.astype(np.float64)).astype(ml_dtypes.bfloat16)
    return np.concatenate([high, low], axis=2)


def regroup(pieces, level, lane):
    piece_lanes = LANES // 8
    upper = lane // piece_lanes >= 4
    if level == 0:
        pieces = [
            jnp.where(upper, pltpu.roll(pieces[i + 4], 4 * piece_lanes, 1), pieces[i])
            for i in range(4)
        ]
    else:
        pieces = [
            jnp.where(upper, pieces[i + 4], pltpu.roll(pieces[i], 4 * piece_lanes, 1))
            for i in range(4)
        ]
    for bit in (1, 2):
        upper = (lane // piece_lanes & bit) != 0
        for one in range(4):
            if one & bit:
                continue
            a, b = pieces[one], pieces[one | bit]
            pieces[one] = jnp.where(upper, pltpu.roll(b, piece_lanes * bit, 1), a)
            pieces[one | bit] = jnp.where(
                upper, b, pltpu.roll(a, LANES - piece_lanes * bit, 1)
            )
    return pieces


def level_rows(level, piece_refs, select_ref, table_ref):
    half = table_ref.shape[2] // 2
    core = lax.axis_index("wave") % 2
    vectors = []
    for ref in piece_refs:
        source = ref[core]
        vectors += [
            source[:, start : start + LANES] for start in range(0, source.shape[1], LANES)
        ]
    lane = lax.broadcasted_iota(jnp.int32, vectors[0].shape, 1)
    columns = [[] for _ in range(4)]
    for start in range(0, len(vectors), 8):
        for kind, piece in enumerate(regroup(vectors[start : start + 8], level, lane)):
            columns[kind].append(piece)
    matrix = jnp.concatenate([jnp.concatenate(c, axis=1) for c in columns], axis=0)
    high, low = split(matrix)
    count = high.shape[0] // 2
    ordered = lax.dot_general(
        jnp.concatenate([high[:count], low[:count], high[count:], low[count:]], axis=0),
        select_ref[...],
        NT,
        preferred_element_type=jnp.float32,
    )
    real = ordered[: 2 * count]
    imag = pltpu.roll(ordered[2 * count :], half // 2, 1)
    first_half = lax.broadcasted_iota(jnp.int32, real.shape, 1) < half // 2
    even = jnp.where(first_half, real, imag).astype(jnp.bfloat16)
    odd = jnp.where(first_half, imag, real).astype(jnp.bfloat16)
    sums = []
    for parity, operand in enumerate((even, odd)):
        main = lax.dot_general(
            operand, table_ref[parity], NN, preferred_element_type=jnp.float32
        )
        sums.append(main[:count, :half] + (main[count:, :half] + main[:count, half:]))
    return sums


def interpolate(sums, field_ref, level, lat_dev, row_step, step, f, g, near_ref):
    half = sums[0].shape[1]
    count = sums[0].shape[0]
    ext_pad = count // 2
    blocks = 2 * half // LANES
    for block in range(blocks // 2):
        here = slice(block * LANES, (block + 1) * LANES)
        for at, rows in (
            (block, sums[0][:, here] + sums[1][:, here]),
            (block + blocks // 2, sums[0][:, here] - sums[1][:, here]),
        ):
            there = slice(at * LANES, (at + 1) * LANES)
            for hemi in range(2):
                start = hemi * ext_pad + HALO
                field_ref[level, hemi * lat_dev : (hemi + 1) * lat_dev, there] = rows[
                    start : start + lat_dev
                ]
            for side in range(3):
                place = (at + 1 - side) % blocks
                near_ref[side, pl.ds(place, count, stride=blocks), :] = rows
    points = 2 * lat_dev * blocks
    point = lax.broadcasted_iota(jnp.int32, (points, LANES), 1)

    def line(side, j):
        return jnp.concatenate(
            [
                near_ref[side, pl.ds((hemi * ext_pad + j) * blocks, lat_dev * blocks), :]
                for hemi in range(2)
            ],
            axis=0,
        )

    lines = [[line(side, j) for j in range(2 * HALO + 1)] for side in range(3)]
    values = []
    for upper in range(2):
        picked = []
        for side in range(3):
            choice = lines[side][upper]
            for j in range(1, 2 * HALO):
                choice = jnp.where(row_step == j, lines[side][j + upper], choice)
            picked.append(choice)
        left = jnp.where(point >= LANES - 28, picked[0], picked[1])
        right = jnp.where(point < 28, picked[2], picked[1])
        for shift in range(2):
            place = (step + shift) & (LANES - 1)
            values.append(
                jnp.where(
                    point < LANES // 2,
                    jnp.take_along_axis(left, place, axis=1),
                    jnp.take_along_axis(right, place, axis=1),
                )
            )
    lower = (1.0 - f) * values[0] + f * values[1]
    higher = (1.0 - f) * values[2] + f * values[3]
    return (1.0 - g) * lower + g * higher


def first_kernel(lat_dev, piece_count, *refs):
    piece_refs, plan_refs = refs[:piece_count], refs[piece_count + 2 : -3]
    select_ref, table_ref = refs[piece_count : piece_count + 2]
    field_ref, horizontal_ref, near_ref = refs[-3:]
    sums = level_rows(0, piece_refs, select_ref, table_ref)
    plans = [ref[...] for ref in plan_refs]
    horizontal_ref[...] = interpolate(sums, field_ref, 0, lat_dev, *plans, near_ref)


def later_kernel(lat_dev, piece_count, *refs):
    piece_refs, plan_refs = refs[:piece_count], refs[piece_count + 2 : -6]
    select_ref, table_ref = refs[piece_count : piece_count + 2]
    vertical_ref, below_ref, field_ref, departed_ref, horizontal_ref, near_ref = refs[-6:]
    vertical = vertical_ref[...]
    below = below_ref[...]
    plans = [ref[...] for ref in plan_refs]
    for level in range(1, departed_ref.shape[0] + 1):
        sums = level_rows(level, piece_refs, select_ref, table_ref)
        horizontal = interpolate(sums, field_ref, level - 1, lat_dev, *plans, near_ref)
        departed_ref[level - 1] = (1.0 - vertical) * below + vertical * horizontal
        below = horizontal
    horizontal_ref[...] = below


def last_kernel(below_ref, even_ref, odd_ref, vertical_ref, out_ref):
    lev = lax.axis_index("lev")
    is_last = lev == lax.axis_size("lev") - 1
    vertical = vertical_ref[...]
    below = below_ref[...]
    above = jnp.where(lev % 2 == 0, even_ref[...], odd_ref[...])
    above = jnp.where(is_last, below, above)
    out_ref[...] = (1.0 - vertical) * below + vertical * above


def per_device(legendre, spectral, pair_low, dep_lat, dep_col, lon_steps, tilt_steps):
    pair_local, level_count, _, slot_count = spectral.shape
    wavenumber_count = slot_count - 1
    lon_count = 2 * wavenumber_count
    lat_all = legendre.shape[1]
    wave_size = lax.axis_size("wave")
    lat_dev = lat_all // wave_size
    slots = pl.cdiv(pair_local, GROUP) * GROUP
    extra = slots - pair_local
    if extra:
        spectral = jnp.pad(spectral, ((0, extra), (0, 0), (0, 0), (0, 0)))
        legendre = jnp.pad(legendre, ((0, extra), (0, 0), (0, 0)))
    parts = legendre_sums(pair_low, spectral, legendre, pair_local, wave_size)
    received = [swap(part, 2 * step) if step else part for step, part in enumerate(parts)]
    blocks = lon_count // LANES
    points = 2 * lat_dev * blocks
    ext_pad = parts[0].shape[1]
    select, *plans, vertical, tables = plan(
        parts[0],
        jnp.asarray(fourier_tables(wavenumber_count)),
        pair_low,
        dep_lat,
        dep_col,
        lon_steps,
        tilt_steps,
        pair_local,
        lat_dev,
        2 * wave_size * slots,
    )
    if len(received) > 1:
        received[1], select = lax.optimization_barrier((received[1], select))
    pieces = []
    for piece in received:
        pieces += [piece, swap(piece, 1)]
    vmem = pl.BlockSpec(memory_space=pltpu.VMEM)
    params = pltpu.CompilerParams(vmem_limit_bytes=24 * MIB)
    operands = (
        *pieces,
        select,
        tables,
        *plans,
    )
    near = pltpu.VMEM((3, 2 * ext_pad * blocks, LANES), jnp.float32)
    flat = jax.ShapeDtypeStruct((points, LANES), jnp.float32)
    field_first, horizontal = pl.pallas_call(
        functools.partial(first_kernel, lat_dev, len(pieces)),
        in_specs=[vmem] * len(operands),
        out_specs=[vmem] * 2,
        out_shape=[jax.ShapeDtypeStruct((1, 2 * lat_dev, lon_count), jnp.float32), flat],
        scratch_shapes=[near],
        compiler_params=params,
        cost_estimate=pl.CostEstimate(
            flops=10**8, bytes_accessed=4 * 10**6, transcendentals=0
        ),
        name="first_level",
    )(*operands)
    above_even = trade(horizontal, 0)
    above_odd = trade(horizontal, 1)
    field_later, departed, top = pl.pallas_call(
        functools.partial(later_kernel, lat_dev, len(pieces)),
        in_specs=[vmem] * (len(operands) + 2),
        out_specs=[vmem] * 3,
        out_shape=[
            jax.ShapeDtypeStruct((level_count - 1, 2 * lat_dev, lon_count), jnp.float32),
            jax.ShapeDtypeStruct((level_count - 1, points, LANES), jnp.float32),
            flat,
        ],
        scratch_shapes=[near],
        compiler_params=params,
        cost_estimate=pl.CostEstimate(
            flops=10**8, bytes_accessed=4 * 10**6, transcendentals=0
        ),
        name="later_levels",
    )(*operands, vertical, horizontal)
    grid_field = jnp.concatenate([field_first, field_later], axis=0)
    final = pl.pallas_call(
        last_kernel,
        in_specs=[vmem] * 4,
        out_specs=vmem,
        out_shape=flat,
        compiler_params=params,
        name="top_level",
    )(top, above_even, above_odd, vertical)
    departed = jnp.concatenate([departed, final[None]], axis=0)
    return grid_field, departed.reshape(level_count, 2 * lat_dev, lon_count)


def solution(mesh):
    return jax.shard_map(
        per_device,
        mesh=mesh,
        in_specs=(
            P("wave", None, None),
            P("wave", "lev", None, None),
            P(),
            P("wave"),
            P("wave"),
            P("wave", None),
            P("wave", None),
        ),
        out_specs=(P("lev", "wave", None), P("lev", "wave", None)),
        check_vma=False,
    )
```

```python
import functools
import math

import jax
import jax.numpy as jnp
import ml_dtypes
import numpy as np
from jax import lax
from jax.experimental import pallas as pl
from jax.experimental.pallas import tpu as pltpu
from jax.sharding import PartitionSpec as P

LANES = 128
GROUP = 8
HALO = 2
WAIT_AT = (0, 2)
MIB = 1024 * 1024
FAR = -(2**20)
ORDER = (0, 2, 1, 3)
NT = (((1,), (1,)), ((), ()))
NN = (((1,), (0,)), ((), ()))


def split(value):
    high = value.astype(jnp.bfloat16)
    low = (value - high.astype(jnp.float32)).astype(jnp.bfloat16)
    return high, low


def widen(value, width):
    lane = lax.broadcasted_iota(jnp.int32, (value.shape[0], LANES), 1)
    full = value.shape[1] // LANES * LANES
    parts = [value[:, :full]]
    for start in range(full, value.shape[1]):
        column = jnp.broadcast_to(value[:, start : start + 1], lane.shape)
        parts.append(jnp.where(lane == start - full, column, 0.0))
    assert len(parts) <= 2 and full + LANES * (len(parts) - 1) == width
    return jnp.concatenate(parts, axis=1)


def wave_rows(low_ref, wave, pair_local, waves_ref):
    row = lax.broadcasted_iota(jnp.int32, (GROUP, LANES), 0)
    groups = pl.cdiv(pair_local, GROUP)
    for index in range(waves_ref.shape[0] // GROUP):
        source, group = divmod(index, groups)
        base = (wave ^ source) * pair_local + group * GROUP
        value = jnp.full((GROUP, LANES), FAR, jnp.int32)
        for slot in range(min(GROUP, pair_local - group * GROUP)):
            value = jnp.where(row == slot, low_ref[base + slot], value)
        waves_ref[index * GROUP : (index + 1) * GROUP] = value


def departure(wave, lat_dev, half, lat_ref, col_ref, lon, tilt, out_refs):
    row_step_ref, place_ref, lon_frac_ref, lat_frac_ref, vertical_ref = out_refs
    points = lon.shape[0]
    blocks = points // (2 * lat_dev)
    row = lax.broadcasted_iota(jnp.int32, lon.shape, 0)
    point = lax.broadcasted_iota(jnp.int32, lon.shape, 1)
    row_step = jnp.zeros(lon.shape, jnp.int32)
    col_step = jnp.zeros(lon.shape, jnp.int32)
    for index in range(points):
        own = wave * lat_dev + index // blocks % lat_dev - HALO
        row_step = jnp.where(row == index, lat_ref[index] - own, row_step)
        first = LANES * (index % blocks)
        col_step = jnp.where(row == index, col_ref[index] - first, col_step)
    col_step = jnp.where(col_step >= half, col_step - 2 * half, col_step)
    col_step = jnp.where(col_step < -half, col_step + 2 * half, col_step)
    quarters = 4 * col_step + lon - 12
    row_step_ref[...] = row_step
    place_ref[...] = point + (quarters >> 2)
    lon_frac_ref[...] = (quarters & 3).astype(jnp.float32) * 0.25
    lat_frac_ref[...] = (tilt & 3).astype(jnp.float32) * 0.25
    vertical_ref[...] = (tilt >> 2).astype(jnp.float32) * 0.25


def legendre_kernel(pair_local, lat_dev, *refs):
    low_hbm, spec_hbm, leg_hbm, table_hbm = refs[:4]
    *chip_refs, table_ref = refs[4:-7]
    low_ref, spec_ref, leg_ref, sums_ref, small_sem, spec_sem, leg_sem = refs[-7:]
    slots, lat_all, slot_count = leg_ref.shape
    level_count = spec_ref.shape[1]
    pair_total = low_ref.shape[0]
    ext_pad = sums_ref.shape[1]
    width = pl.cdiv(slot_count, LANES) * LANES
    low_copy = pltpu.make_async_copy(low_hbm, low_ref, small_sem.at[0])
    table_copy = pltpu.make_async_copy(table_hbm, table_ref, small_sem.at[1])
    low_copy.start()
    copies = []
    for start in range(0, slots, GROUP):
        part = pl.ds(start, GROUP)
        index = start // GROUP
        pair = (
            pltpu.make_async_copy(spec_hbm.at[part], spec_ref.at[part], spec_sem.at[index]),
            pltpu.make_async_copy(leg_hbm.at[part], leg_ref.at[part], leg_sem.at[index]),
        )
        for copy in pair:
            copy.start()
        copies.append(pair)
    table_copy.start()
    wave = lax.axis_index("wave")
    slot_of_row = lax.broadcasted_iota(jnp.int32, (GROUP, LANES), 0)
    slot_pos = lax.broadcasted_iota(jnp.int32, (GROUP, width), 1)
    low_copy.wait()
    groups = slots // GROUP
    for index in range(groups):
        if index in WAIT_AT:
            later = [at for at in WAIT_AT if at > index]
            for at in range(index, later[0] if later else groups):
                for copy in copies[at]:
                    copy.wait()
        start = index * GROUP
        base = wave * pair_local + start
        first = jnp.zeros((GROUP, LANES), jnp.int32)
        for slot in range(GROUP):
            low = low_ref[jnp.minimum(base + slot, pair_total - 1)]
            first = jnp.where(slot_of_row == slot, slot_count - 1 - low, first)
        first = jnp.concatenate([first] * (width // LANES), axis=1)
        second = slot_pos >= first
        sign = (1 - 2 * ((slot_pos - jnp.where(second, first, 0)) & 1)).astype(jnp.float32)
        member = [jnp.where(second, 0.0, 1.0), jnp.where(second, 1.0, 0.0)]
        masks = [
            jnp.concatenate(member, axis=0).astype(jnp.bfloat16),
            jnp.concatenate([m * sign for m in member], axis=0).astype(jnp.bfloat16),
        ]
        highs, lows = [], []
        for level in range(level_count):
            for part in range(2):
                row = widen(spec_ref[pl.ds(start, GROUP), level, part, :], width)
                high, low = split(jnp.concatenate([row, row], axis=0))
                highs += [high * mask for mask in masks]
                lows += [low * mask for mask in masks]
        columns = jnp.concatenate(highs + lows, axis=0)
        count = columns.shape[0] // 2
        half = GROUP * lat_all
        table = leg_ref[pl.ds(start, GROUP)].reshape(half, slot_count)
        rows = jnp.concatenate(split(widen(table, width)), axis=0)
        crossed = lax.dot_general(rows, columns, NT, preferred_element_type=jnp.float32)
        crossed = (crossed[:half, :count] + crossed[:half, count:]) + (
            crossed[half:, :count] + crossed[half:, count:]
        )
        slot_of_lane = lax.broadcasted_iota(jnp.int32, (lat_all, count), 1) % GROUP
        sums = crossed[:lat_all]
        for slot in range(1, GROUP):
            block = crossed[slot * lat_all : (slot + 1) * lat_all]
            sums = jnp.where(slot_of_lane == slot, block, sums)
        edge = jnp.zeros((HALO, count), jnp.float32)
        tail = jnp.zeros((ext_pad, count), jnp.float32)
        padded = jnp.concatenate([edge, sums, tail], axis=0)
        here = slice(index * count, (index + 1) * count)
        for dest in range(sums_ref.shape[0]):
            sums_ref[dest, :, here] = padded[dest * lat_dev : dest * lat_dev + ext_pad]
    for step, chip_ref in enumerate(chip_refs):
        dest = (wave // 2 ^ step) * 2
        for core in range(2):
            chip_ref[core] = sums_ref[dest + core]
    table_copy.wait()


def legendre_sums(operands, pair_local, wave_size):
    pair_low, spectral, legendre, tables = operands
    slots, level_count = spectral.shape[:2]
    lat_all = legendre.shape[1]
    lat_dev = lat_all // wave_size
    lanes = 8 * level_count * slots
    ext_pad = pl.cdiv(lat_dev + 2 * HALO, 8) * 8
    chips = wave_size // 2
    out = jax.ShapeDtypeStruct((2, ext_pad, lanes), jnp.float32)
    outs = [out] * chips + [jax.ShapeDtypeStruct(tables.shape, tables.dtype)]
    results = pl.pallas_call(
        functools.partial(legendre_kernel, pair_local, lat_dev),
        in_specs=[pl.BlockSpec(memory_space=pltpu.HBM)] * len(operands),
        out_specs=[pl.BlockSpec(memory_space=pltpu.VMEM)] * len(outs),
        out_shape=outs,
        scratch_shapes=[
            pltpu.SMEM(pair_low.shape, jnp.int32),
            pltpu.VMEM(spectral.shape, jnp.float32),
            pltpu.VMEM(legendre.shape, jnp.float32),
            pltpu.VMEM((wave_size, ext_pad, lanes), jnp.float32),
            pltpu.SemaphoreType.DMA((2,)),
            pltpu.SemaphoreType.DMA((slots // GROUP,)),
            pltpu.SemaphoreType.DMA((slots // GROUP,)),
        ],
        compiler_params=pltpu.CompilerParams(vmem_limit_bytes=24 * MIB),
        name="legendre",
    )(*[pltpu.with_memory_space_constraint(x, pltpu.HBM) for x in operands])
    return results[:chips], results[chips]


def swap(value, by):
    wave_size = lax.axis_size("wave")
    return lax.ppermute(value, "wave", [(i, i ^ by) for i in range(wave_size)])


def trade(value, offset):
    lev_size, wave_size = lax.axis_size("lev"), lax.axis_size("wave")
    pairs = []
    for lev in range(lev_size):
        other = lev + 1 if (lev - offset) % 2 == 0 else lev - 1
        for wave in range(wave_size):
            there = (other, wave) if 0 <= other < lev_size else (lev, wave ^ 1)
            pairs.append((lev * wave_size + wave, there[0] * wave_size + there[1]))
    return lax.ppermute(value, ("lev", "wave"), pairs)


def plan_kernel(pair_local, lat_dev, after_ref, *refs):
    sources = refs[:5]
    select_ref, *plan_refs = refs[5:-7]
    low_ref, lat_ref, col_ref, lon_ref, tilt_ref, waves_ref, sems = refs[-7:]
    copies = [
        pltpu.make_async_copy(there, here, sems.at[i])
        for i, (there, here) in enumerate(zip(sources, refs[-7:-2], strict=True))
    ]
    for copy in copies:
        copy.start()
    half = select_ref.shape[1]
    quarter = half // 4
    lane = lax.broadcasted_iota(jnp.int32, (2 * GROUP, half), 1)
    kind = sum((lane >= quarter * i).astype(jnp.int32) for i in range(1, 4))
    order = 4 * (lane - quarter * kind)
    for i, first in enumerate(ORDER):
        order = jnp.where(kind == i, order + first, order)
    wave = lax.axis_index("wave")
    for copy in copies:
        copy.wait()
    departure(wave, lat_dev, half, lat_ref, col_ref, lon_ref[...], tilt_ref[...], plan_refs)
    wave_rows(low_ref, wave, pair_local, waves_ref)
    for start in range(0, waves_ref.shape[0], GROUP):
        waves = waves_ref[start : start + GROUP]
        waves = jnp.concatenate([waves, half - 1 - waves], axis=0)
        waves = jnp.concatenate([waves] * (half // LANES), axis=1)
        match = jnp.where(waves == order, 1.0, 0.0).astype(jnp.bfloat16)
        select_ref[2 * start : 2 * (start + GROUP)] = match


def plan(after, pair_low, dep_lat, dep_col, lon_steps, tilt_steps, pair_local, lat_dev, slots, half):
    operands = (pair_low, dep_lat, dep_col, lon_steps, tilt_steps)
    integer = jax.ShapeDtypeStruct(lon_steps.shape, jnp.int32)
    fraction = jax.ShapeDtypeStruct(lon_steps.shape, jnp.float32)
    outs = [
        jax.ShapeDtypeStruct((2 * slots, half), jnp.bfloat16),
        integer,
        integer,
        fraction,
        fraction,
        fraction,
    ]
    return pl.pallas_call(
        functools.partial(plan_kernel, pair_local, lat_dev),
        in_specs=[pl.BlockSpec(memory_space=pl.ANY)]
        + [pl.BlockSpec(memory_space=pltpu.HBM)] * len(operands),
        out_specs=[pl.BlockSpec(memory_space=pltpu.VMEM)] * len(outs),
        out_shape=outs,
        scratch_shapes=[
            pltpu.SMEM(pair_low.shape, jnp.int32),
            pltpu.SMEM(dep_lat.shape, jnp.int32),
            pltpu.SMEM(dep_col.shape, jnp.int32),
            pltpu.VMEM(lon_steps.shape, jnp.int32),
            pltpu.VMEM(tilt_steps.shape, jnp.int32),
            pltpu.VMEM((slots, LANES), jnp.int32),
            pltpu.SemaphoreType.DMA((len(operands),)),
        ],
        compiler_params=pltpu.CompilerParams(vmem_limit_bytes=24 * MIB),
        cost_estimate=pl.CostEstimate(
            flops=10**7, bytes_accessed=4 * 10**6, transcendentals=0
        ),
        name="plan",
    )(after, *[pltpu.with_memory_space_constraint(x, pltpu.HBM) for x in operands])


def fourier_tables(wavenumber_count):
    lon_count = 2 * wavenumber_count
    quarter = lon_count // 4
    whole = quarter // LANES * LANES
    tables = []
    for parity in range(2):
        kinds = ORDER[2 * parity : 2 * parity + 2]
        wave = np.concatenate([np.arange(kind, wavenumber_count, 4) for kind in kinds])
        phase = wave[:, None] * np.arange(quarter)[None, :] % lon_count
        angle = phase * (2.0 * math.pi / lon_count)
        weight = np.where(wave == 0, 1.0, 2.0)[:, None]
        parts = [weight * np.cos(angle), -weight * np.sin(angle)]
        tables.append(np.concatenate(parts if parity == 0 else parts[::-1], axis=0))
    exact = np.stack(tables)
    high = exact.astype(ml_dtypes.bfloat16)
    low = (exact - high.astype(np.float64)).astype(ml_dtypes.bfloat16)
    return np.concatenate(
        [high[..., :whole], low[..., :whole], high[..., whole:], low[..., whole:]], axis=2
    )


def add_halves(product, start, count):
    high = product[start : start + count]
    low = product[start + count : start + 2 * count]
    whole = (product.shape[1] - LANES) // 2
    tail = high[:, 2 * whole :]
    tail = tail + (low[:, 2 * whole :] + pltpu.roll(tail, LANES // 2, 1))
    pieces = [
        high[:, at : at + LANES] + (low[:, at : at + LANES] + high[:, whole + at : whole + at + LANES])
        for at in range(0, whole, LANES)
    ]
    return pieces + [tail]


def join(first, second):
    lane = lax.broadcasted_iota(jnp.int32, first[0].shape, 1)
    rolled = [pltpu.roll(piece, LANES // 2, 1) for piece in second]
    before = [first[-1], *rolled[:-1]]
    return first[:-1] + [
        jnp.where(lane < LANES // 2, a, b) for a, b in zip(before, rolled, strict=True)
    ]


def regroup(pieces, level, lane):
    piece_lanes = LANES // 8
    upper = lane // piece_lanes >= 4
    if level == 0:
        pieces = [
            jnp.where(upper, pltpu.roll(pieces[i + 4], 4 * piece_lanes, 1), pieces[i])
            for i in range(4)
        ]
    else:
        pieces = [
            jnp.where(upper, pieces[i + 4], pltpu.roll(pieces[i], 4 * piece_lanes, 1))
            for i in range(4)
        ]
    for bit in (1, 2):
        upper = (lane // piece_lanes & bit) != 0
        for one in range(4):
            if one & bit:
                continue
            a, b = pieces[one], pieces[one | bit]
            pieces[one] = jnp.where(upper, pltpu.roll(b, piece_lanes * bit, 1), a)
            pieces[one | bit] = jnp.where(
                upper, b, pltpu.roll(a, LANES - piece_lanes * bit, 1)
            )
    return pieces


def level_rows(level, piece_refs, select_ref, table_ref):
    half = table_ref.shape[2] // 2
    core = lax.axis_index("wave") % 2
    vectors = []
    for ref in piece_refs:
        source = ref[core]
        vectors += [
            source[:, start : start + LANES] for start in range(0, source.shape[1], LANES)
        ]
    lane = lax.broadcasted_iota(jnp.int32, vectors[0].shape, 1)
    columns = [[] for _ in range(4)]
    for start in range(0, len(vectors), 8):
        for kind, piece in enumerate(regroup(vectors[start : start + 8], level, lane)):
            columns[kind].append(piece)
    matrix = jnp.concatenate([jnp.concatenate(c, axis=1) for c in columns], axis=0)
    high, low = split(matrix)
    count = high.shape[0] // 2
    ordered = lax.dot_general(
        jnp.concatenate([high[:count], low[:count], high[count:], low[count:]], axis=0),
        select_ref[...],
        NN,
        preferred_element_type=jnp.float32,
    )
    half = ordered.shape[1]
    real = ordered[: 2 * count]
    imag = pltpu.roll(ordered[2 * count :], half // 2, 1)
    lane = lax.broadcasted_iota(jnp.int32, real.shape, 1)
    first_half = lane < half // 2
    outer = (lane < half // 4) | (lane >= half // 4 * 3)
    even = jnp.where(first_half, real, imag)
    odd = jnp.where(first_half, imag, real)
    turned = pltpu.roll(odd, half // 2, 1)
    even_turned = jnp.where(first_half == outer, even, -even)
    odd_turned = jnp.where(outer, turned, -turned)
    products = [
        lax.dot_general(
            jnp.concatenate(rows, axis=0).astype(jnp.bfloat16),
            table_ref[parity],
            NN,
            preferred_element_type=jnp.float32,
        )
        for parity, rows in enumerate(((even, even_turned), (odd, odd_turned)))
    ]
    near, far = [
        [add_halves(product, start, count) for product in products] for start in (0, 2 * count)
    ]
    first = join(
        [a + b for a, b in zip(*near, strict=True)], [a + b for a, b in zip(*far, strict=True)]
    )
    later = join(
        [a - b for a, b in zip(*near, strict=True)], [a - b for a, b in zip(*far, strict=True)]
    )
    return first + later


def store_rows(rows, field_ref, level, lat_dev, near_ref):
    blocks = len(rows)
    count = rows[0].shape[0]
    for at, value in enumerate(rows):
        there = slice(at * LANES, (at + 1) * LANES)
        for hemi in range(2):
            start = hemi * (count // 2) + HALO
            field_ref[level, hemi * lat_dev : (hemi + 1) * lat_dev, there] = value[
                start : start + lat_dev
            ]
        for side in range(3):
            place = (at + 1 - side) % blocks
            near_ref[side, pl.ds(place, count, stride=blocks), :] = value


def interpolate(lat_dev, row_step, step, f, g, near_ref):
    blocks = row_step.shape[0] // (2 * lat_dev)
    ext_pad = near_ref.shape[1] // (2 * blocks)
    points = 2 * lat_dev * blocks
    point = lax.broadcasted_iota(jnp.int32, (points, LANES), 1)

    def line(side, j):
        return jnp.concatenate(
            [
                near_ref[side, pl.ds((hemi * ext_pad + j) * blocks, lat_dev * blocks), :]
                for hemi in range(2)
            ],
            axis=0,
        )

    lines = [[line(side, j) for j in range(2 * HALO + 1)] for side in range(3)]
    values = []
    for upper in range(2):
        picked = []
        for side in range(3):
            choice = lines[side][upper]
            for j in range(1, 2 * HALO):
                choice = jnp.where(row_step == j, lines[side][j + upper], choice)
            picked.append(choice)
        left = jnp.where(point >= LANES - 28, picked[0], picked[1])
        right = jnp.where(point < 28, picked[2], picked[1])
        for shift in range(2):
            place = (step + shift) & (LANES - 1)
            values.append(
                jnp.where(
                    point < LANES // 2,
                    jnp.take_along_axis(left, place, axis=1),
                    jnp.take_along_axis(right, place, axis=1),
                )
            )
    lower = (1.0 - f) * values[0] + f * values[1]
    higher = (1.0 - f) * values[2] + f * values[3]
    return (1.0 - g) * lower + g * higher


def first_kernel(lat_dev, piece_count, *refs):
    piece_refs, plan_refs = refs[:piece_count], refs[piece_count + 2 : -3]
    select_ref, table_ref = refs[piece_count : piece_count + 2]
    field_ref, horizontal_ref, near_ref = refs[-3:]
    rows = level_rows(0, piece_refs, select_ref, table_ref)
    store_rows(rows, field_ref, 0, lat_dev, near_ref)
    horizontal_ref[...] = interpolate(lat_dev, *[ref[...] for ref in plan_refs], near_ref)


def later_kernel(lat_dev, piece_count, *refs):
    piece_refs, plan_refs = refs[:piece_count], refs[piece_count + 2 : -9]
    select_ref, table_ref = refs[piece_count : piece_count + 2]
    vertical_ref, below_ref, first_ref = refs[-9:-6]
    field_hbm, departed_ref, horizontal_ref, field_ref, near_ref, sems = refs[-6:]
    copies = [pltpu.make_async_copy(first_ref, field_hbm.at[pl.ds(0, 1)], sems.at[0])]
    copies[0].start()
    vertical = vertical_ref[...]
    below = below_ref[...]
    plans = [ref[...] for ref in plan_refs]
    for level in range(1, departed_ref.shape[0] + 1):
        rows = level_rows(level, piece_refs, select_ref, table_ref)
        store_rows(rows, field_ref, level - 1, lat_dev, near_ref)
        copy = pltpu.make_async_copy(
            field_ref.at[pl.ds(level - 1, 1)], field_hbm.at[pl.ds(level, 1)], sems.at[level]
        )
        copy.start()
        copies.append(copy)
        horizontal = interpolate(lat_dev, *plans, near_ref)
        departed_ref[level - 1] = (1.0 - vertical) * below + vertical * horizontal
        below = horizontal
    horizontal_ref[...] = below
    for copy in copies:
        copy.wait()


def last_kernel(below_ref, even_ref, odd_ref, vertical_ref, out_ref):
    lev = lax.axis_index("lev")
    is_last = lev == lax.axis_size("lev") - 1
    vertical = vertical_ref[...]
    below = below_ref[...]
    above = jnp.where(lev % 2 == 0, even_ref[...], odd_ref[...])
    above = jnp.where(is_last, below, above)
    out_ref[...] = (1.0 - vertical) * below + vertical * above


def per_device(legendre, spectral, pair_low, dep_lat, dep_col, lon_steps, tilt_steps):
    pair_local, level_count, _, slot_count = spectral.shape
    wavenumber_count = slot_count - 1
    lon_count = 2 * wavenumber_count
    lat_all = legendre.shape[1]
    wave_size = lax.axis_size("wave")
    lat_dev = lat_all // wave_size
    slots = pl.cdiv(pair_local, GROUP) * GROUP
    extra = slots - pair_local
    if extra:
        spectral = jnp.pad(spectral, ((0, extra), (0, 0), (0, 0), (0, 0)))
        legendre = jnp.pad(legendre, ((0, extra), (0, 0), (0, 0)))
    tables = jnp.asarray(fourier_tables(wavenumber_count))
    parts, tables = legendre_sums(
        (pair_low, spectral, legendre, tables), pair_local, wave_size
    )
    received = [swap(part, 2 * step) if step else part for step, part in enumerate(parts)]
    select, *plans, vertical = plan(
        parts[0],
        pair_low,
        dep_lat,
        dep_col,
        lon_steps,
        tilt_steps,
        pair_local,
        lat_dev,
        wave_size * slots,
        wavenumber_count,
    )
    *received[:2], select = lax.optimization_barrier((*received[:2], select))
    blocks = lon_count // LANES
    points = 2 * lat_dev * blocks
    ext_pad = parts[0].shape[1]
    pieces = []
    for piece in received:
        pieces += [piece, swap(piece, 1)]
    vmem = pl.BlockSpec(memory_space=pltpu.VMEM)
    params = pltpu.CompilerParams(vmem_limit_bytes=24 * MIB)
    operands = (
        *pieces,
        select,
        tables,
        *plans,
    )
    near = pltpu.VMEM((3, 2 * ext_pad * blocks, LANES), jnp.float32)
    flat = jax.ShapeDtypeStruct((points, LANES), jnp.float32)
    field_first, horizontal = pl.pallas_call(
        functools.partial(first_kernel, lat_dev, len(pieces)),
        in_specs=[vmem] * len(operands),
        out_specs=[vmem] * 2,
        out_shape=[jax.ShapeDtypeStruct((1, 2 * lat_dev, lon_count), jnp.float32), flat],
        scratch_shapes=[near],
        compiler_params=params,
        cost_estimate=pl.CostEstimate(
            flops=10**8, bytes_accessed=4 * 10**6, transcendentals=0
        ),
        name="first_level",
    )(*operands)
    above_even = trade(horizontal, 0)
    above_odd = trade(horizontal, 1)
    levels = jax.ShapeDtypeStruct((level_count, 2 * lat_dev, lon_count), jnp.float32)
    grid_field, departed, top = pl.pallas_call(
        functools.partial(later_kernel, lat_dev, len(pieces)),
        in_specs=[vmem] * (len(operands) + 3),
        out_specs=[pl.BlockSpec(memory_space=pltpu.HBM), vmem, vmem],
        out_shape=[
            levels,
            jax.ShapeDtypeStruct((level_count - 1, points, LANES), jnp.float32),
            flat,
        ],
        scratch_shapes=[
            pltpu.VMEM((level_count - 1, 2 * lat_dev, lon_count), jnp.float32),
            near,
            pltpu.SemaphoreType.DMA((level_count,)),
        ],
        compiler_params=params,
        cost_estimate=pl.CostEstimate(
            flops=10**8, bytes_accessed=4 * 10**6, transcendentals=0
        ),
        name="later_levels",
    )(*operands, vertical, horizontal, field_first)
    final = pl.pallas_call(
        last_kernel,
        in_specs=[vmem] * 4,
        out_specs=vmem,
        out_shape=flat,
        compiler_params=params,
        name="top_level",
    )(top, above_even, above_odd, vertical)
    departed = jnp.concatenate([departed, final[None]], axis=0)
    return grid_field, departed.reshape(level_count, 2 * lat_dev, lon_count)


def solution(mesh):
    return jax.shard_map(
        per_device,
        mesh=mesh,
        in_specs=(
            P("wave", None, None),
            P("wave", "lev", None, None),
            P(),
            P("wave"),
            P("wave"),
            P("wave", None),
            P("wave", None),
        ),
        out_specs=(P("lev", "wave", None), P("lev", "wave", None)),
        check_vma=False,
    )
```

```python
import functools
import math

import jax
import jax.numpy as jnp
import ml_dtypes
import numpy as np
from jax import lax
from jax.experimental import pallas as pl
from jax.experimental.pallas import tpu as pltpu
from jax.sharding import PartitionSpec as P

LANES = 128
GROUP = 8
HALO = 2
WAIT_AT = (0, 2)
MIB = 1024 * 1024
FAR = -(2**20)
ORDER = (0, 2, 1, 3)
NT = (((1,), (1,)), ((), ()))
NN = (((1,), (0,)), ((), ()))


def split(value):
    high = value.astype(jnp.bfloat16)
    low = (value - high.astype(jnp.float32)).astype(jnp.bfloat16)
    return high, low


def widen(value, width):
    lane = lax.broadcasted_iota(jnp.int32, (value.shape[0], LANES), 1)
    full = value.shape[1] // LANES * LANES
    parts = [value[:, :full]]
    for start in range(full, value.shape[1]):
        column = jnp.broadcast_to(value[:, start : start + 1], lane.shape)
        parts.append(jnp.where(lane == start - full, column, 0.0))
    assert len(parts) <= 2 and full + LANES * (len(parts) - 1) == width
    return jnp.concatenate(parts, axis=1)


def wave_rows(low_ref, wave, pair_local, waves_ref):
    row = lax.broadcasted_iota(jnp.int32, (GROUP, LANES), 0)
    groups = pl.cdiv(pair_local, GROUP)
    for index in range(waves_ref.shape[0] // GROUP):
        source, group = divmod(index, groups)
        base = (wave ^ source) * pair_local + group * GROUP
        value = jnp.full((GROUP, LANES), FAR, jnp.int32)
        for slot in range(min(GROUP, pair_local - group * GROUP)):
            value = jnp.where(row == slot, low_ref[base + slot], value)
        waves_ref[index * GROUP : (index + 1) * GROUP] = value


def departure(wave, lat_dev, half, lat_ref, col_ref, lon, tilt, out_refs):
    row_step_ref, place_ref, lon_frac_ref, lat_frac_ref, vertical_ref = out_refs
    points = lon.shape[0]
    blocks = points // (2 * lat_dev)
    row = lax.broadcasted_iota(jnp.int32, lon.shape, 0)
    point = lax.broadcasted_iota(jnp.int32, lon.shape, 1)
    row_step = jnp.zeros(lon.shape, jnp.int32)
    col_step = jnp.zeros(lon.shape, jnp.int32)
    for index in range(points):
        own = wave * lat_dev + index // blocks % lat_dev - HALO
        row_step = jnp.where(row == index, lat_ref[index] - own, row_step)
        first = LANES * (index % blocks)
        col_step = jnp.where(row == index, col_ref[index] - first, col_step)
    col_step = jnp.where(col_step >= half, col_step - 2 * half, col_step)
    col_step = jnp.where(col_step < -half, col_step + 2 * half, col_step)
    quarters = 4 * col_step + lon - 12
    row_step_ref[...] = row_step
    place_ref[...] = point + (quarters >> 2)
    lon_frac_ref[...] = (quarters & 3).astype(jnp.float32) * 0.25
    lat_frac_ref[...] = (tilt & 3).astype(jnp.float32) * 0.25
    vertical_ref[...] = (tilt >> 2).astype(jnp.float32) * 0.25


def legendre_kernel(pair_local, lat_dev, *refs):
    low_hbm, spec_hbm, leg_hbm, table_hbm = refs[:4]
    *chip_refs, table_ref = refs[4:-7]
    low_ref, spec_ref, leg_ref, sums_ref, small_sem, spec_sem, leg_sem = refs[-7:]
    slots, lat_all, slot_count = leg_ref.shape
    level_count = spec_ref.shape[1]
    pair_total = low_ref.shape[0]
    ext_pad = sums_ref.shape[1]
    width = pl.cdiv(slot_count, LANES) * LANES
    low_copy = pltpu.make_async_copy(low_hbm, low_ref, small_sem.at[0])
    table_copy = pltpu.make_async_copy(table_hbm, table_ref, small_sem.at[1])
    low_copy.start()
    copies = []
    for start in range(0, slots, GROUP):
        part = pl.ds(start, GROUP)
        index = start // GROUP
        pair = (
            pltpu.make_async_copy(spec_hbm.at[part], spec_ref.at[part], spec_sem.at[index]),
            pltpu.make_async_copy(leg_hbm.at[part], leg_ref.at[part], leg_sem.at[index]),
        )
        for copy in pair:
            copy.start()
        copies.append(pair)
    table_copy.start()
    wave = lax.axis_index("wave")
    slot_of_row = lax.broadcasted_iota(jnp.int32, (GROUP, LANES), 0)
    slot_pos = lax.broadcasted_iota(jnp.int32, (GROUP, width), 1)
    low_copy.wait()
    groups = slots // GROUP
    for index in range(groups):
        if index in WAIT_AT:
            later = [at for at in WAIT_AT if at > index]
            for at in range(index, later[0] if later else groups):
                for copy in copies[at]:
                    copy.wait()
        start = index * GROUP
        base = wave * pair_local + start
        first = jnp.zeros((GROUP, LANES), jnp.int32)
        for slot in range(GROUP):
            low = low_ref[jnp.minimum(base + slot, pair_total - 1)]
            first = jnp.where(slot_of_row == slot, slot_count - 1 - low, first)
        first = jnp.concatenate([first] * (width // LANES), axis=1)
        second = slot_pos >= first
        sign = (1 - 2 * ((slot_pos - jnp.where(second, first, 0)) & 1)).astype(jnp.float32)
        member = [jnp.where(second, 0.0, 1.0), jnp.where(second, 1.0, 0.0)]
        masks = [
            jnp.concatenate(member, axis=0).astype(jnp.bfloat16),
            jnp.concatenate([m * sign for m in member], axis=0).astype(jnp.bfloat16),
        ]
        highs, lows = [], []
        for level in range(level_count):
            for part in range(2):
                row = widen(spec_ref[pl.ds(start, GROUP), level, part, :], width)
                high, low = split(jnp.concatenate([row, row], axis=0))
                highs += [high * mask for mask in masks]
                lows += [low * mask for mask in masks]
        columns = jnp.concatenate(highs + lows, axis=0)
        count = columns.shape[0] // 2
        half = GROUP * lat_all
        table = leg_ref[pl.ds(start, GROUP)].reshape(half, slot_count)
        rows = jnp.concatenate(split(widen(table, width)), axis=0)
        crossed = lax.dot_general(rows, columns, NT, preferred_element_type=jnp.float32)
        crossed = (crossed[:half, :count] + crossed[:half, count:]) + (
            crossed[half:, :count] + crossed[half:, count:]
        )
        slot_of_lane = lax.broadcasted_iota(jnp.int32, (lat_all, count), 1) % GROUP
        sums = crossed[:lat_all]
        for slot in range(1, GROUP):
            block = crossed[slot * lat_all : (slot + 1) * lat_all]
            sums = jnp.where(slot_of_lane == slot, block, sums)
        edge = jnp.zeros((HALO, count), jnp.float32)
        tail = jnp.zeros((ext_pad, count), jnp.float32)
        padded = jnp.concatenate([edge, sums, tail], axis=0)
        here = slice(index * count, (index + 1) * count)
        for dest in range(sums_ref.shape[0]):
            sums_ref[dest, :, here] = padded[dest * lat_dev : dest * lat_dev + ext_pad]
    for step, chip_ref in enumerate(chip_refs):
        dest = (wave // 2 ^ step) * 2
        for core in range(2):
            chip_ref[core] = sums_ref[dest + core]
    table_copy.wait()


def legendre_sums(operands, pair_local, wave_size):
    pair_low, spectral, legendre, tables = operands
    slots, level_count = spectral.shape[:2]
    lat_all = legendre.shape[1]
    lat_dev = lat_all // wave_size
    lanes = 8 * level_count * slots
    ext_pad = pl.cdiv(lat_dev + 2 * HALO, 8) * 8
    chips = wave_size // 2
    out = jax.ShapeDtypeStruct((2, ext_pad, lanes), jnp.float32)
    outs = [out] * chips + [jax.ShapeDtypeStruct(tables.shape, tables.dtype)]
    results = pl.pallas_call(
        functools.partial(legendre_kernel, pair_local, lat_dev),
        in_specs=[pl.BlockSpec(memory_space=pltpu.HBM)] * len(operands),
        out_specs=[pl.BlockSpec(memory_space=pltpu.VMEM)] * len(outs),
        out_shape=outs,
        scratch_shapes=[
            pltpu.SMEM(pair_low.shape, jnp.int32),
            pltpu.VMEM(spectral.shape, jnp.float32),
            pltpu.VMEM(legendre.shape, jnp.float32),
            pltpu.VMEM((wave_size, ext_pad, lanes), jnp.float32),
            pltpu.SemaphoreType.DMA((2,)),
            pltpu.SemaphoreType.DMA((slots // GROUP,)),
            pltpu.SemaphoreType.DMA((slots // GROUP,)),
        ],
        compiler_params=pltpu.CompilerParams(vmem_limit_bytes=24 * MIB),
        name="legendre",
    )(*[pltpu.with_memory_space_constraint(x, pltpu.HBM) for x in operands])
    return results[:chips], results[chips]


def chip_order(count):
    return [0, *range(count - 1, 0, -1)]


def swap(value, by):
    wave_size = lax.axis_size("wave")
    return lax.ppermute(value, "wave", [(i, i ^ by) for i in range(wave_size)])


def trade(value, offset):
    lev_size, wave_size = lax.axis_size("lev"), lax.axis_size("wave")
    pairs = []
    for lev in range(lev_size):
        other = lev + 1 if (lev - offset) % 2 == 0 else lev - 1
        for wave in range(wave_size):
            there = (other, wave) if 0 <= other < lev_size else (lev, wave ^ 1)
            pairs.append((lev * wave_size + wave, there[0] * wave_size + there[1]))
    return lax.ppermute(value, ("lev", "wave"), pairs)


def plan_kernel(pair_local, lat_dev, after_ref, *refs):
    sources = refs[:5]
    select_ref, *plan_refs = refs[5:-7]
    low_ref, lat_ref, col_ref, lon_ref, tilt_ref, waves_ref, sems = refs[-7:]
    copies = [
        pltpu.make_async_copy(there, here, sems.at[i])
        for i, (there, here) in enumerate(zip(sources, refs[-7:-2], strict=True))
    ]
    for copy in copies:
        copy.start()
    half = select_ref.shape[1]
    quarter = half // 4
    lane = lax.broadcasted_iota(jnp.int32, (2 * GROUP, half), 1)
    kind = sum((lane >= quarter * i).astype(jnp.int32) for i in range(1, 4))
    order = 4 * (lane - quarter * kind)
    for i, first in enumerate(ORDER):
        order = jnp.where(kind == i, order + first, order)
    wave = lax.axis_index("wave")
    for copy in copies:
        copy.wait()
    departure(wave, lat_dev, half, lat_ref, col_ref, lon_ref[...], tilt_ref[...], plan_refs)
    wave_rows(low_ref, wave, pair_local, waves_ref)
    for start in range(0, waves_ref.shape[0], GROUP):
        waves = waves_ref[start : start + GROUP]
        waves = jnp.concatenate([waves, half - 1 - waves], axis=0)
        waves = jnp.concatenate([waves] * (half // LANES), axis=1)
        match = jnp.where(waves == order, 1.0, 0.0).astype(jnp.bfloat16)
        select_ref[2 * start : 2 * (start + GROUP)] = match


def plan(after, pair_low, dep_lat, dep_col, lon_steps, tilt_steps, pair_local, lat_dev, slots, half):
    operands = (pair_low, dep_lat, dep_col, lon_steps, tilt_steps)
    integer = jax.ShapeDtypeStruct(lon_steps.shape, jnp.int32)
    fraction = jax.ShapeDtypeStruct(lon_steps.shape, jnp.float32)
    outs = [
        jax.ShapeDtypeStruct((2 * slots, half), jnp.bfloat16),
        integer,
        integer,
        fraction,
        fraction,
        fraction,
    ]
    return pl.pallas_call(
        functools.partial(plan_kernel, pair_local, lat_dev),
        in_specs=[pl.BlockSpec(memory_space=pl.ANY)]
        + [pl.BlockSpec(memory_space=pltpu.HBM)] * len(operands),
        out_specs=[pl.BlockSpec(memory_space=pltpu.VMEM)] * len(outs),
        out_shape=outs,
        scratch_shapes=[
            pltpu.SMEM(pair_low.shape, jnp.int32),
            pltpu.SMEM(dep_lat.shape, jnp.int32),
            pltpu.SMEM(dep_col.shape, jnp.int32),
            pltpu.VMEM(lon_steps.shape, jnp.int32),
            pltpu.VMEM(tilt_steps.shape, jnp.int32),
            pltpu.VMEM((slots, LANES), jnp.int32),
            pltpu.SemaphoreType.DMA((len(operands),)),
        ],
        compiler_params=pltpu.CompilerParams(vmem_limit_bytes=24 * MIB),
        cost_estimate=pl.CostEstimate(
            flops=10**7, bytes_accessed=4 * 10**6, transcendentals=0
        ),
        name="plan",
    )(after, *[pltpu.with_memory_space_constraint(x, pltpu.HBM) for x in operands])


def fourier_tables(wavenumber_count):
    lon_count = 2 * wavenumber_count
    quarter = lon_count // 4
    whole = quarter // LANES * LANES
    tables = []
    for parity in range(2):
        kinds = ORDER[2 * parity : 2 * parity + 2]
        wave = np.concatenate([np.arange(kind, wavenumber_count, 4) for kind in kinds])
        phase = wave[:, None] * np.arange(quarter)[None, :] % lon_count
        angle = phase * (2.0 * math.pi / lon_count)
        weight = np.where(wave == 0, 1.0, 2.0)[:, None]
        parts = [weight * np.cos(angle), -weight * np.sin(angle)]
        tables.append(np.concatenate(parts if parity == 0 else parts[::-1], axis=0))
    exact = np.stack(tables)
    high = exact.astype(ml_dtypes.bfloat16)
    low = (exact - high.astype(np.float64)).astype(ml_dtypes.bfloat16)
    return np.concatenate(
        [high[..., :whole], low[..., :whole], high[..., whole:], low[..., whole:]], axis=2
    )


def add_halves(product, start, count):
    high = product[start : start + count]
    low = product[start + count : start + 2 * count]
    whole = (product.shape[1] - LANES) // 2
    tail = high[:, 2 * whole :]
    tail = tail + (low[:, 2 * whole :] + pltpu.roll(tail, LANES // 2, 1))
    pieces = [
        high[:, at : at + LANES] + (low[:, at : at + LANES] + high[:, whole + at : whole + at + LANES])
        for at in range(0, whole, LANES)
    ]
    return pieces + [tail]


def join(first, second):
    lane = lax.broadcasted_iota(jnp.int32, first[0].shape, 1)
    rolled = [pltpu.roll(piece, LANES // 2, 1) for piece in second]
    before = [first[-1], *rolled[:-1]]
    return first[:-1] + [
        jnp.where(lane < LANES // 2, a, b) for a, b in zip(before, rolled, strict=True)
    ]


def regroup(pieces, level, lane):
    piece_lanes = LANES // 8
    upper = lane // piece_lanes >= 4
    if level == 0:
        pieces = [
            jnp.where(upper, pltpu.roll(pieces[i + 4], 4 * piece_lanes, 1), pieces[i])
            for i in range(4)
        ]
    else:
        pieces = [
            jnp.where(upper, pieces[i + 4], pltpu.roll(pieces[i], 4 * piece_lanes, 1))
            for i in range(4)
        ]
    for bit in (1, 2):
        upper = (lane // piece_lanes & bit) != 0
        for one in range(4):
            if one & bit:
                continue
            a, b = pieces[one], pieces[one | bit]
            pieces[one] = jnp.where(upper, pltpu.roll(b, piece_lanes * bit, 1), a)
            pieces[one | bit] = jnp.where(
                upper, b, pltpu.roll(a, LANES - piece_lanes * bit, 1)
            )
    return pieces


def level_rows(level, piece_refs, select_ref, table_ref):
    half = table_ref.shape[2] // 2
    core = lax.axis_index("wave") % 2
    vectors = []
    order = chip_order(len(piece_refs) // 2)
    for ref in [piece_refs[2 * order.index(i // 2) + i % 2] for i in range(len(piece_refs))]:
        source = ref[core]
        vectors += [
            source[:, start : start + LANES] for start in range(0, source.shape[1], LANES)
        ]
    lane = lax.broadcasted_iota(jnp.int32, vectors[0].shape, 1)
    columns = [[] for _ in range(4)]
    for start in range(0, len(vectors), 8):
        for kind, piece in enumerate(regroup(vectors[start : start + 8], level, lane)):
            columns[kind].append(piece)
    matrix = jnp.concatenate([jnp.concatenate(c, axis=1) for c in columns], axis=0)
    high, low = split(matrix)
    count = high.shape[0] // 2
    ordered = lax.dot_general(
        jnp.concatenate([high[:count], low[:count], high[count:], low[count:]], axis=0),
        select_ref[...],
        NN,
        preferred_element_type=jnp.float32,
    )
    half = ordered.shape[1]
    real = ordered[: 2 * count]
    imag = pltpu.roll(ordered[2 * count :], half // 2, 1)
    lane = lax.broadcasted_iota(jnp.int32, real.shape, 1)
    first_half = lane < half // 2
    outer = (lane < half // 4) | (lane >= half // 4 * 3)
    even = jnp.where(first_half, real, imag)
    odd = jnp.where(first_half, imag, real)
    turned = pltpu.roll(odd, half // 2, 1)
    even_turned = jnp.where(first_half == outer, even, -even)
    odd_turned = jnp.where(outer, turned, -turned)
    products = [
        lax.dot_general(
            jnp.concatenate(rows, axis=0).astype(jnp.bfloat16),
            table_ref[parity],
            NN,
            preferred_element_type=jnp.float32,
        )
        for parity, rows in enumerate(((even, even_turned), (odd, odd_turned)))
    ]
    near, far = [
        [add_halves(product, start, count) for product in products] for start in (0, 2 * count)
    ]
    first = join(
        [a + b for a, b in zip(*near, strict=True)], [a + b for a, b in zip(*far, strict=True)]
    )
    later = join(
        [a - b for a, b in zip(*near, strict=True)], [a - b for a, b in zip(*far, strict=True)]
    )
    return first + later


def store_rows(rows, field_ref, level, lat_dev, near_ref):
    blocks = len(rows)
    count = rows[0].shape[0]
    for at, value in enumerate(rows):
        there = slice(at * LANES, (at + 1) * LANES)
        for hemi in range(2):
            start = hemi * (count // 2) + HALO
            field_ref[level, hemi * lat_dev : (hemi + 1) * lat_dev, there] = value[
                start : start + lat_dev
            ]
        for side in range(3):
            place = (at + 1 - side) % blocks
            near_ref[side, pl.ds(place, count, stride=blocks), :] = value


def interpolate(lat_dev, row_step, step, f, g, near_ref):
    blocks = row_step.shape[0] // (2 * lat_dev)
    ext_pad = near_ref.shape[1] // (2 * blocks)
    points = 2 * lat_dev * blocks
    point = lax.broadcasted_iota(jnp.int32, (points, LANES), 1)

    def line(side, j):
        return jnp.concatenate(
            [
                near_ref[side, pl.ds((hemi * ext_pad + j) * blocks, lat_dev * blocks), :]
                for hemi in range(2)
            ],
            axis=0,
        )

    lines = [[line(side, j) for j in range(2 * HALO + 1)] for side in range(3)]
    values = []
    for upper in range(2):
        picked = []
        for side in range(3):
            choice = lines[side][upper]
            for j in range(1, 2 * HALO):
                choice = jnp.where(row_step == j, lines[side][j + upper], choice)
            picked.append(choice)
        left = jnp.where(point >= LANES - 28, picked[0], picked[1])
        right = jnp.where(point < 28, picked[2], picked[1])
        for shift in range(2):
            place = (step + shift) & (LANES - 1)
            values.append(
                jnp.where(
                    point < LANES // 2,
                    jnp.take_along_axis(left, place, axis=1),
                    jnp.take_along_axis(right, place, axis=1),
                )
            )
    lower = (1.0 - f) * values[0] + f * values[1]
    higher = (1.0 - f) * values[2] + f * values[3]
    return (1.0 - g) * lower + g * higher


def first_kernel(lat_dev, piece_count, *refs):
    piece_refs, plan_refs = refs[:piece_count], refs[piece_count + 2 : -3]
    select_ref, table_ref = refs[piece_count : piece_count + 2]
    field_ref, horizontal_ref, near_ref = refs[-3:]
    rows = level_rows(0, piece_refs, select_ref, table_ref)
    store_rows(rows, field_ref, 0, lat_dev, near_ref)
    horizontal_ref[...] = interpolate(lat_dev, *[ref[...] for ref in plan_refs], near_ref)


def later_kernel(lat_dev, piece_count, *refs):
    piece_refs, plan_refs = refs[:piece_count], refs[piece_count + 2 : -9]
    select_ref, table_ref = refs[piece_count : piece_count + 2]
    vertical_ref, below_ref, first_ref = refs[-9:-6]
    field_hbm, departed_ref, horizontal_ref, field_ref, near_ref, sems = refs[-6:]
    copies = [pltpu.make_async_copy(first_ref, field_hbm.at[pl.ds(0, 1)], sems.at[0])]
    copies[0].start()
    vertical = vertical_ref[...]
    below = below_ref[...]
    plans = [ref[...] for ref in plan_refs]
    for level in range(1, departed_ref.shape[0] + 1):
        rows = level_rows(level, piece_refs, select_ref, table_ref)
        store_rows(rows, field_ref, level - 1, lat_dev, near_ref)
        copy = pltpu.make_async_copy(
            field_ref.at[pl.ds(level - 1, 1)], field_hbm.at[pl.ds(level, 1)], sems.at[level]
        )
        copy.start()
        copies.append(copy)
        horizontal = interpolate(lat_dev, *plans, near_ref)
        departed_ref[level - 1] = (1.0 - vertical) * below + vertical * horizontal
        below = horizontal
    horizontal_ref[...] = below
    for copy in copies:
        copy.wait()


def last_kernel(below_ref, odd_ref, even_ref, vertical_ref, out_ref):
    lev = lax.axis_index("lev")
    is_last = lev == lax.axis_size("lev") - 1
    vertical = vertical_ref[...]
    below = below_ref[...]
    above = jnp.where(lev % 2 == 0, even_ref[...], odd_ref[...])
    above = jnp.where(is_last, below, above)
    out_ref[...] = (1.0 - vertical) * below + vertical * above


def per_device(legendre, spectral, pair_low, dep_lat, dep_col, lon_steps, tilt_steps):
    pair_local, level_count, _, slot_count = spectral.shape
    wavenumber_count = slot_count - 1
    lon_count = 2 * wavenumber_count
    lat_all = legendre.shape[1]
    wave_size = lax.axis_size("wave")
    lat_dev = lat_all // wave_size
    slots = pl.cdiv(pair_local, GROUP) * GROUP
    extra = slots - pair_local
    if extra:
        spectral = jnp.pad(spectral, ((0, extra), (0, 0), (0, 0), (0, 0)))
        legendre = jnp.pad(legendre, ((0, extra), (0, 0), (0, 0)))
    tables = jnp.asarray(fourier_tables(wavenumber_count))
    parts, tables = legendre_sums(
        (pair_low, spectral, legendre, tables), pair_local, wave_size
    )
    received = [swap(part, 2 * step) if step else part for step, part in enumerate(parts)]
    select, *plans, vertical = plan(
        parts[0],
        pair_low,
        dep_lat,
        dep_col,
        lon_steps,
        tilt_steps,
        pair_local,
        lat_dev,
        wave_size * slots,
        wavenumber_count,
    )
    received[-1], select = lax.optimization_barrier((received[-1], select))
    blocks = lon_count // LANES
    points = 2 * lat_dev * blocks
    ext_pad = parts[0].shape[1]
    pieces = []
    for step in chip_order(len(received)):
        pieces += [received[step], swap(received[step], 1)]
    vmem = pl.BlockSpec(memory_space=pltpu.VMEM)
    params = pltpu.CompilerParams(vmem_limit_bytes=24 * MIB)
    operands = (
        *pieces,
        select,
        tables,
        *plans,
    )
    near = pltpu.VMEM((3, 2 * ext_pad * blocks, LANES), jnp.float32)
    flat = jax.ShapeDtypeStruct((points, LANES), jnp.float32)
    field_first, horizontal = pl.pallas_call(
        functools.partial(first_kernel, lat_dev, len(pieces)),
        in_specs=[vmem] * len(operands),
        out_specs=[vmem] * 2,
        out_shape=[jax.ShapeDtypeStruct((1, 2 * lat_dev, lon_count), jnp.float32), flat],
        scratch_shapes=[near],
        compiler_params=params,
        cost_estimate=pl.CostEstimate(
            flops=10**8, bytes_accessed=4 * 10**6, transcendentals=0
        ),
        name="first_level",
    )(*operands)
    above_even = trade(horizontal, 0)
    above_odd = trade(horizontal, 1)
    levels = jax.ShapeDtypeStruct((level_count, 2 * lat_dev, lon_count), jnp.float32)
    grid_field, departed, top = pl.pallas_call(
        functools.partial(later_kernel, lat_dev, len(pieces)),
        in_specs=[vmem] * (len(operands) + 3),
        out_specs=[pl.BlockSpec(memory_space=pltpu.HBM), vmem, vmem],
        out_shape=[
            levels,
            jax.ShapeDtypeStruct((level_count - 1, points, LANES), jnp.float32),
            flat,
        ],
        scratch_shapes=[
            pltpu.VMEM((level_count - 1, 2 * lat_dev, lon_count), jnp.float32),
            near,
            pltpu.SemaphoreType.DMA((level_count,)),
        ],
        compiler_params=params,
        cost_estimate=pl.CostEstimate(
            flops=10**8, bytes_accessed=4 * 10**6, transcendentals=0
        ),
        name="later_levels",
    )(*operands, vertical, horizontal, field_first)
    final = pl.pallas_call(
        last_kernel,
        in_specs=[vmem] * 4,
        out_specs=vmem,
        out_shape=flat,
        compiler_params=params,
        name="top_level",
    )(top, above_odd, above_even, vertical)
    departed = jnp.concatenate([departed, final[None]], axis=0)
    return grid_field, departed.reshape(level_count, 2 * lat_dev, lon_count)


def solution(mesh):
    return jax.shard_map(
        per_device,
        mesh=mesh,
        in_specs=(
            P("wave", None, None),
            P("wave", "lev", None, None),
            P(),
            P("wave"),
            P("wave"),
            P("wave", None),
            P("wave", None),
        ),
        out_specs=(P("lev", "wave", None), P("lev", "wave", None)),
        check_vma=False,
    )
```

```python
import functools
import math

import jax
import jax.numpy as jnp
import ml_dtypes
import numpy as np
from jax import lax
from jax.experimental import pallas as pl
from jax.experimental.pallas import tpu as pltpu
from jax.sharding import PartitionSpec as P

LANES = 128
GROUP = 8
HALO = 2
MIB = 1024 * 1024
FAR = -(2**20)
COLORS = 3
ORDER = (0, 2, 1, 3)
NT = (((1,), (1,)), ((), ()))
NN = (((1,), (0,)), ((), ()))


def split(value):
    high = value.astype(jnp.bfloat16)
    low = (value - high.astype(jnp.float32)).astype(jnp.bfloat16)
    return high, low


def widen(value, width):
    lane = lax.broadcasted_iota(jnp.int32, (value.shape[0], LANES), 1)
    full = value.shape[1] // LANES * LANES
    parts = [value[:, :full]]
    for start in range(full, value.shape[1]):
        column = jnp.broadcast_to(value[:, start : start + 1], lane.shape)
        parts.append(jnp.where(lane == start - full, column, 0.0))
    assert len(parts) <= 2 and full + LANES * (len(parts) - 1) == width
    return jnp.concatenate(parts, axis=1)


def wave_rows(low_ref, wave, pair_local, waves_ref):
    row = lax.broadcasted_iota(jnp.int32, (GROUP, LANES), 0)
    groups = pl.cdiv(pair_local, GROUP)
    for index in range(waves_ref.shape[0] // GROUP):
        source, group = divmod(index, groups)
        base = (wave ^ source) * pair_local + group * GROUP
        value = jnp.full((GROUP, LANES), FAR, jnp.int32)
        for slot in range(min(GROUP, pair_local - group * GROUP)):
            value = jnp.where(row == slot, low_ref[base + slot], value)
        waves_ref[index * GROUP : (index + 1) * GROUP] = value


def departure(wave, lat_dev, half, lat_ref, col_ref, lon, tilt, out_refs):
    row_step_ref, place_ref, lon_frac_ref, lat_frac_ref, vertical_ref = out_refs
    points = lon.shape[0]
    blocks = points // (2 * lat_dev)
    row = lax.broadcasted_iota(jnp.int32, lon.shape, 0)
    point = lax.broadcasted_iota(jnp.int32, lon.shape, 1)
    row_step = jnp.zeros(lon.shape, jnp.int32)
    col_step = jnp.zeros(lon.shape, jnp.int32)
    for index in range(points):
        own = wave * lat_dev + index // blocks % lat_dev - HALO
        row_step = jnp.where(row == index, lat_ref[index] - own, row_step)
        first = LANES * (index % blocks)
        col_step = jnp.where(row == index, col_ref[index] - first, col_step)
    col_step = jnp.where(col_step >= half, col_step - 2 * half, col_step)
    col_step = jnp.where(col_step < -half, col_step + 2 * half, col_step)
    quarters = 4 * col_step + lon - 12
    row_step_ref[...] = row_step
    place_ref[...] = point + (quarters >> 2)
    lon_frac_ref[...] = (quarters & 3).astype(jnp.float32) * 0.25
    lat_frac_ref[...] = (tilt & 3).astype(jnp.float32) * 0.25
    vertical_ref[...] = (tilt >> 2).astype(jnp.float32) * 0.25


def legendre_kernel(pair_local, lat_dev, *refs):
    low_hbm, spec_hbm, leg_hbm, table_hbm = refs[:4]
    *chip_refs, table_ref = refs[4:-7]
    low_ref, spec_ref, leg_ref, sums_ref, small_sem, spec_sem, leg_sem = refs[-7:]
    slots, lat_all, slot_count = leg_ref.shape
    level_count = spec_ref.shape[1]
    pair_total = low_ref.shape[0]
    ext = lat_dev + 2 * HALO
    width = pl.cdiv(slot_count, LANES) * LANES
    low_copy = pltpu.make_async_copy(low_hbm, low_ref, small_sem.at[0])
    table_copy = pltpu.make_async_copy(table_hbm, table_ref, small_sem.at[1])
    low_copy.start()
    groups = slots // GROUP
    bounds = sorted({0, min(2, groups), groups})
    copies = []
    for index, (start, stop) in enumerate(zip(bounds[:-1], bounds[1:], strict=True)):
        part = pl.ds(start * GROUP, (stop - start) * GROUP)
        pair = (
            pltpu.make_async_copy(spec_hbm.at[part], spec_ref.at[part], spec_sem.at[index]),
            pltpu.make_async_copy(leg_hbm.at[part], leg_ref.at[part], leg_sem.at[index]),
        )
        for copy in pair:
            copy.start()
        copies.append((start, pair))
    table_copy.start()
    wave = lax.axis_index("wave")
    slot_of_row = lax.broadcasted_iota(jnp.int32, (GROUP, LANES), 0)
    slot_pos = lax.broadcasted_iota(jnp.int32, (GROUP, width), 1)
    low_copy.wait()
    for index in range(groups):
        for at, pair in copies:
            if at == index:
                for copy in pair:
                    copy.wait()
        start = index * GROUP
        base = wave * pair_local + start
        first = jnp.zeros((GROUP, LANES), jnp.int32)
        for slot in range(GROUP):
            low = low_ref[jnp.minimum(base + slot, pair_total - 1)]
            first = jnp.where(slot_of_row == slot, slot_count - 1 - low, first)
        first = jnp.concatenate([first] * (width // LANES), axis=1)
        second = slot_pos >= first
        sign = (1 - 2 * ((slot_pos - jnp.where(second, first, 0)) & 1)).astype(jnp.float32)
        member = [jnp.where(second, 0.0, 1.0), jnp.where(second, 1.0, 0.0)]
        masks = [
            jnp.concatenate(member, axis=0).astype(jnp.bfloat16),
            jnp.concatenate([m * sign for m in member], axis=0).astype(jnp.bfloat16),
        ]
        highs, lows = [], []
        for level in range(level_count):
            for part in range(2):
                row = widen(spec_ref[pl.ds(start, GROUP), level, part, :], width)
                high, low = split(jnp.concatenate([row, row], axis=0))
                highs += [high * mask for mask in masks]
                lows += [low * mask for mask in masks]
        columns = jnp.concatenate(highs + lows, axis=0)
        count = columns.shape[0] // 2
        half = GROUP * lat_all
        table = leg_ref[pl.ds(start, GROUP)].reshape(half, slot_count)
        rows = jnp.concatenate(split(widen(table, width)), axis=0)
        crossed = lax.dot_general(rows, columns, NT, preferred_element_type=jnp.float32)
        crossed = (crossed[:half, :count] + crossed[:half, count:]) + (
            crossed[half:, :count] + crossed[half:, count:]
        )
        slot_of_lane = lax.broadcasted_iota(jnp.int32, (lat_all, count), 1) % GROUP
        sums = crossed[:lat_all]
        for slot in range(1, GROUP):
            block = crossed[slot * lat_all : (slot + 1) * lat_all]
            sums = jnp.where(slot_of_lane == slot, block, sums)
        edge = jnp.zeros((HALO, count), jnp.float32)
        padded = jnp.concatenate([edge, sums, edge], axis=0)
        here = slice(index * ext, (index + 1) * ext)
        for dest in range(sums_ref.shape[0]):
            sums_ref[dest, here] = padded[dest * lat_dev : dest * lat_dev + ext]
    used = groups * ext
    sums_ref[:, used:] = jnp.zeros_like(sums_ref[:, used:])
    for step, chip_ref in enumerate(chip_refs):
        dest = (wave // 2 ^ step) * 2
        for core in range(2):
            chip_ref[core] = sums_ref[dest + core]
    table_copy.wait()


def legendre_sums(operands, pair_local, wave_size):
    pair_low, spectral, legendre, tables = operands
    slots, level_count = spectral.shape[:2]
    lat_all = legendre.shape[1]
    lat_dev = lat_all // wave_size
    lanes = 8 * level_count * GROUP
    ext = lat_dev + 2 * HALO
    rows = pl.cdiv((slots // GROUP - 1) * ext + pl.cdiv(ext, 8) * 8, 8) * 8
    chips = wave_size // 2
    out = jax.ShapeDtypeStruct((2, rows, lanes), jnp.float32)
    outs = [out] * chips + [jax.ShapeDtypeStruct(tables.shape, tables.dtype)]
    results = pl.pallas_call(
        functools.partial(legendre_kernel, pair_local, lat_dev),
        in_specs=[pl.BlockSpec(memory_space=pltpu.HBM)] * len(operands),
        out_specs=[pl.BlockSpec(memory_space=pltpu.VMEM)] * len(outs),
        out_shape=outs,
        scratch_shapes=[
            pltpu.SMEM(pair_low.shape, jnp.int32),
            pltpu.VMEM(spectral.shape, jnp.float32),
            pltpu.VMEM(legendre.shape, jnp.float32),
            pltpu.VMEM((wave_size, rows, lanes), jnp.float32),
            pltpu.SemaphoreType.DMA((2,)),
            pltpu.SemaphoreType.DMA((2,)),
            pltpu.SemaphoreType.DMA((2,)),
        ],
        compiler_params=pltpu.CompilerParams(vmem_limit_bytes=24 * MIB),
        name="legendre",
    )(*[pltpu.with_memory_space_constraint(x, pltpu.HBM) for x in operands])
    return results[:chips], results[chips]


def chip_order(count):
    return [0, *range(count - 1, 0, -1)]


def swap(value, by):
    wave_size = lax.axis_size("wave")
    return lax.ppermute(value, "wave", [(i, i ^ by) for i in range(wave_size)])


def trade(value, color):
    lev_size, wave_size = lax.axis_size("lev"), lax.axis_size("wave")
    pairs = []
    for lev in range(lev_size):
        other = lev
        if lev % COLORS == color and lev + 1 < lev_size:
            other = lev + 1
        if lev > 0 and (lev - 1) % COLORS == color:
            other = lev - 1
        for wave in range(wave_size):
            there = other * wave_size + (wave ^ 1 if other == lev else wave)
            pairs.append((lev * wave_size + wave, there))
    return lax.ppermute(value, ("lev", "wave"), pairs)


def plan_kernel(pair_local, lat_dev, after_ref, *refs):
    sources = refs[:5]
    select_ref, *plan_refs = refs[5:-7]
    low_ref, lat_ref, col_ref, lon_ref, tilt_ref, waves_ref, sems = refs[-7:]
    copies = [
        pltpu.make_async_copy(there, here, sems.at[i])
        for i, (there, here) in enumerate(zip(sources, refs[-7:-2], strict=True))
    ]
    for copy in copies:
        copy.start()
    half = select_ref.shape[1]
    quarter = half // 4
    lane = lax.broadcasted_iota(jnp.int32, (2 * GROUP, half), 1)
    kind = sum((lane >= quarter * i).astype(jnp.int32) for i in range(1, 4))
    order = 4 * (lane - quarter * kind)
    for i, first in enumerate(ORDER):
        order = jnp.where(kind == i, order + first, order)
    wave = lax.axis_index("wave")
    for copy in copies:
        copy.wait()
    departure(wave, lat_dev, half, lat_ref, col_ref, lon_ref[...], tilt_ref[...], plan_refs)
    wave_rows(low_ref, wave, pair_local, waves_ref)
    for start in range(0, waves_ref.shape[0], GROUP):
        waves = waves_ref[start : start + GROUP]
        waves = jnp.concatenate([waves, half - 1 - waves], axis=0)
        waves = jnp.concatenate([waves] * (half // LANES), axis=1)
        match = jnp.where(waves == order, 1.0, 0.0).astype(jnp.bfloat16)
        select_ref[2 * start : 2 * (start + GROUP)] = match


def plan(after, pair_low, dep_lat, dep_col, lon_steps, tilt_steps, pair_local, lat_dev, slots, half):
    operands = (pair_low, dep_lat, dep_col, lon_steps, tilt_steps)
    integer = jax.ShapeDtypeStruct(lon_steps.shape, jnp.int32)
    fraction = jax.ShapeDtypeStruct(lon_steps.shape, jnp.float32)
    outs = [
        jax.ShapeDtypeStruct((2 * slots, half), jnp.bfloat16),
        integer,
        integer,
        fraction,
        fraction,
        fraction,
    ]
    return pl.pallas_call(
        functools.partial(plan_kernel, pair_local, lat_dev),
        in_specs=[pl.BlockSpec(memory_space=pl.ANY)]
        + [pl.BlockSpec(memory_space=pltpu.HBM)] * len(operands),
        out_specs=[pl.BlockSpec(memory_space=pltpu.VMEM)] * len(outs),
        out_shape=outs,
        scratch_shapes=[
            pltpu.SMEM(pair_low.shape, jnp.int32),
            pltpu.SMEM(dep_lat.shape, jnp.int32),
            pltpu.SMEM(dep_col.shape, jnp.int32),
            pltpu.VMEM(lon_steps.shape, jnp.int32),
            pltpu.VMEM(tilt_steps.shape, jnp.int32),
            pltpu.VMEM((slots, LANES), jnp.int32),
            pltpu.SemaphoreType.DMA((len(operands),)),
        ],
        compiler_params=pltpu.CompilerParams(vmem_limit_bytes=24 * MIB),
        cost_estimate=pl.CostEstimate(
            flops=10**7, bytes_accessed=4 * 10**6, transcendentals=0
        ),
        name="plan",
    )(after, *[pltpu.with_memory_space_constraint(x, pltpu.HBM) for x in operands])


def fourier_tables(wavenumber_count):
    lon_count = 2 * wavenumber_count
    quarter = lon_count // 4
    whole = quarter // LANES * LANES
    tables = []
    for parity in range(2):
        kinds = ORDER[2 * parity : 2 * parity + 2]
        wave = np.concatenate([np.arange(kind, wavenumber_count, 4) for kind in kinds])
        phase = wave[:, None] * np.arange(quarter)[None, :] % lon_count
        angle = phase * (2.0 * math.pi / lon_count)
        weight = np.where(wave == 0, 1.0, 2.0)[:, None]
        parts = [weight * np.cos(angle), -weight * np.sin(angle)]
        tables.append(np.concatenate(parts if parity == 0 else parts[::-1], axis=0))
    exact = np.stack(tables)
    high = exact.astype(ml_dtypes.bfloat16)
    low = (exact - high.astype(np.float64)).astype(ml_dtypes.bfloat16)
    return np.concatenate(
        [high[..., :whole], low[..., :whole], high[..., whole:], low[..., whole:]], axis=2
    )


def add_halves(product, start, count):
    high = product[start : start + count]
    low = product[start + count : start + 2 * count]
    whole = (product.shape[1] - LANES) // 2
    tail = high[:, 2 * whole :]
    tail = tail + (low[:, 2 * whole :] + pltpu.roll(tail, LANES // 2, 1))
    pieces = [
        high[:, at : at + LANES] + (low[:, at : at + LANES] + high[:, whole + at : whole + at + LANES])
        for at in range(0, whole, LANES)
    ]
    return pieces + [tail]


def join(first, second):
    lane = lax.broadcasted_iota(jnp.int32, first[0].shape, 1)
    rolled = [pltpu.roll(piece, LANES // 2, 1) for piece in second]
    before = [first[-1], *rolled[:-1]]
    return first[:-1] + [
        jnp.where(lane < LANES // 2, a, b) for a, b in zip(before, rolled, strict=True)
    ]


def regroup(pieces, level, lane):
    piece_lanes = LANES // 8
    upper = lane // piece_lanes >= 4
    if level == 0:
        pieces = [
            jnp.where(upper, pltpu.roll(pieces[i + 4], 4 * piece_lanes, 1), pieces[i])
            for i in range(4)
        ]
    else:
        pieces = [
            jnp.where(upper, pieces[i + 4], pltpu.roll(pieces[i], 4 * piece_lanes, 1))
            for i in range(4)
        ]
    for bit in (1, 2):
        upper = (lane // piece_lanes & bit) != 0
        for one in range(4):
            if one & bit:
                continue
            a, b = pieces[one], pieces[one | bit]
            pieces[one] = jnp.where(upper, pltpu.roll(b, piece_lanes * bit, 1), a)
            pieces[one | bit] = jnp.where(
                upper, b, pltpu.roll(a, LANES - piece_lanes * bit, 1)
            )
    return pieces


def level_rows(level, lat_dev, piece_refs, select_ref, table_ref):
    ext = lat_dev + 2 * HALO
    ext_pad = pl.cdiv(ext, 8) * 8
    half = table_ref.shape[2] // 2
    core = lax.axis_index("wave") % 2
    vectors = []
    order = chip_order(len(piece_refs) // 2)
    for ref in [piece_refs[2 * order.index(i // 2) + i % 2] for i in range(len(piece_refs))]:
        source = ref[core]
        vectors += [
            source[start : start + ext_pad]
            for start in range(0, source.shape[0] - ext_pad + 1, ext)
        ]
    lane = lax.broadcasted_iota(jnp.int32, vectors[0].shape, 1)
    columns = [[] for _ in range(4)]
    for start in range(0, len(vectors), 8):
        for kind, piece in enumerate(regroup(vectors[start : start + 8], level, lane)):
            columns[kind].append(piece)
    matrix = jnp.concatenate([jnp.concatenate(c, axis=1) for c in columns], axis=0)
    high, low = split(matrix)
    count = high.shape[0] // 2
    ordered = lax.dot_general(
        jnp.concatenate([high[:count], low[:count], high[count:], low[count:]], axis=0),
        select_ref[...],
        NN,
        preferred_element_type=jnp.float32,
    )
    half = ordered.shape[1]
    real = ordered[: 2 * count]
    imag = pltpu.roll(ordered[2 * count :], half // 2, 1)
    lane = lax.broadcasted_iota(jnp.int32, real.shape, 1)
    first_half = lane < half // 2
    outer = (lane < half // 4) | (lane >= half // 4 * 3)
    even = jnp.where(first_half, real, imag)
    odd = jnp.where(first_half, imag, real)
    turned = pltpu.roll(odd, half // 2, 1)
    even_turned = jnp.where(first_half == outer, even, -even)
    odd_turned = jnp.where(outer, turned, -turned)
    products = [
        lax.dot_general(
            jnp.concatenate(rows, axis=0).astype(jnp.bfloat16),
            table_ref[parity],
            NN,
            preferred_element_type=jnp.float32,
        )
        for parity, rows in enumerate(((even, even_turned), (odd, odd_turned)))
    ]
    near, far = [
        [add_halves(product, start, count) for product in products] for start in (0, 2 * count)
    ]
    first = join(
        [a + b for a, b in zip(*near, strict=True)], [a + b for a, b in zip(*far, strict=True)]
    )
    later = join(
        [a - b for a, b in zip(*near, strict=True)], [a - b for a, b in zip(*far, strict=True)]
    )
    return first + later


def store_rows(rows, field_ref, level, lat_dev, near_ref):
    blocks = len(rows)
    count = rows[0].shape[0]
    for at, value in enumerate(rows):
        there = slice(at * LANES, (at + 1) * LANES)
        for hemi in range(2):
            start = hemi * (count // 2) + HALO
            field_ref[level, hemi * lat_dev : (hemi + 1) * lat_dev, there] = value[
                start : start + lat_dev
            ]
        for side in range(3):
            place = (at + 1 - side) % blocks
            near_ref[side, pl.ds(place, count, stride=blocks), :] = value


def interpolate(lat_dev, row_step, step, f, g, near_ref):
    blocks = row_step.shape[0] // (2 * lat_dev)
    ext_pad = near_ref.shape[1] // (2 * blocks)
    points = 2 * lat_dev * blocks
    point = lax.broadcasted_iota(jnp.int32, (points, LANES), 1)

    def line(side, j):
        return jnp.concatenate(
            [
                near_ref[side, pl.ds((hemi * ext_pad + j) * blocks, lat_dev * blocks), :]
                for hemi in range(2)
            ],
            axis=0,
        )

    lines = [[line(side, j) for j in range(2 * HALO + 1)] for side in range(3)]
    values = []
    for upper in range(2):
        picked = []
        for side in range(3):
            choice = lines[side][upper]
            for j in range(1, 2 * HALO):
                choice = jnp.where(row_step == j, lines[side][j + upper], choice)
            picked.append(choice)
        left = jnp.where(point >= LANES - 28, picked[0], picked[1])
        right = jnp.where(point < 28, picked[2], picked[1])
        for shift in range(2):
            place = (step + shift) & (LANES - 1)
            values.append(
                jnp.where(
                    point < LANES // 2,
                    jnp.take_along_axis(left, place, axis=1),
                    jnp.take_along_axis(right, place, axis=1),
                )
            )
    lower = (1.0 - f) * values[0] + f * values[1]
    higher = (1.0 - f) * values[2] + f * values[3]
    return (1.0 - g) * lower + g * higher


def first_kernel(lat_dev, piece_count, *refs):
    piece_refs, plan_refs = refs[:piece_count], refs[piece_count + 2 : -3]
    select_ref, table_ref = refs[piece_count : piece_count + 2]
    field_ref, horizontal_ref, near_ref = refs[-3:]
    rows = level_rows(0, lat_dev, piece_refs, select_ref, table_ref)
    store_rows(rows, field_ref, 0, lat_dev, near_ref)
    horizontal_ref[...] = interpolate(lat_dev, *[ref[...] for ref in plan_refs], near_ref)


def later_kernel(lat_dev, piece_count, *refs):
    piece_refs, plan_refs = refs[:piece_count], refs[piece_count + 2 : -9]
    select_ref, table_ref = refs[piece_count : piece_count + 2]
    vertical_ref, below_ref, first_ref = refs[-9:-6]
    field_hbm, departed_ref, horizontal_ref, field_ref, near_ref, sems = refs[-6:]
    copies = [pltpu.make_async_copy(first_ref, field_hbm.at[pl.ds(0, 1)], sems.at[0])]
    copies[0].start()
    vertical = vertical_ref[...]
    below = below_ref[...]
    plans = [ref[...] for ref in plan_refs]
    for level in range(1, departed_ref.shape[0] + 1):
        rows = level_rows(level, lat_dev, piece_refs, select_ref, table_ref)
        store_rows(rows, field_ref, level - 1, lat_dev, near_ref)
        copy = pltpu.make_async_copy(
            field_ref.at[pl.ds(level - 1, 1)], field_hbm.at[pl.ds(level, 1)], sems.at[level]
        )
        copy.start()
        copies.append(copy)
        horizontal = interpolate(lat_dev, *plans, near_ref)
        departed_ref[level - 1] = (1.0 - vertical) * below + vertical * horizontal
        below = horizontal
    horizontal_ref[...] = below
    for copy in copies:
        copy.wait()


def last_kernel(below_ref, *refs):
    *above_refs, vertical_ref, out_ref = refs
    lev = lax.axis_index("lev")
    is_last = lev == lax.axis_size("lev") - 1
    vertical = vertical_ref[...]
    below = below_ref[...]
    above = below
    for color, above_ref in enumerate(above_refs[::-1]):
        above = jnp.where(lev % COLORS == color, above_ref[...], above)
    above = jnp.where(is_last, below, above)
    out_ref[...] = (1.0 - vertical) * below + vertical * above


def per_device(legendre, spectral, pair_low, dep_lat, dep_col, lon_steps, tilt_steps):
    pair_local, level_count, _, slot_count = spectral.shape
    wavenumber_count = slot_count - 1
    lon_count = 2 * wavenumber_count
    lat_all = legendre.shape[1]
    wave_size = lax.axis_size("wave")
    lat_dev = lat_all // wave_size
    slots = pl.cdiv(pair_local, GROUP) * GROUP
    extra = slots - pair_local
    if extra:
        spectral = jnp.pad(spectral, ((0, extra), (0, 0), (0, 0), (0, 0)))
        legendre = jnp.pad(legendre, ((0, extra), (0, 0), (0, 0)))
    tables = jnp.asarray(fourier_tables(wavenumber_count))
    parts, tables = legendre_sums(
        (pair_low, spectral, legendre, tables), pair_local, wave_size
    )
    received = [swap(part, 2 * step) if step else part for step, part in enumerate(parts)]
    select, *plans, vertical = plan(
        parts[0],
        pair_low,
        dep_lat,
        dep_col,
        lon_steps,
        tilt_steps,
        pair_local,
        lat_dev,
        wave_size * slots,
        wavenumber_count,
    )
    received[-1], select = lax.optimization_barrier((received[-1], select))
    blocks = lon_count // LANES
    points = 2 * lat_dev * blocks
    ext_pad = pl.cdiv(lat_dev + 2 * HALO, 8) * 8
    pieces = []
    for step in chip_order(len(received)):
        pieces += [received[step], swap(received[step], 1)]
    vmem = pl.BlockSpec(memory_space=pltpu.VMEM)
    params = pltpu.CompilerParams(vmem_limit_bytes=24 * MIB)
    operands = (
        *pieces,
        select,
        tables,
        *plans,
    )
    near = pltpu.VMEM((3, 2 * ext_pad * blocks, LANES), jnp.float32)
    flat = jax.ShapeDtypeStruct((points, LANES), jnp.float32)
    field_first, horizontal = pl.pallas_call(
        functools.partial(first_kernel, lat_dev, len(pieces)),
        in_specs=[vmem] * len(operands),
        out_specs=[vmem] * 2,
        out_shape=[jax.ShapeDtypeStruct((1, 2 * lat_dev, lon_count), jnp.float32), flat],
        scratch_shapes=[near],
        compiler_params=params,
        cost_estimate=pl.CostEstimate(
            flops=10**8, bytes_accessed=4 * 10**6, transcendentals=0
        ),
        name="first_level",
    )(*operands)
    above = [trade(horizontal, color) for color in range(COLORS)]
    levels = jax.ShapeDtypeStruct((level_count, 2 * lat_dev, lon_count), jnp.float32)
    grid_field, departed, top = pl.pallas_call(
        functools.partial(later_kernel, lat_dev, len(pieces)),
        in_specs=[vmem] * (len(operands) + 3),
        out_specs=[pl.BlockSpec(memory_space=pltpu.HBM), vmem, vmem],
        out_shape=[
            levels,
            jax.ShapeDtypeStruct((level_count - 1, points, LANES), jnp.float32),
            flat,
        ],
        scratch_shapes=[
            pltpu.VMEM((level_count - 1, 2 * lat_dev, lon_count), jnp.float32),
            near,
            pltpu.SemaphoreType.DMA((level_count,)),
        ],
        compiler_params=params,
        cost_estimate=pl.CostEstimate(
            flops=10**8, bytes_accessed=4 * 10**6, transcendentals=0
        ),
        name="later_levels",
    )(*operands, vertical, horizontal, field_first)
    final = pl.pallas_call(
        last_kernel,
        in_specs=[vmem] * (COLORS + 2),
        out_specs=vmem,
        out_shape=flat,
        compiler_params=params,
        name="top_level",
    )(top, *above[::-1], vertical)
    departed = jnp.concatenate([departed, final[None]], axis=0)
    return grid_field, departed.reshape(level_count, 2 * lat_dev, lon_count)


def solution(mesh):
    return jax.shard_map(
        per_device,
        mesh=mesh,
        in_specs=(
            P("wave", None, None),
            P("wave", "lev", None, None),
            P(),
            P("wave"),
            P("wave"),
            P("wave", None),
            P("wave", None),
        ),
        out_specs=(P("lev", "wave", None), P("lev", "wave", None)),
        check_vma=False,
    )
```

```python
import functools
import math

import jax
import jax.numpy as jnp
import ml_dtypes
import numpy as np
from jax import lax
from jax.experimental import pallas as pl
from jax.experimental.pallas import tpu as pltpu
from jax.sharding import PartitionSpec as P

LANES = 128
GROUP = 8
HALO = 2
MIB = 1024 * 1024
FAR = -(2**20)
COLORS = 3
ORDER = (0, 2, 1, 3)
NT = (((1,), (1,)), ((), ()))
NN = (((1,), (0,)), ((), ()))


def split(value):
    high = value.astype(jnp.bfloat16)
    low = (value - high.astype(jnp.float32)).astype(jnp.bfloat16)
    return high, low


def widen(value, width):
    lane = lax.broadcasted_iota(jnp.int32, (value.shape[0], LANES), 1)
    full = value.shape[1] // LANES * LANES
    parts = [value[:, :full]]
    for start in range(full, value.shape[1]):
        column = jnp.broadcast_to(value[:, start : start + 1], lane.shape)
        parts.append(jnp.where(lane == start - full, column, 0.0))
    assert len(parts) <= 2 and full + LANES * (len(parts) - 1) == width
    return jnp.concatenate(parts, axis=1)


def half_vectors(chips, groups):
    return pl.cdiv(chips * groups, 8) * 8


def wave_rows(low_ref, wave, pair_local, waves_ref):
    row = lax.broadcasted_iota(jnp.int32, (GROUP, LANES), 0)
    groups = pl.cdiv(pair_local, GROUP)
    chips = low_ref.shape[0] // pair_local // 2
    count = half_vectors(chips, groups)
    for index in range(2 * count):
        half, place = divmod(index, count)
        chip, group = divmod(place, groups)
        value = jnp.full((GROUP, LANES), FAR, jnp.int32)
        if chip < chips:
            base = (wave ^ (2 * chip + half)) * pair_local + group * GROUP
            for slot in range(min(GROUP, pair_local - group * GROUP)):
                value = jnp.where(row == slot, low_ref[base + slot], value)
        waves_ref[index * GROUP : (index + 1) * GROUP] = value


def departure(wave, lat_dev, half, lat_ref, col_ref, lon, tilt, out_refs):
    row_step_ref, place_ref, lon_frac_ref, lat_frac_ref, vertical_ref = out_refs
    points = lon.shape[0]
    blocks = points // (2 * lat_dev)
    row = lax.broadcasted_iota(jnp.int32, lon.shape, 0)
    point = lax.broadcasted_iota(jnp.int32, lon.shape, 1)
    row_step = jnp.zeros(lon.shape, jnp.int32)
    col_step = jnp.zeros(lon.shape, jnp.int32)
    for index in range(points):
        own = wave * lat_dev + index // blocks % lat_dev - HALO
        row_step = jnp.where(row == index, lat_ref[index] - own, row_step)
        first = LANES * (index % blocks)
        col_step = jnp.where(row == index, col_ref[index] - first, col_step)
    col_step = jnp.where(col_step >= half, col_step - 2 * half, col_step)
    col_step = jnp.where(col_step < -half, col_step + 2 * half, col_step)
    quarters = 4 * col_step + lon - 12
    row_step_ref[...] = row_step
    place_ref[...] = point + (quarters >> 2)
    lon_frac_ref[...] = (quarters & 3).astype(jnp.float32) * 0.25
    lat_frac_ref[...] = (tilt & 3).astype(jnp.float32) * 0.25
    vertical_ref[...] = (tilt >> 2).astype(jnp.float32) * 0.25


def legendre_kernel(pair_local, lat_dev, *refs):
    low_hbm, spec_hbm, leg_hbm, table_hbm = refs[:4]
    *chip_refs, table_ref = refs[4:-7]
    low_ref, spec_ref, leg_ref, sums_ref, small_sem, spec_sem, leg_sem = refs[-7:]
    slots, lat_all, slot_count = leg_ref.shape
    level_count = spec_ref.shape[1]
    pair_total = low_ref.shape[0]
    ext = lat_dev + 2 * HALO
    width = pl.cdiv(slot_count, LANES) * LANES
    low_copy = pltpu.make_async_copy(low_hbm, low_ref, small_sem.at[0])
    table_copy = pltpu.make_async_copy(table_hbm, table_ref, small_sem.at[1])
    low_copy.start()
    groups = slots // GROUP
    bounds = sorted({0, min(2, groups), groups})
    copies = []
    for index, (start, stop) in enumerate(zip(bounds[:-1], bounds[1:], strict=True)):
        part = pl.ds(start * GROUP, (stop - start) * GROUP)
        pair = (
            pltpu.make_async_copy(spec_hbm.at[part], spec_ref.at[part], spec_sem.at[index]),
            pltpu.make_async_copy(leg_hbm.at[part], leg_ref.at[part], leg_sem.at[index]),
        )
        for copy in pair:
            copy.start()
        copies.append((start, pair))
    table_copy.start()
    wave = lax.axis_index("wave")
    slot_of_row = lax.broadcasted_iota(jnp.int32, (GROUP, LANES), 0)
    slot_pos = lax.broadcasted_iota(jnp.int32, (GROUP, width), 1)
    low_copy.wait()
    for index in range(groups):
        for at, pair in copies:
            if at == index:
                for copy in pair:
                    copy.wait()
        start = index * GROUP
        base = wave * pair_local + start
        first = jnp.zeros((GROUP, LANES), jnp.int32)
        for slot in range(GROUP):
            low = low_ref[jnp.minimum(base + slot, pair_total - 1)]
            first = jnp.where(slot_of_row == slot, slot_count - 1 - low, first)
        first = jnp.concatenate([first] * (width // LANES), axis=1)
        second = slot_pos >= first
        sign = (1 - 2 * ((slot_pos - jnp.where(second, first, 0)) & 1)).astype(jnp.float32)
        member = [jnp.where(second, 0.0, 1.0), jnp.where(second, 1.0, 0.0)]
        masks = [
            jnp.concatenate(member, axis=0).astype(jnp.bfloat16),
            jnp.concatenate([m * sign for m in member], axis=0).astype(jnp.bfloat16),
        ]
        highs, lows = [], []
        for level in range(level_count):
            for part in range(2):
                row = widen(spec_ref[pl.ds(start, GROUP), level, part, :], width)
                high, low = split(jnp.concatenate([row, row], axis=0))
                highs += [high * mask for mask in masks]
                lows += [low * mask for mask in masks]
        columns = jnp.concatenate(highs + lows, axis=0)
        count = columns.shape[0] // 2
        half = GROUP * lat_all
        table = leg_ref[pl.ds(start, GROUP)].reshape(half, slot_count)
        rows = jnp.concatenate(split(widen(table, width)), axis=0)
        crossed = lax.dot_general(rows, columns, NT, preferred_element_type=jnp.float32)
        crossed = (crossed[:half, :count] + crossed[:half, count:]) + (
            crossed[half:, :count] + crossed[half:, count:]
        )
        slot_of_lane = lax.broadcasted_iota(jnp.int32, (lat_all, count), 1) % GROUP
        sums = crossed[:lat_all]
        for slot in range(1, GROUP):
            block = crossed[slot * lat_all : (slot + 1) * lat_all]
            sums = jnp.where(slot_of_lane == slot, block, sums)
        edge = jnp.zeros((HALO, count), jnp.float32)
        padded = jnp.concatenate([edge, sums, edge], axis=0)
        here = slice(index * ext, (index + 1) * ext)
        for dest in range(sums_ref.shape[0]):
            sums_ref[dest, here] = padded[dest * lat_dev : dest * lat_dev + ext]
    used = groups * ext
    sums_ref[:, used:] = jnp.zeros_like(sums_ref[:, used:])
    for step, chip_ref in enumerate(chip_refs):
        dest = (wave // 2 ^ step) * 2
        for core in range(2):
            chip_ref[core] = sums_ref[dest + core]
    table_copy.wait()


def legendre_sums(operands, pair_local, wave_size):
    pair_low, spectral, legendre, tables = operands
    slots, level_count = spectral.shape[:2]
    lat_all = legendre.shape[1]
    lat_dev = lat_all // wave_size
    lanes = 8 * level_count * GROUP
    ext = lat_dev + 2 * HALO
    rows = pl.cdiv((slots // GROUP - 1) * ext + pl.cdiv(ext, 8) * 8, 8) * 8
    chips = wave_size // 2
    out = jax.ShapeDtypeStruct((2, rows, lanes), jnp.float32)
    outs = [out] * chips + [jax.ShapeDtypeStruct(tables.shape, tables.dtype)]
    results = pl.pallas_call(
        functools.partial(legendre_kernel, pair_local, lat_dev),
        in_specs=[pl.BlockSpec(memory_space=pltpu.HBM)] * len(operands),
        out_specs=[pl.BlockSpec(memory_space=pltpu.VMEM)] * len(outs),
        out_shape=outs,
        scratch_shapes=[
            pltpu.SMEM(pair_low.shape, jnp.int32),
            pltpu.VMEM(spectral.shape, jnp.float32),
            pltpu.VMEM(legendre.shape, jnp.float32),
            pltpu.VMEM((wave_size, rows, lanes), jnp.float32),
            pltpu.SemaphoreType.DMA((2,)),
            pltpu.SemaphoreType.DMA((2,)),
            pltpu.SemaphoreType.DMA((2,)),
        ],
        compiler_params=pltpu.CompilerParams(vmem_limit_bytes=24 * MIB),
        name="legendre",
    )(*[pltpu.with_memory_space_constraint(x, pltpu.HBM) for x in operands])
    return results[:chips], results[chips]


def chip_order(count):
    return [0, *range(count - 1, 0, -1)]


def swap(value, by):
    wave_size = lax.axis_size("wave")
    return lax.ppermute(value, "wave", [(i, i ^ by) for i in range(wave_size)])


def trade(value, color):
    lev_size, wave_size = lax.axis_size("lev"), lax.axis_size("wave")
    pairs = []
    for lev in range(lev_size):
        other = lev
        if lev % COLORS == color and lev + 1 < lev_size:
            other = lev + 1
        if lev > 0 and (lev - 1) % COLORS == color:
            other = lev - 1
        for wave in range(wave_size):
            there = other * wave_size + (wave ^ 1 if other == lev else wave)
            pairs.append((lev * wave_size + wave, there))
    return lax.ppermute(value, ("lev", "wave"), pairs)


def plan_kernel(pair_local, lat_dev, after_ref, *refs):
    sources = refs[:5]
    select_ref, *plan_refs = refs[5:-7]
    low_ref, lat_ref, col_ref, lon_ref, tilt_ref, waves_ref, sems = refs[-7:]
    copies = [
        pltpu.make_async_copy(there, here, sems.at[i])
        for i, (there, here) in enumerate(zip(sources, refs[-7:-2], strict=True))
    ]
    for copy in copies:
        copy.start()
    half = select_ref.shape[1]
    quarter = half // 4
    lane = lax.broadcasted_iota(jnp.int32, (2 * GROUP, half), 1)
    kind = sum((lane >= quarter * i).astype(jnp.int32) for i in range(1, 4))
    order = 4 * (lane - quarter * kind)
    for i, first in enumerate(ORDER):
        order = jnp.where(kind == i, order + first, order)
    wave = lax.axis_index("wave")
    for copy in copies:
        copy.wait()
    departure(wave, lat_dev, half, lat_ref, col_ref, lon_ref[...], tilt_ref[...], plan_refs)
    wave_rows(low_ref, wave, pair_local, waves_ref)
    for start in range(0, waves_ref.shape[0], GROUP):
        waves = waves_ref[start : start + GROUP]
        waves = jnp.concatenate([waves, half - 1 - waves], axis=0)
        waves = jnp.concatenate([waves] * (half // LANES), axis=1)
        match = jnp.where(waves == order, 1.0, 0.0).astype(jnp.bfloat16)
        select_ref[2 * start : 2 * (start + GROUP)] = match


def plan(after, pair_low, dep_lat, dep_col, lon_steps, tilt_steps, pair_local, lat_dev, slots, half):
    operands = (pair_low, dep_lat, dep_col, lon_steps, tilt_steps)
    integer = jax.ShapeDtypeStruct(lon_steps.shape, jnp.int32)
    fraction = jax.ShapeDtypeStruct(lon_steps.shape, jnp.float32)
    outs = [
        jax.ShapeDtypeStruct((2 * slots, half), jnp.bfloat16),
        integer,
        integer,
        fraction,
        fraction,
        fraction,
    ]
    return pl.pallas_call(
        functools.partial(plan_kernel, pair_local, lat_dev),
        in_specs=[pl.BlockSpec(memory_space=pl.ANY)]
        + [pl.BlockSpec(memory_space=pltpu.HBM)] * len(operands),
        out_specs=[pl.BlockSpec(memory_space=pltpu.VMEM)] * len(outs),
        out_shape=outs,
        scratch_shapes=[
            pltpu.SMEM(pair_low.shape, jnp.int32),
            pltpu.SMEM(dep_lat.shape, jnp.int32),
            pltpu.SMEM(dep_col.shape, jnp.int32),
            pltpu.VMEM(lon_steps.shape, jnp.int32),
            pltpu.VMEM(tilt_steps.shape, jnp.int32),
            pltpu.VMEM((slots, LANES), jnp.int32),
            pltpu.SemaphoreType.DMA((len(operands),)),
        ],
        compiler_params=pltpu.CompilerParams(vmem_limit_bytes=24 * MIB),
        cost_estimate=pl.CostEstimate(
            flops=10**7, bytes_accessed=4 * 10**6, transcendentals=0
        ),
        name="plan",
    )(after, *[pltpu.with_memory_space_constraint(x, pltpu.HBM) for x in operands])


def fourier_tables(wavenumber_count):
    lon_count = 2 * wavenumber_count
    quarter = lon_count // 4
    whole = quarter // LANES * LANES
    tables = []
    for parity in range(2):
        kinds = ORDER[2 * parity : 2 * parity + 2]
        wave = np.concatenate([np.arange(kind, wavenumber_count, 4) for kind in kinds])
        phase = wave[:, None] * np.arange(quarter)[None, :] % lon_count
        angle = phase * (2.0 * math.pi / lon_count)
        weight = np.where(wave == 0, 1.0, 2.0)[:, None]
        parts = [weight * np.cos(angle), -weight * np.sin(angle)]
        tables.append(np.concatenate(parts if parity == 0 else parts[::-1], axis=0))
    exact = np.stack(tables)
    high = exact.astype(ml_dtypes.bfloat16)
    low = (exact - high.astype(np.float64)).astype(ml_dtypes.bfloat16)
    return np.concatenate(
        [high[..., :whole], low[..., :whole], high[..., whole:], low[..., whole:]], axis=2
    )


def add_halves(product, start, count):
    high = product[start : start + count]
    low = product[start + count : start + 2 * count]
    whole = (product.shape[1] - LANES) // 2
    tail = high[:, 2 * whole :]
    tail = tail + (low[:, 2 * whole :] + pltpu.roll(tail, LANES // 2, 1))
    pieces = [
        high[:, at : at + LANES] + (low[:, at : at + LANES] + high[:, whole + at : whole + at + LANES])
        for at in range(0, whole, LANES)
    ]
    return pieces + [tail]


def join(first, second):
    lane = lax.broadcasted_iota(jnp.int32, first[0].shape, 1)
    rolled = [pltpu.roll(piece, LANES // 2, 1) for piece in second]
    before = [first[-1], *rolled[:-1]]
    return first[:-1] + [
        jnp.where(lane < LANES // 2, a, b) for a, b in zip(before, rolled, strict=True)
    ]


def regroup(pieces, level, lane):
    piece_lanes = LANES // 8
    upper = lane // piece_lanes >= 4
    if level == 0:
        pieces = [
            jnp.where(upper, pltpu.roll(pieces[i + 4], 4 * piece_lanes, 1), pieces[i])
            for i in range(4)
        ]
    else:
        pieces = [
            jnp.where(upper, pieces[i + 4], pltpu.roll(pieces[i], 4 * piece_lanes, 1))
            for i in range(4)
        ]
    for bit in (1, 2):
        upper = (lane // piece_lanes & bit) != 0
        for one in range(4):
            if one & bit:
                continue
            a, b = pieces[one], pieces[one | bit]
            pieces[one] = jnp.where(upper, pltpu.roll(b, piece_lanes * bit, 1), a)
            pieces[one | bit] = jnp.where(
                upper, b, pltpu.roll(a, LANES - piece_lanes * bit, 1)
            )
    return pieces


def ordered_part(level, lat_dev, piece_refs, half, select_ref):
    ext = lat_dev + 2 * HALO
    ext_pad = pl.cdiv(ext, 8) * 8
    core = lax.axis_index("wave") % 2
    vectors = []
    order = chip_order(len(piece_refs))
    for ref in [piece_refs[order.index(step)] for step in range(len(piece_refs))]:
        source = ref[core]
        vectors += [
            source[start : start + ext_pad]
            for start in range(0, source.shape[0] - ext_pad + 1, ext)
        ]
    vectors += [jnp.zeros_like(vectors[0])] * (-len(vectors) % 8)
    lane = lax.broadcasted_iota(jnp.int32, vectors[0].shape, 1)
    columns = [[] for _ in range(4)]
    for start in range(0, len(vectors), 8):
        for kind, piece in enumerate(regroup(vectors[start : start + 8], level, lane)):
            columns[kind].append(piece)
    matrix = jnp.concatenate([jnp.concatenate(c, axis=1) for c in columns], axis=0)
    high, low = split(matrix)
    count = high.shape[0] // 2
    lanes = matrix.shape[1]
    return lax.dot_general(
        jnp.concatenate([high[:count], low[:count], high[count:], low[count:]], axis=0),
        select_ref[half * lanes : (half + 1) * lanes],
        NN,
        preferred_element_type=jnp.float32,
    )


def level_rows(ordered, table_ref):
    count = ordered.shape[0] // 4
    half = ordered.shape[1]
    real = ordered[: 2 * count]
    imag = pltpu.roll(ordered[2 * count :], half // 2, 1)
    lane = lax.broadcasted_iota(jnp.int32, real.shape, 1)
    first_half = lane < half // 2
    outer = (lane < half // 4) | (lane >= half // 4 * 3)
    even = jnp.where(first_half, real, imag)
    odd = jnp.where(first_half, imag, real)
    turned = pltpu.roll(odd, half // 2, 1)
    even_turned = jnp.where(first_half == outer, even, -even)
    odd_turned = jnp.where(outer, turned, -turned)
    products = [
        lax.dot_general(
            jnp.concatenate(rows, axis=0).astype(jnp.bfloat16),
            table_ref[parity],
            NN,
            preferred_element_type=jnp.float32,
        )
        for parity, rows in enumerate(((even, even_turned), (odd, odd_turned)))
    ]
    near, far = [
        [add_halves(product, start, count) for product in products] for start in (0, 2 * count)
    ]
    first = join(
        [a + b for a, b in zip(*near, strict=True)], [a + b for a, b in zip(*far, strict=True)]
    )
    later = join(
        [a - b for a, b in zip(*near, strict=True)], [a - b for a, b in zip(*far, strict=True)]
    )
    return first + later


def store_rows(rows, field_ref, level, lat_dev, near_ref):
    blocks = len(rows)
    count = rows[0].shape[0]
    for at, value in enumerate(rows):
        there = slice(at * LANES, (at + 1) * LANES)
        for hemi in range(2):
            start = hemi * (count // 2) + HALO
            field_ref[level, hemi * lat_dev : (hemi + 1) * lat_dev, there] = value[
                start : start + lat_dev
            ]
        for side in range(3):
            place = (at + 1 - side) % blocks
            near_ref[side, pl.ds(place, count, stride=blocks), :] = value


def interpolate(lat_dev, row_step, step, f, g, near_ref):
    blocks = row_step.shape[0] // (2 * lat_dev)
    ext_pad = near_ref.shape[1] // (2 * blocks)
    points = 2 * lat_dev * blocks
    point = lax.broadcasted_iota(jnp.int32, (points, LANES), 1)

    def line(side, j):
        return jnp.concatenate(
            [
                near_ref[side, pl.ds((hemi * ext_pad + j) * blocks, lat_dev * blocks), :]
                for hemi in range(2)
            ],
            axis=0,
        )

    lines = [[line(side, j) for j in range(2 * HALO + 1)] for side in range(3)]
    values = []
    for upper in range(2):
        picked = []
        for side in range(3):
            choice = lines[side][upper]
            for j in range(1, 2 * HALO):
                choice = jnp.where(row_step == j, lines[side][j + upper], choice)
            picked.append(choice)
        left = jnp.where(point >= LANES - 28, picked[0], picked[1])
        right = jnp.where(point < 28, picked[2], picked[1])
        for shift in range(2):
            place = (step + shift) & (LANES - 1)
            values.append(
                jnp.where(
                    point < LANES // 2,
                    jnp.take_along_axis(left, place, axis=1),
                    jnp.take_along_axis(right, place, axis=1),
                )
            )
    lower = (1.0 - f) * values[0] + f * values[1]
    higher = (1.0 - f) * values[2] + f * values[3]
    return (1.0 - g) * lower + g * higher


def early_kernel(lat_dev, *refs):
    *piece_refs, select_ref, out_ref = refs
    for level in range(out_ref.shape[0]):
        out_ref[level] = ordered_part(level, lat_dev, piece_refs, 0, select_ref)


def first_kernel(lat_dev, piece_count, *refs):
    piece_refs, plan_refs = refs[:piece_count], refs[piece_count + 3 : -3]
    early_ref, select_ref, table_ref = refs[piece_count : piece_count + 3]
    field_ref, horizontal_ref, near_ref = refs[-3:]
    ordered = early_ref[0] + ordered_part(0, lat_dev, piece_refs, 1, select_ref)
    rows = level_rows(ordered, table_ref)
    store_rows(rows, field_ref, 0, lat_dev, near_ref)
    horizontal_ref[...] = interpolate(lat_dev, *[ref[...] for ref in plan_refs], near_ref)


def later_kernel(lat_dev, piece_count, *refs):
    piece_refs, plan_refs = refs[:piece_count], refs[piece_count + 3 : -9]
    early_ref, select_ref, table_ref = refs[piece_count : piece_count + 3]
    vertical_ref, below_ref, first_ref = refs[-9:-6]
    field_hbm, departed_ref, horizontal_ref, field_ref, near_ref, sems = refs[-6:]
    copies = [pltpu.make_async_copy(first_ref, field_hbm.at[pl.ds(0, 1)], sems.at[0])]
    copies[0].start()
    vertical = vertical_ref[...]
    below = below_ref[...]
    plans = [ref[...] for ref in plan_refs]
    for level in range(1, departed_ref.shape[0] + 1):
        ordered = early_ref[level] + ordered_part(level, lat_dev, piece_refs, 1, select_ref)
        rows = level_rows(ordered, table_ref)
        store_rows(rows, field_ref, level - 1, lat_dev, near_ref)
        copy = pltpu.make_async_copy(
            field_ref.at[pl.ds(level - 1, 1)], field_hbm.at[pl.ds(level, 1)], sems.at[level]
        )
        copy.start()
        copies.append(copy)
        horizontal = interpolate(lat_dev, *plans, near_ref)
        departed_ref[level - 1] = (1.0 - vertical) * below + vertical * horizontal
        below = horizontal
    horizontal_ref[...] = below
    for copy in copies:
        copy.wait()


def last_kernel(below_ref, *refs):
    *above_refs, vertical_ref, out_ref = refs
    lev = lax.axis_index("lev")
    is_last = lev == lax.axis_size("lev") - 1
    vertical = vertical_ref[...]
    below = below_ref[...]
    above = below
    for color, above_ref in enumerate(above_refs):
        above = jnp.where(lev % COLORS == color, above_ref[...], above)
    above = jnp.where(is_last, below, above)
    out_ref[...] = (1.0 - vertical) * below + vertical * above


def per_device(legendre, spectral, pair_low, dep_lat, dep_col, lon_steps, tilt_steps):
    pair_local, level_count, _, slot_count = spectral.shape
    wavenumber_count = slot_count - 1
    lon_count = 2 * wavenumber_count
    lat_all = legendre.shape[1]
    wave_size = lax.axis_size("wave")
    lat_dev = lat_all // wave_size
    slots = pl.cdiv(pair_local, GROUP) * GROUP
    extra = slots - pair_local
    if extra:
        spectral = jnp.pad(spectral, ((0, extra), (0, 0), (0, 0), (0, 0)))
        legendre = jnp.pad(legendre, ((0, extra), (0, 0), (0, 0)))
    tables = jnp.asarray(fourier_tables(wavenumber_count))
    parts, tables = legendre_sums(
        (pair_low, spectral, legendre, tables), pair_local, wave_size
    )
    received = [swap(part, 2 * step) if step else part for step, part in enumerate(parts)]
    select, *plans, vertical = plan(
        parts[0],
        pair_low,
        dep_lat,
        dep_col,
        lon_steps,
        tilt_steps,
        pair_local,
        lat_dev,
        2 * GROUP * half_vectors(wave_size // 2, slots // GROUP),
        wavenumber_count,
    )
    received[-1], select = lax.optimization_barrier((received[-1], select))
    blocks = lon_count // LANES
    points = 2 * lat_dev * blocks
    ext_pad = pl.cdiv(lat_dev + 2 * HALO, 8) * 8
    received = [received[step] for step in chip_order(len(received))]
    pieces = [swap(piece, 1) for piece in received]
    vmem = pl.BlockSpec(memory_space=pltpu.VMEM)
    params = pltpu.CompilerParams(vmem_limit_bytes=24 * MIB)
    early = pl.pallas_call(
        functools.partial(early_kernel, lat_dev),
        in_specs=[vmem] * (len(received) + 1),
        out_specs=vmem,
        out_shape=jax.ShapeDtypeStruct(
            (level_count, 8 * ext_pad, wavenumber_count), jnp.float32
        ),
        compiler_params=params,
        cost_estimate=pl.CostEstimate(
            flops=10**8, bytes_accessed=2 * 10**6, transcendentals=0
        ),
        name="early",
    )(*received, select)
    operands = (
        *pieces,
        early,
        select,
        tables,
        *plans,
    )
    near = pltpu.VMEM((3, 2 * ext_pad * blocks, LANES), jnp.float32)
    flat = jax.ShapeDtypeStruct((points, LANES), jnp.float32)
    field_first, horizontal = pl.pallas_call(
        functools.partial(first_kernel, lat_dev, len(pieces)),
        in_specs=[vmem] * len(operands),
        out_specs=[vmem] * 2,
        out_shape=[jax.ShapeDtypeStruct((1, 2 * lat_dev, lon_count), jnp.float32), flat],
        scratch_shapes=[near],
        compiler_params=params,
        cost_estimate=pl.CostEstimate(
            flops=10**8, bytes_accessed=4 * 10**6, transcendentals=0
        ),
        name="first_level",
    )(*operands)
    above = [trade(horizontal, color) for color in range(COLORS)]
    levels = jax.ShapeDtypeStruct((level_count, 2 * lat_dev, lon_count), jnp.float32)
    grid_field, departed, top = pl.pallas_call(
        functools.partial(later_kernel, lat_dev, len(pieces)),
        in_specs=[vmem] * (len(operands) + 3),
        out_specs=[pl.BlockSpec(memory_space=pltpu.HBM), vmem, vmem],
        out_shape=[
            levels,
            jax.ShapeDtypeStruct((level_count - 1, points, LANES), jnp.float32),
            flat,
        ],
        scratch_shapes=[
            pltpu.VMEM((level_count - 1, 2 * lat_dev, lon_count), jnp.float32),
            near,
            pltpu.SemaphoreType.DMA((level_count,)),
        ],
        compiler_params=params,
        cost_estimate=pl.CostEstimate(
            flops=10**8, bytes_accessed=4 * 10**6, transcendentals=0
        ),
        name="later_levels",
    )(*operands, vertical, horizontal, field_first)
    final = pl.pallas_call(
        last_kernel,
        in_specs=[vmem] * (COLORS + 2),
        out_specs=vmem,
        out_shape=flat,
        compiler_params=params,
        name="top_level",
    )(top, *above, vertical)
    departed = jnp.concatenate([departed, final[None]], axis=0)
    return grid_field, departed.reshape(level_count, 2 * lat_dev, lon_count)


def solution(mesh):
    return jax.shard_map(
        per_device,
        mesh=mesh,
        in_specs=(
            P("wave", None, None),
            P("wave", "lev", None, None),
            P(),
            P("wave"),
            P("wave"),
            P("wave", None),
            P("wave", None),
        ),
        out_specs=(P("lev", "wave", None), P("lev", "wave", None)),
        check_vma=False,
    )
```

```python
import functools
import math

import jax
import jax.numpy as jnp
import ml_dtypes
import numpy as np
from jax import lax
from jax.experimental import pallas as pl
from jax.experimental.pallas import tpu as pltpu
from jax.sharding import PartitionSpec as P

LANES = 128
GROUP = 8
HALO = 2
MIB = 1024 * 1024
FAR = -(2**20)
COLORS = 3
ORDER = (0, 2, 1, 3)
NT = (((1,), (1,)), ((), ()))
NN = (((1,), (0,)), ((), ()))


def split(value):
    high = value.astype(jnp.bfloat16)
    low = (value - high.astype(jnp.float32)).astype(jnp.bfloat16)
    return high, low


def widen(value, width):
    lane = lax.broadcasted_iota(jnp.int32, (value.shape[0], LANES), 1)
    full = value.shape[1] // LANES * LANES
    parts = [value[:, :full]]
    for start in range(full, value.shape[1]):
        column = jnp.broadcast_to(value[:, start : start + 1], lane.shape)
        parts.append(jnp.where(lane == start - full, column, 0.0))
    assert len(parts) <= 2 and full + LANES * (len(parts) - 1) == width
    return jnp.concatenate(parts, axis=1)


def half_vectors(chips, groups):
    return pl.cdiv(chips * groups, 8) * 8


def wave_rows(low_ref, wave, pair_local, waves_ref):
    row = lax.broadcasted_iota(jnp.int32, (GROUP, LANES), 0)
    groups = pl.cdiv(pair_local, GROUP)
    chips = low_ref.shape[0] // pair_local // 2
    count = half_vectors(chips, groups)
    for index in range(2 * count):
        half, place = divmod(index, count)
        chip, group = divmod(place, groups)
        value = jnp.full((GROUP, LANES), FAR, jnp.int32)
        if chip < chips:
            base = (wave ^ (2 * chip + half)) * pair_local + group * GROUP
            for slot in range(min(GROUP, pair_local - group * GROUP)):
                value = jnp.where(row == slot, low_ref[base + slot], value)
        waves_ref[index * GROUP : (index + 1) * GROUP] = value


def departure(wave, lat_dev, half, lat_ref, col_ref, lon, tilt, out_refs):
    row_step_ref, place_ref, lon_frac_ref, lat_frac_ref, vertical_ref = out_refs
    points = lon.shape[0]
    blocks = points // (2 * lat_dev)
    row = lax.broadcasted_iota(jnp.int32, lon.shape, 0)
    point = lax.broadcasted_iota(jnp.int32, lon.shape, 1)
    row_step = jnp.zeros(lon.shape, jnp.int32)
    col_step = jnp.zeros(lon.shape, jnp.int32)
    for index in range(points):
        own = wave * lat_dev + index // blocks % lat_dev - HALO
        row_step = jnp.where(row == index, lat_ref[index] - own, row_step)
        first = LANES * (index % blocks)
        col_step = jnp.where(row == index, col_ref[index] - first, col_step)
    col_step = jnp.where(col_step >= half, col_step - 2 * half, col_step)
    col_step = jnp.where(col_step < -half, col_step + 2 * half, col_step)
    quarters = 4 * col_step + lon - 12
    row_step_ref[...] = row_step
    place_ref[...] = point + (quarters >> 2)
    lon_frac_ref[...] = (quarters & 3).astype(jnp.float32) * 0.25
    lat_frac_ref[...] = (tilt & 3).astype(jnp.float32) * 0.25
    vertical_ref[...] = (tilt >> 2).astype(jnp.float32) * 0.25


def legendre_kernel(pair_local, lat_dev, *refs):
    low_hbm, spec_hbm, leg_hbm, table_hbm = refs[:4]
    *chip_refs, table_ref = refs[4:-7]
    low_ref, spec_ref, leg_ref, sums_ref, small_sem, spec_sem, leg_sem = refs[-7:]
    slots, lat_all, slot_count = leg_ref.shape
    level_count = spec_ref.shape[1]
    pair_total = low_ref.shape[0]
    ext = lat_dev + 2 * HALO
    width = pl.cdiv(slot_count, LANES) * LANES
    low_copy = pltpu.make_async_copy(low_hbm, low_ref, small_sem.at[0])
    table_copy = pltpu.make_async_copy(table_hbm, table_ref, small_sem.at[1])
    low_copy.start()
    groups = slots // GROUP
    bounds = sorted({0, min(2, groups), groups})
    copies = []
    for index, (start, stop) in enumerate(zip(bounds[:-1], bounds[1:], strict=True)):
        part = pl.ds(start * GROUP, (stop - start) * GROUP)
        pair = (
            pltpu.make_async_copy(spec_hbm.at[part], spec_ref.at[part], spec_sem.at[index]),
            pltpu.make_async_copy(leg_hbm.at[part], leg_ref.at[part], leg_sem.at[index]),
        )
        for copy in pair:
            copy.start()
        copies.append((start, pair))
    table_copy.start()
    wave = lax.axis_index("wave")
    slot_of_row = lax.broadcasted_iota(jnp.int32, (GROUP, LANES), 0)
    slot_pos = lax.broadcasted_iota(jnp.int32, (GROUP, width), 1)
    low_copy.wait()
    for index in range(groups):
        for at, pair in copies:
            if at == index:
                for copy in pair:
                    copy.wait()
        start = index * GROUP
        base = wave * pair_local + start
        first = jnp.zeros((GROUP, LANES), jnp.int32)
        for slot in range(GROUP):
            low = low_ref[jnp.minimum(base + slot, pair_total - 1)]
            first = jnp.where(slot_of_row == slot, slot_count - 1 - low, first)
        first = jnp.concatenate([first] * (width // LANES), axis=1)
        second = slot_pos >= first
        sign = (1 - 2 * ((slot_pos - jnp.where(second, first, 0)) & 1)).astype(jnp.float32)
        member = [jnp.where(second, 0.0, 1.0), jnp.where(second, 1.0, 0.0)]
        masks = [
            jnp.concatenate(member, axis=0).astype(jnp.bfloat16),
            jnp.concatenate([m * sign for m in member], axis=0).astype(jnp.bfloat16),
        ]
        highs, lows = [], []
        for level in range(level_count):
            for part in range(2):
                row = widen(spec_ref[pl.ds(start, GROUP), level, part, :], width)
                high, low = split(jnp.concatenate([row, row], axis=0))
                highs += [high * mask for mask in masks]
                lows += [low * mask for mask in masks]
        columns = jnp.concatenate(highs + lows, axis=0)
        count = columns.shape[0] // 2
        half = GROUP * lat_all
        table = leg_ref[pl.ds(start, GROUP)].reshape(half, slot_count)
        rows = jnp.concatenate(split(widen(table, width)), axis=0)
        crossed = lax.dot_general(rows, columns, NT, preferred_element_type=jnp.float32)
        crossed = (crossed[:half, :count] + crossed[:half, count:]) + (
            crossed[half:, :count] + crossed[half:, count:]
        )
        slot_of_lane = lax.broadcasted_iota(jnp.int32, (lat_all, count), 1) % GROUP
        sums = crossed[:lat_all]
        for slot in range(1, GROUP):
            block = crossed[slot * lat_all : (slot + 1) * lat_all]
            sums = jnp.where(slot_of_lane == slot, block, sums)
        edge = jnp.zeros((HALO, count), jnp.float32)
        padded = jnp.concatenate([edge, sums, edge], axis=0)
        here = slice(index * ext, (index + 1) * ext)
        for dest in range(sums_ref.shape[0]):
            sums_ref[dest, here] = padded[dest * lat_dev : dest * lat_dev + ext]
    used = groups * ext
    sums_ref[:, used:] = jnp.zeros_like(sums_ref[:, used:])
    for step, chip_ref in enumerate(chip_refs):
        dest = (wave // 2 ^ step) * 2
        for core in range(2):
            chip_ref[core] = sums_ref[dest + core]
    table_copy.wait()


def legendre_sums(operands, pair_local, wave_size):
    pair_low, spectral, legendre, tables = operands
    slots, level_count = spectral.shape[:2]
    lat_all = legendre.shape[1]
    lat_dev = lat_all // wave_size
    lanes = 8 * level_count * GROUP
    ext = lat_dev + 2 * HALO
    rows = pl.cdiv((slots // GROUP - 1) * ext + pl.cdiv(ext, 8) * 8, 8) * 8
    chips = wave_size // 2
    out = jax.ShapeDtypeStruct((2, rows, lanes), jnp.float32)
    outs = [out] * chips + [jax.ShapeDtypeStruct(tables.shape, tables.dtype)]
    results = pl.pallas_call(
        functools.partial(legendre_kernel, pair_local, lat_dev),
        in_specs=[pl.BlockSpec(memory_space=pltpu.HBM)] * len(operands),
        out_specs=[pl.BlockSpec(memory_space=pltpu.VMEM)] * len(outs),
        out_shape=outs,
        scratch_shapes=[
            pltpu.SMEM(pair_low.shape, jnp.int32),
            pltpu.VMEM(spectral.shape, jnp.float32),
            pltpu.VMEM(legendre.shape, jnp.float32),
            pltpu.VMEM((wave_size, rows, lanes), jnp.float32),
            pltpu.SemaphoreType.DMA((2,)),
            pltpu.SemaphoreType.DMA((2,)),
            pltpu.SemaphoreType.DMA((2,)),
        ],
        compiler_params=pltpu.CompilerParams(vmem_limit_bytes=24 * MIB),
        name="legendre",
    )(*[pltpu.with_memory_space_constraint(x, pltpu.HBM) for x in operands])
    return results[:chips], results[chips]


def chip_order(count):
    return [0, *range(count - 1, 0, -1)]


def swap(value, by):
    wave_size = lax.axis_size("wave")
    return lax.ppermute(value, "wave", [(i, i ^ by) for i in range(wave_size)])


def trade(value, color):
    lev_size, wave_size = lax.axis_size("lev"), lax.axis_size("wave")
    pairs = []
    for lev in range(lev_size):
        other = lev
        if lev % COLORS == color and lev + 1 < lev_size:
            other = lev + 1
        if lev > 0 and (lev - 1) % COLORS == color:
            other = lev - 1
        for wave in range(wave_size):
            there = other * wave_size + (wave ^ 1 if other == lev else wave)
            pairs.append((lev * wave_size + wave, there))
    return lax.ppermute(value, ("lev", "wave"), pairs)


def plan_kernel(pair_local, lat_dev, table_ref, *refs):
    sources = refs[:5]
    select_ref, turned_ref, turn_ref, *plan_refs = refs[5:-7]
    low_ref, lat_ref, col_ref, lon_ref, tilt_ref, waves_ref, sems = refs[-7:]
    copies = [
        pltpu.make_async_copy(there, here, sems.at[i])
        for i, (there, here) in enumerate(zip(sources, refs[-7:-2], strict=True))
    ]
    for copy in copies:
        copy.start()
    half = select_ref.shape[1]
    quarter = half // 4
    lane = lax.broadcasted_iota(jnp.int32, (2 * GROUP, half), 1)
    kind = sum((lane >= quarter * i).astype(jnp.int32) for i in range(1, 4))
    order = 4 * (lane - quarter * kind)
    for i, first in enumerate(ORDER):
        order = jnp.where(kind == i, order + first, order)
    wave = lax.axis_index("wave")
    for copy in copies:
        copy.wait()
    departure(wave, lat_dev, half, lat_ref, col_ref, lon_ref[...], tilt_ref[...], plan_refs)
    wave_rows(low_ref, wave, pair_local, waves_ref)
    for start in range(0, waves_ref.shape[0], GROUP):
        waves = waves_ref[start : start + GROUP]
        waves = jnp.concatenate([waves, half - 1 - waves], axis=0)
        waves = jnp.concatenate([waves] * (half // LANES), axis=1)
        match = jnp.where(waves == order, 1.0, 0.0).astype(jnp.bfloat16)
        select_ref[2 * start : 2 * (start + GROUP)] = match
    row = lax.broadcasted_iota(jnp.int32, (2 * GROUP, half), 0)
    sign = jnp.where((kind == 0) | (kind == 2), 1.0, -1.0)
    turns = jnp.where((row == 0) == (kind < 2), sign, 0.0)
    turns = jnp.where(row < 2, turns, 0.0).astype(jnp.bfloat16)
    lanes = select_ref.shape[0] // 2
    late = select_ref[lanes:]
    turn_ref[...] = lax.dot_general(turns, late, NT, preferred_element_type=jnp.float32)
    even, odd = table_ref[0], table_ref[1]
    both = (
        jnp.concatenate([even[: half // 2], odd[half // 2 :]], axis=0),
        jnp.concatenate([even[half // 2 :], odd[: half // 2]], axis=0),
    )
    for part, table in enumerate(both):
        turned_ref[part * lanes : (part + 1) * lanes] = lax.dot_general(
            late, table, NN, preferred_element_type=jnp.float32
        ).astype(jnp.bfloat16)


def plan(tables, pair_low, dep_lat, dep_col, lon_steps, tilt_steps, pair_local, lat_dev, slots, half):
    operands = (pair_low, dep_lat, dep_col, lon_steps, tilt_steps)
    integer = jax.ShapeDtypeStruct(lon_steps.shape, jnp.int32)
    fraction = jax.ShapeDtypeStruct(lon_steps.shape, jnp.float32)
    outs = [
        jax.ShapeDtypeStruct((2 * slots, half), jnp.bfloat16),
        jax.ShapeDtypeStruct((2 * slots, tables.shape[2]), jnp.bfloat16),
        jax.ShapeDtypeStruct((2 * GROUP, slots), jnp.float32),
        integer,
        integer,
        fraction,
        fraction,
        fraction,
    ]
    return pl.pallas_call(
        functools.partial(plan_kernel, pair_local, lat_dev),
        in_specs=[pl.BlockSpec(memory_space=pltpu.VMEM)]
        + [pl.BlockSpec(memory_space=pltpu.HBM)] * len(operands),
        out_specs=[pl.BlockSpec(memory_space=pltpu.VMEM)] * len(outs),
        out_shape=outs,
        scratch_shapes=[
            pltpu.SMEM(pair_low.shape, jnp.int32),
            pltpu.SMEM(dep_lat.shape, jnp.int32),
            pltpu.SMEM(dep_col.shape, jnp.int32),
            pltpu.VMEM(lon_steps.shape, jnp.int32),
            pltpu.VMEM(tilt_steps.shape, jnp.int32),
            pltpu.VMEM((slots, LANES), jnp.int32),
            pltpu.SemaphoreType.DMA((len(operands),)),
        ],
        compiler_params=pltpu.CompilerParams(vmem_limit_bytes=24 * MIB),
        cost_estimate=pl.CostEstimate(
            flops=10**7, bytes_accessed=4 * 10**6, transcendentals=0
        ),
        name="plan",
    )(tables, *[pltpu.with_memory_space_constraint(x, pltpu.HBM) for x in operands])


def fourier_tables(wavenumber_count):
    lon_count = 2 * wavenumber_count
    quarter = lon_count // 4
    whole = quarter // LANES * LANES
    tables = []
    for parity in range(2):
        kinds = ORDER[2 * parity : 2 * parity + 2]
        wave = np.concatenate([np.arange(kind, wavenumber_count, 4) for kind in kinds])
        phase = wave[:, None] * np.arange(quarter)[None, :] % lon_count
        angle = phase * (2.0 * math.pi / lon_count)
        weight = np.where(wave == 0, 1.0, 2.0)[:, None]
        parts = [weight * np.cos(angle), -weight * np.sin(angle)]
        tables.append(np.concatenate(parts if parity == 0 else parts[::-1], axis=0))
    exact = np.stack(tables)
    high = exact.astype(ml_dtypes.bfloat16)
    low = (exact - high.astype(np.float64)).astype(ml_dtypes.bfloat16)
    return np.concatenate(
        [high[..., :whole], low[..., :whole], high[..., whole:], low[..., whole:]], axis=2
    )


def add_halves(product, start, count):
    high = product[start : start + count]
    low = product[start + count : start + 2 * count]
    whole = (product.shape[1] - LANES) // 2
    tail = high[:, 2 * whole :]
    tail = tail + (low[:, 2 * whole :] + pltpu.roll(tail, LANES // 2, 1))
    pieces = [
        high[:, at : at + LANES] + (low[:, at : at + LANES] + high[:, whole + at : whole + at + LANES])
        for at in range(0, whole, LANES)
    ]
    return pieces + [tail]


def join(first, second):
    lane = lax.broadcasted_iota(jnp.int32, first[0].shape, 1)
    rolled = [pltpu.roll(piece, LANES // 2, 1) for piece in second]
    before = [first[-1], *rolled[:-1]]
    return first[:-1] + [
        jnp.where(lane < LANES // 2, a, b) for a, b in zip(before, rolled, strict=True)
    ]


def regroup(pieces, level, lane):
    piece_lanes = LANES // 8
    upper = lane // piece_lanes >= 4
    if level == 0:
        pieces = [
            jnp.where(upper, pltpu.roll(pieces[i + 4], 4 * piece_lanes, 1), pieces[i])
            for i in range(4)
        ]
    else:
        pieces = [
            jnp.where(upper, pieces[i + 4], pltpu.roll(pieces[i], 4 * piece_lanes, 1))
            for i in range(4)
        ]
    for bit in (1, 2):
        upper = (lane // piece_lanes & bit) != 0
        for one in range(4):
            if one & bit:
                continue
            a, b = pieces[one], pieces[one | bit]
            pieces[one] = jnp.where(upper, pltpu.roll(b, piece_lanes * bit, 1), a)
            pieces[one | bit] = jnp.where(
                upper, b, pltpu.roll(a, LANES - piece_lanes * bit, 1)
            )
    return pieces


def slot_matrix(level, lat_dev, piece_refs):
    ext = lat_dev + 2 * HALO
    ext_pad = pl.cdiv(ext, 8) * 8
    core = lax.axis_index("wave") % 2
    vectors = []
    order = chip_order(len(piece_refs))
    for ref in [piece_refs[order.index(step)] for step in range(len(piece_refs))]:
        source = ref[core]
        vectors += [
            source[start : start + ext_pad]
            for start in range(0, source.shape[0] - ext_pad + 1, ext)
        ]
    vectors += [jnp.zeros_like(vectors[0])] * (-len(vectors) % 8)
    lane = lax.broadcasted_iota(jnp.int32, vectors[0].shape, 1)
    columns = [[] for _ in range(4)]
    for start in range(0, len(vectors), 8):
        for kind, piece in enumerate(regroup(vectors[start : start + 8], level, lane)):
            columns[kind].append(piece)
    matrix = jnp.concatenate([jnp.concatenate(c, axis=1) for c in columns], axis=0)
    return matrix


def ordered_part(level, lat_dev, piece_refs, half, select_ref):
    matrix = slot_matrix(level, lat_dev, piece_refs)
    high, low = split(matrix)
    count = high.shape[0] // 2
    lanes = matrix.shape[1]
    return lax.dot_general(
        jnp.concatenate([high[:count], low[:count], high[count:], low[count:]], axis=0),
        select_ref[half * lanes : (half + 1) * lanes],
        NN,
        preferred_element_type=jnp.float32,
    )


def level_quarters(ordered, table_ref):
    count = ordered.shape[0] // 4
    half = ordered.shape[1]
    real = ordered[: 2 * count]
    imag = pltpu.roll(ordered[2 * count :], half // 2, 1)
    lane = lax.broadcasted_iota(jnp.int32, real.shape, 1)
    first_half = lane < half // 2
    outer = (lane < half // 4) | (lane >= half // 4 * 3)
    even = jnp.where(first_half, real, imag)
    odd = jnp.where(first_half, imag, real)
    turned = pltpu.roll(odd, half // 2, 1)
    even_turned = jnp.where(first_half == outer, even, -even)
    odd_turned = jnp.where(outer, turned, -turned)
    products = [
        lax.dot_general(
            jnp.concatenate(rows, axis=0).astype(jnp.bfloat16),
            table_ref[parity],
            NN,
            preferred_element_type=jnp.float32,
        )
        for parity, rows in enumerate(((even, even_turned), (odd, odd_turned)))
    ]
    near, far = [
        [add_halves(product, start, count) for product in products] for start in (0, 2 * count)
    ]
    return [
        [a + b for a, b in zip(*near, strict=True)],
        [a + b for a, b in zip(*far, strict=True)],
        [a - b for a, b in zip(*near, strict=True)],
        [a - b for a, b in zip(*far, strict=True)],
    ]


def level_rows(quarters):
    return join(quarters[0], quarters[1]) + join(quarters[2], quarters[3])


def late_quarters(matrix, turned_ref, turn_ref):
    count = matrix.shape[0] // 2
    cosine = jnp.broadcast_to(turn_ref[0:1], (count, matrix.shape[1]))
    sine = jnp.broadcast_to(turn_ref[1:2], (count, matrix.shape[1]))
    square = cosine * cosine - sine * sine
    parts = [
        (part[:count].astype(jnp.float32), part[count:].astype(jnp.float32))
        for part in split(matrix)
    ]
    rows = []
    rows += [(re, im) for re, im in parts]
    rows += [(cosine * re - sine * im, cosine * im + sine * re) for re, im in parts]
    rows += [(square * re, square * im) for re, im in parts]
    rows += [(cosine * re + sine * im, cosine * im - sine * re) for re, im in parts]
    product = lax.dot_general(
        jnp.concatenate([jnp.concatenate(row, axis=1) for row in rows], axis=0).astype(
            jnp.bfloat16
        ),
        turned_ref[...],
        NN,
        preferred_element_type=jnp.float32,
    )
    return [add_halves(product, 2 * count * quarter, count) for quarter in range(4)]


def store_rows(rows, field_ref, level, lat_dev, near_ref):
    blocks = len(rows)
    count = rows[0].shape[0]
    for at, value in enumerate(rows):
        there = slice(at * LANES, (at + 1) * LANES)
        for hemi in range(2):
            start = hemi * (count // 2) + HALO
            field_ref[level, hemi * lat_dev : (hemi + 1) * lat_dev, there] = value[
                start : start + lat_dev
            ]
        for side in range(3):
            place = (at + 1 - side) % blocks
            near_ref[side, pl.ds(place, count, stride=blocks), :] = value


def interpolate(lat_dev, row_step, step, f, g, near_ref):
    blocks = row_step.shape[0] // (2 * lat_dev)
    ext_pad = near_ref.shape[1] // (2 * blocks)
    points = 2 * lat_dev * blocks
    point = lax.broadcasted_iota(jnp.int32, (points, LANES), 1)

    def line(side, j):
        return jnp.concatenate(
            [
                near_ref[side, pl.ds((hemi * ext_pad + j) * blocks, lat_dev * blocks), :]
                for hemi in range(2)
            ],
            axis=0,
        )

    lines = [[line(side, j) for j in range(2 * HALO + 1)] for side in range(3)]
    values = []
    for upper in range(2):
        picked = []
        for side in range(3):
            choice = lines[side][upper]
            for j in range(1, 2 * HALO):
                choice = jnp.where(row_step == j, lines[side][j + upper], choice)
            picked.append(choice)
        left = jnp.where(point >= LANES - 28, picked[0], picked[1])
        right = jnp.where(point < 28, picked[2], picked[1])
        for shift in range(2):
            place = (step + shift) & (LANES - 1)
            values.append(
                jnp.where(
                    point < LANES // 2,
                    jnp.take_along_axis(left, place, axis=1),
                    jnp.take_along_axis(right, place, axis=1),
                )
            )
    lower = (1.0 - f) * values[0] + f * values[1]
    higher = (1.0 - f) * values[2] + f * values[3]
    return (1.0 - g) * lower + g * higher


def early_kernel(lat_dev, piece_count, *refs):
    piece_refs = refs[:piece_count]
    select_ref, table_ref, quarters_ref, later_ref = refs[piece_count:]
    ordered = ordered_part(0, lat_dev, piece_refs, 0, select_ref)
    pieces = sum(level_quarters(ordered, table_ref), [])
    for index, piece in enumerate(pieces):
        quarters_ref[index] = piece
    for level in range(later_ref.shape[0]):
        later_ref[level] = ordered_part(level + 1, lat_dev, piece_refs, 0, select_ref)


def first_kernel(lat_dev, piece_count, *refs):
    piece_refs, plan_refs = refs[:piece_count], refs[piece_count + 3 : -3]
    quarters_ref, turned_ref, turn_ref = refs[piece_count : piece_count + 3]
    field_ref, horizontal_ref, near_ref = refs[-3:]
    matrix = slot_matrix(0, lat_dev, piece_refs)
    quarters = late_quarters(matrix, turned_ref, turn_ref)
    size = len(quarters[0])
    quarters = [
        [piece + quarters_ref[size * i + j] for j, piece in enumerate(quarter)]
        for i, quarter in enumerate(quarters)
    ]
    store_rows(level_rows(quarters), field_ref, 0, lat_dev, near_ref)
    horizontal_ref[...] = interpolate(lat_dev, *[ref[...] for ref in plan_refs], near_ref)


def later_kernel(lat_dev, piece_count, *refs):
    piece_refs, plan_refs = refs[:piece_count], refs[piece_count + 3 : -9]
    early_ref, select_ref, table_ref = refs[piece_count : piece_count + 3]
    vertical_ref, below_ref, first_ref = refs[-9:-6]
    field_hbm, departed_ref, horizontal_ref, field_ref, near_ref, sems = refs[-6:]
    copies = [pltpu.make_async_copy(first_ref, field_hbm.at[pl.ds(0, 1)], sems.at[0])]
    copies[0].start()
    vertical = vertical_ref[...]
    below = below_ref[...]
    plans = [ref[...] for ref in plan_refs]
    for level in range(1, departed_ref.shape[0] + 1):
        ordered = early_ref[level - 1]
        ordered = ordered + ordered_part(level, lat_dev, piece_refs, 1, select_ref)
        rows = level_rows(level_quarters(ordered, table_ref))
        store_rows(rows, field_ref, level - 1, lat_dev, near_ref)
        copy = pltpu.make_async_copy(
            field_ref.at[pl.ds(level - 1, 1)], field_hbm.at[pl.ds(level, 1)], sems.at[level]
        )
        copy.start()
        copies.append(copy)
        horizontal = interpolate(lat_dev, *plans, near_ref)
        departed_ref[level - 1] = (1.0 - vertical) * below + vertical * horizontal
        below = horizontal
    horizontal_ref[...] = below
    for copy in copies:
        copy.wait()


def last_kernel(below_ref, *refs):
    *above_refs, vertical_ref, out_ref = refs
    lev = lax.axis_index("lev")
    is_last = lev == lax.axis_size("lev") - 1
    vertical = vertical_ref[...]
    below = below_ref[...]
    above = below
    for color, above_ref in enumerate(above_refs):
        above = jnp.where(lev % COLORS == color, above_ref[...], above)
    above = jnp.where(is_last, below, above)
    out_ref[...] = (1.0 - vertical) * below + vertical * above


def per_device(legendre, spectral, pair_low, dep_lat, dep_col, lon_steps, tilt_steps):
    pair_local, level_count, _, slot_count = spectral.shape
    wavenumber_count = slot_count - 1
    lon_count = 2 * wavenumber_count
    lat_all = legendre.shape[1]
    wave_size = lax.axis_size("wave")
    lat_dev = lat_all // wave_size
    slots = pl.cdiv(pair_local, GROUP) * GROUP
    extra = slots - pair_local
    if extra:
        spectral = jnp.pad(spectral, ((0, extra), (0, 0), (0, 0), (0, 0)))
        legendre = jnp.pad(legendre, ((0, extra), (0, 0), (0, 0)))
    tables = jnp.asarray(fourier_tables(wavenumber_count))
    parts, tables = legendre_sums(
        (pair_low, spectral, legendre, tables), pair_local, wave_size
    )
    received = [swap(part, 2 * step) if step else part for step, part in enumerate(parts)]
    select, turned, turn, *plans, vertical = plan(
        tables,
        pair_low,
        dep_lat,
        dep_col,
        lon_steps,
        tilt_steps,
        pair_local,
        lat_dev,
        2 * GROUP * half_vectors(wave_size // 2, slots // GROUP),
        wavenumber_count,
    )
    received[-1], select = lax.optimization_barrier((received[-1], select))
    blocks = lon_count // LANES
    points = 2 * lat_dev * blocks
    ext_pad = pl.cdiv(lat_dev + 2 * HALO, 8) * 8
    received = [received[step] for step in chip_order(len(received))]
    pieces = [swap(piece, 1) for piece in received]
    vmem = pl.BlockSpec(memory_space=pltpu.VMEM)
    params = pltpu.CompilerParams(vmem_limit_bytes=24 * MIB)
    quarter_pieces = 4 * pl.cdiv(lon_count // 4, LANES)
    quarters, early = pl.pallas_call(
        functools.partial(early_kernel, lat_dev, len(received)),
        in_specs=[vmem] * (len(received) + 2),
        out_specs=[vmem] * 2,
        out_shape=[
            jax.ShapeDtypeStruct((quarter_pieces, 2 * ext_pad, LANES), jnp.float32),
            jax.ShapeDtypeStruct(
                (level_count - 1, 8 * ext_pad, wavenumber_count), jnp.float32
            ),
        ],
        compiler_params=params,
        cost_estimate=pl.CostEstimate(
            flops=10**8, bytes_accessed=2 * 10**6, transcendentals=0
        ),
        name="early",
    )(*received, select, tables)
    first_operands = (*pieces, quarters, turned, turn, *plans)
    operands = (*pieces, early, select, tables, *plans)
    near = pltpu.VMEM((3, 2 * ext_pad * blocks, LANES), jnp.float32)
    flat = jax.ShapeDtypeStruct((points, LANES), jnp.float32)
    field_first, horizontal = pl.pallas_call(
        functools.partial(first_kernel, lat_dev, len(pieces)),
        in_specs=[vmem] * len(first_operands),
        out_specs=[vmem] * 2,
        out_shape=[jax.ShapeDtypeStruct((1, 2 * lat_dev, lon_count), jnp.float32), flat],
        scratch_shapes=[near],
        compiler_params=params,
        cost_estimate=pl.CostEstimate(
            flops=10**8, bytes_accessed=4 * 10**6, transcendentals=0
        ),
        name="first_level",
    )(*first_operands)
    above = [trade(horizontal, color) for color in range(COLORS)]
    levels = jax.ShapeDtypeStruct((level_count, 2 * lat_dev, lon_count), jnp.float32)
    grid_field, departed, top = pl.pallas_call(
        functools.partial(later_kernel, lat_dev, len(pieces)),
        in_specs=[vmem] * (len(operands) + 3),
        out_specs=[pl.BlockSpec(memory_space=pltpu.HBM), vmem, vmem],
        out_shape=[
            levels,
            jax.ShapeDtypeStruct((level_count - 1, points, LANES), jnp.float32),
            flat,
        ],
        scratch_shapes=[
            pltpu.VMEM((level_count - 1, 2 * lat_dev, lon_count), jnp.float32),
            near,
            pltpu.SemaphoreType.DMA((level_count,)),
        ],
        compiler_params=params,
        cost_estimate=pl.CostEstimate(
            flops=10**8, bytes_accessed=4 * 10**6, transcendentals=0
        ),
        name="later_levels",
    )(*operands, vertical, horizontal, field_first)
    final = pl.pallas_call(
        last_kernel,
        in_specs=[vmem] * (COLORS + 2),
        out_specs=vmem,
        out_shape=flat,
        compiler_params=params,
        name="top_level",
    )(top, *above, vertical)
    departed = jnp.concatenate([departed, final[None]], axis=0)
    return grid_field, departed.reshape(level_count, 2 * lat_dev, lon_count)


def solution(mesh):
    return jax.shard_map(
        per_device,
        mesh=mesh,
        in_specs=(
            P("wave", None, None),
            P("wave", "lev", None, None),
            P(),
            P("wave"),
            P("wave"),
            P("wave", None),
            P("wave", None),
        ),
        out_specs=(P("lev", "wave", None), P("lev", "wave", None)),
        check_vma=False,
    )
```

```python
import functools
import math

import jax
import jax.numpy as jnp
import ml_dtypes
import numpy as np
from jax import lax
from jax.experimental import pallas as pl
from jax.experimental.pallas import tpu as pltpu
from jax.sharding import PartitionSpec as P

LANES = 128
GROUP = 8
HALO = 2
MIB = 1024 * 1024
FAR = -(2**20)
COLORS = 3
ORDER = (0, 2, 1, 3)
NT = (((1,), (1,)), ((), ()))
NN = (((1,), (0,)), ((), ()))


def split(value):
    high = value.astype(jnp.bfloat16)
    low = (value - high.astype(jnp.float32)).astype(jnp.bfloat16)
    return high, low


def widen(value, width):
    lane = lax.broadcasted_iota(jnp.int32, (value.shape[0], LANES), 1)
    full = value.shape[1] // LANES * LANES
    parts = [value[:, :full]]
    for start in range(full, value.shape[1]):
        column = jnp.broadcast_to(value[:, start : start + 1], lane.shape)
        parts.append(jnp.where(lane == start - full, column, 0.0))
    assert len(parts) <= 2 and full + LANES * (len(parts) - 1) == width
    return jnp.concatenate(parts, axis=1)


def half_vectors(chips, groups):
    return pl.cdiv(chips * groups, 8) * 8


def wave_rows(low_ref, wave, pair_local, waves_ref):
    row = lax.broadcasted_iota(jnp.int32, (GROUP, LANES), 0)
    groups = pl.cdiv(pair_local, GROUP)
    chips = low_ref.shape[0] // pair_local // 2
    count = half_vectors(chips, groups)
    for index in range(2 * count):
        half, place = divmod(index, count)
        chip, group = divmod(place, groups)
        value = jnp.full((GROUP, LANES), FAR, jnp.int32)
        if chip < chips:
            base = (wave ^ (2 * chip + half)) * pair_local + group * GROUP
            for slot in range(min(GROUP, pair_local - group * GROUP)):
                value = jnp.where(row == slot, low_ref[base + slot], value)
        waves_ref[index * GROUP : (index + 1) * GROUP] = value


def departure(wave, lat_dev, half, lat_ref, col_ref, lon, tilt, out_refs):
    row_step_ref, place_ref, lon_frac_ref, lat_frac_ref, vertical_ref = out_refs
    points = lon.shape[0]
    blocks = points // (2 * lat_dev)
    row = lax.broadcasted_iota(jnp.int32, lon.shape, 0)
    point = lax.broadcasted_iota(jnp.int32, lon.shape, 1)
    row_step = jnp.zeros(lon.shape, jnp.int32)
    col_step = jnp.zeros(lon.shape, jnp.int32)
    for index in range(points):
        own = wave * lat_dev + index // blocks % lat_dev - HALO
        row_step = jnp.where(row == index, lat_ref[index] - own, row_step)
        first = LANES * (index % blocks)
        col_step = jnp.where(row == index, col_ref[index] - first, col_step)
    col_step = jnp.where(col_step >= half, col_step - 2 * half, col_step)
    col_step = jnp.where(col_step < -half, col_step + 2 * half, col_step)
    quarters = 4 * col_step + lon - 12
    row_step_ref[...] = row_step
    place_ref[...] = point + (quarters >> 2)
    lon_frac_ref[...] = (quarters & 3).astype(jnp.float32) * 0.25
    lat_frac_ref[...] = (tilt & 3).astype(jnp.float32) * 0.25
    vertical_ref[...] = (tilt >> 2).astype(jnp.float32) * 0.25


def legendre_kernel(pair_local, lat_dev, *refs):
    low_hbm, spec_hbm, leg_hbm, table_hbm = refs[:4]
    *chip_refs, table_ref = refs[4:-7]
    low_ref, spec_ref, leg_ref, sums_ref, small_sem, spec_sem, leg_sem = refs[-7:]
    slots, lat_all, slot_count = leg_ref.shape
    level_count = spec_ref.shape[1]
    pair_total = low_ref.shape[0]
    ext = lat_dev + 2 * HALO
    width = pl.cdiv(slot_count, LANES) * LANES
    low_copy = pltpu.make_async_copy(low_hbm, low_ref, small_sem.at[0])
    table_copy = pltpu.make_async_copy(table_hbm, table_ref, small_sem.at[1])
    low_copy.start()
    groups = slots // GROUP
    bounds = sorted({0, min(2, groups), groups})
    copies = []
    for index, (start, stop) in enumerate(zip(bounds[:-1], bounds[1:], strict=True)):
        part = pl.ds(start * GROUP, (stop - start) * GROUP)
        pair = (
            pltpu.make_async_copy(spec_hbm.at[part], spec_ref.at[part], spec_sem.at[index]),
            pltpu.make_async_copy(leg_hbm.at[part], leg_ref.at[part], leg_sem.at[index]),
        )
        for copy in pair:
            copy.start()
        copies.append((start, pair))
    table_copy.start()
    wave = lax.axis_index("wave")
    slot_of_row = lax.broadcasted_iota(jnp.int32, (GROUP, LANES), 0)
    slot_pos = lax.broadcasted_iota(jnp.int32, (GROUP, width), 1)
    low_copy.wait()
    for index in range(groups):
        for at, pair in copies:
            if at == index:
                for copy in pair:
                    copy.wait()
        start = index * GROUP
        base = wave * pair_local + start
        first = jnp.zeros((GROUP, LANES), jnp.int32)
        for slot in range(GROUP):
            low = low_ref[jnp.minimum(base + slot, pair_total - 1)]
            first = jnp.where(slot_of_row == slot, slot_count - 1 - low, first)
        first = jnp.concatenate([first] * (width // LANES), axis=1)
        second = slot_pos >= first
        sign = (1 - 2 * ((slot_pos - jnp.where(second, first, 0)) & 1)).astype(jnp.float32)
        member = [jnp.where(second, 0.0, 1.0), jnp.where(second, 1.0, 0.0)]
        masks = [
            jnp.concatenate(member, axis=0).astype(jnp.bfloat16),
            jnp.concatenate([m * sign for m in member], axis=0).astype(jnp.bfloat16),
        ]
        highs, lows = [], []
        for level in range(level_count):
            for part in range(2):
                row = widen(spec_ref[pl.ds(start, GROUP), level, part, :], width)
                high, low = split(jnp.concatenate([row, row], axis=0))
                highs += [high * mask for mask in masks]
                lows += [low * mask for mask in masks]
        columns = jnp.concatenate(highs + lows, axis=0)
        count = columns.shape[0] // 2
        half = GROUP * lat_all
        table = leg_ref[pl.ds(start, GROUP)].reshape(half, slot_count)
        rows = jnp.concatenate(split(widen(table, width)), axis=0)
        crossed = lax.dot_general(rows, columns, NT, preferred_element_type=jnp.float32)
        crossed = (crossed[:half, :count] + crossed[:half, count:]) + (
            crossed[half:, :count] + crossed[half:, count:]
        )
        slot_of_lane = lax.broadcasted_iota(jnp.int32, (lat_all, count), 1) % GROUP
        sums = crossed[:lat_all]
        for slot in range(1, GROUP):
            block = crossed[slot * lat_all : (slot + 1) * lat_all]
            sums = jnp.where(slot_of_lane == slot, block, sums)
        edge = jnp.zeros((HALO, count), jnp.float32)
        padded = jnp.concatenate([edge, sums, edge], axis=0)
        here = slice(index * ext, (index + 1) * ext)
        for dest in range(sums_ref.shape[0]):
            sums_ref[dest, here] = padded[dest * lat_dev : dest * lat_dev + ext]
    used = groups * ext
    sums_ref[:, used:] = jnp.zeros_like(sums_ref[:, used:])
    for step, chip_ref in enumerate(chip_refs):
        dest = (wave // 2 ^ step) * 2
        for core in range(2):
            chip_ref[core] = sums_ref[dest + core]
    table_copy.wait()


def legendre_sums(operands, pair_local, wave_size):
    pair_low, spectral, legendre, tables = operands
    slots, level_count = spectral.shape[:2]
    lat_all = legendre.shape[1]
    lat_dev = lat_all // wave_size
    lanes = 8 * level_count * GROUP
    ext = lat_dev + 2 * HALO
    rows = pl.cdiv((slots // GROUP - 1) * ext + pl.cdiv(ext, 8) * 8, 8) * 8
    chips = wave_size // 2
    out = jax.ShapeDtypeStruct((2, rows, lanes), jnp.float32)
    outs = [out] * chips + [jax.ShapeDtypeStruct(tables.shape, tables.dtype)]
    results = pl.pallas_call(
        functools.partial(legendre_kernel, pair_local, lat_dev),
        in_specs=[pl.BlockSpec(memory_space=pltpu.HBM)] * len(operands),
        out_specs=[pl.BlockSpec(memory_space=pltpu.VMEM)] * len(outs),
        out_shape=outs,
        scratch_shapes=[
            pltpu.SMEM(pair_low.shape, jnp.int32),
            pltpu.VMEM(spectral.shape, jnp.float32),
            pltpu.VMEM(legendre.shape, jnp.float32),
            pltpu.VMEM((wave_size, rows, lanes), jnp.float32),
            pltpu.SemaphoreType.DMA((2,)),
            pltpu.SemaphoreType.DMA((2,)),
            pltpu.SemaphoreType.DMA((2,)),
        ],
        compiler_params=pltpu.CompilerParams(vmem_limit_bytes=24 * MIB),
        name="legendre",
    )(*[pltpu.with_memory_space_constraint(x, pltpu.HBM) for x in operands])
    return results[:chips], results[chips]


def chip_order(count):
    return [0, *range(count - 1, 0, -1)]


def swap(value, by):
    wave_size = lax.axis_size("wave")
    return lax.ppermute(value, "wave", [(i, i ^ by) for i in range(wave_size)])


def trade(value, color):
    lev_size, wave_size = lax.axis_size("lev"), lax.axis_size("wave")
    pairs = []
    for lev in range(lev_size):
        other = lev
        if lev % COLORS == color and lev + 1 < lev_size:
            other = lev + 1
        if lev > 0 and (lev - 1) % COLORS == color:
            other = lev - 1
        for wave in range(wave_size):
            there = other * wave_size + (wave ^ 1 if other == lev else wave)
            pairs.append((lev * wave_size + wave, there))
    return lax.ppermute(value, ("lev", "wave"), pairs)


def plan_kernel(pair_local, lat_dev, table_ref, *refs):
    sources = refs[:5]
    select_ref, turned_ref, turn_ref, *plan_refs = refs[5:-7]
    low_ref, lat_ref, col_ref, lon_ref, tilt_ref, waves_ref, sems = refs[-7:]
    copies = [
        pltpu.make_async_copy(there, here, sems.at[i])
        for i, (there, here) in enumerate(zip(sources, refs[-7:-2], strict=True))
    ]
    for copy in copies:
        copy.start()
    half = select_ref.shape[1]
    quarter = half // 4
    lane = lax.broadcasted_iota(jnp.int32, (2 * GROUP, half), 1)
    kind = sum((lane >= quarter * i).astype(jnp.int32) for i in range(1, 4))
    order = 4 * (lane - quarter * kind)
    for i, first in enumerate(ORDER):
        order = jnp.where(kind == i, order + first, order)
    wave = lax.axis_index("wave")
    for copy in copies:
        copy.wait()
    departure(wave, lat_dev, half, lat_ref, col_ref, lon_ref[...], tilt_ref[...], plan_refs)
    wave_rows(low_ref, wave, pair_local, waves_ref)
    for start in range(0, waves_ref.shape[0], GROUP):
        waves = waves_ref[start : start + GROUP]
        waves = jnp.concatenate([waves, half - 1 - waves], axis=0)
        waves = jnp.concatenate([waves] * (half // LANES), axis=1)
        match = jnp.where(waves == order, 1.0, 0.0).astype(jnp.bfloat16)
        select_ref[2 * start : 2 * (start + GROUP)] = match
    row = lax.broadcasted_iota(jnp.int32, (2 * GROUP, half), 0)
    sign = jnp.where((kind == 0) | (kind == 2), 1.0, -1.0)
    turns = jnp.where((row == 0) == (kind < 2), sign, 0.0)
    turns = jnp.where(row < 2, turns, 0.0).astype(jnp.bfloat16)
    lanes = select_ref.shape[0] // 2
    groups = pl.cdiv(pair_local, GROUP)
    used = low_ref.shape[0] // pair_local // 2 * groups * 2 * GROUP
    late = select_ref[lanes:]
    turn_ref[...] = lax.dot_general(turns, late, NT, preferred_element_type=jnp.float32)
    even, odd = table_ref[0], table_ref[1]
    both = (
        jnp.concatenate([even[: half // 2], odd[half // 2 :]], axis=0),
        jnp.concatenate([even[half // 2 :], odd[: half // 2]], axis=0),
    )
    for part, table in enumerate(both):
        turned_ref[part * lanes : part * lanes + used] = lax.dot_general(
            late[:used], table, NN, preferred_element_type=jnp.float32
        ).astype(jnp.bfloat16)
        if used < lanes:
            turned_ref[part * lanes + used : (part + 1) * lanes] = jnp.zeros(
                (lanes - used, table.shape[1]), jnp.bfloat16
            )


def plan(tables, pair_low, dep_lat, dep_col, lon_steps, tilt_steps, pair_local, lat_dev, slots, half):
    operands = (pair_low, dep_lat, dep_col, lon_steps, tilt_steps)
    integer = jax.ShapeDtypeStruct(lon_steps.shape, jnp.int32)
    fraction = jax.ShapeDtypeStruct(lon_steps.shape, jnp.float32)
    outs = [
        jax.ShapeDtypeStruct((2 * slots, half), jnp.bfloat16),
        jax.ShapeDtypeStruct((2 * slots, tables.shape[2]), jnp.bfloat16),
        jax.ShapeDtypeStruct((2 * GROUP, slots), jnp.float32),
        integer,
        integer,
        fraction,
        fraction,
        fraction,
    ]
    return pl.pallas_call(
        functools.partial(plan_kernel, pair_local, lat_dev),
        in_specs=[pl.BlockSpec(memory_space=pltpu.VMEM)]
        + [pl.BlockSpec(memory_space=pltpu.HBM)] * len(operands),
        out_specs=[pl.BlockSpec(memory_space=pltpu.VMEM)] * len(outs),
        out_shape=outs,
        scratch_shapes=[
            pltpu.SMEM(pair_low.shape, jnp.int32),
            pltpu.SMEM(dep_lat.shape, jnp.int32),
            pltpu.SMEM(dep_col.shape, jnp.int32),
            pltpu.VMEM(lon_steps.shape, jnp.int32),
            pltpu.VMEM(tilt_steps.shape, jnp.int32),
            pltpu.VMEM((slots, LANES), jnp.int32),
            pltpu.SemaphoreType.DMA((len(operands),)),
        ],
        compiler_params=pltpu.CompilerParams(vmem_limit_bytes=24 * MIB),
        cost_estimate=pl.CostEstimate(
            flops=10**7, bytes_accessed=4 * 10**6, transcendentals=0
        ),
        name="plan",
    )(tables, *[pltpu.with_memory_space_constraint(x, pltpu.HBM) for x in operands])


def fourier_tables(wavenumber_count):
    lon_count = 2 * wavenumber_count
    quarter = lon_count // 4
    whole = quarter // LANES * LANES
    tables = []
    for parity in range(2):
        kinds = ORDER[2 * parity : 2 * parity + 2]
        wave = np.concatenate([np.arange(kind, wavenumber_count, 4) for kind in kinds])
        phase = wave[:, None] * np.arange(quarter)[None, :] % lon_count
        angle = phase * (2.0 * math.pi / lon_count)
        weight = np.where(wave == 0, 1.0, 2.0)[:, None]
        parts = [weight * np.cos(angle), -weight * np.sin(angle)]
        tables.append(np.concatenate(parts if parity == 0 else parts[::-1], axis=0))
    exact = np.stack(tables)
    high = exact.astype(ml_dtypes.bfloat16)
    low = (exact - high.astype(np.float64)).astype(ml_dtypes.bfloat16)
    return np.concatenate(
        [high[..., :whole], low[..., :whole], high[..., whole:], low[..., whole:]], axis=2
    )


def add_halves(product, start, count):
    high = product[start : start + count]
    low = product[start + count : start + 2 * count]
    whole = (product.shape[1] - LANES) // 2
    tail = high[:, 2 * whole :]
    tail = tail + (low[:, 2 * whole :] + pltpu.roll(tail, LANES // 2, 1))
    pieces = [
        high[:, at : at + LANES] + (low[:, at : at + LANES] + high[:, whole + at : whole + at + LANES])
        for at in range(0, whole, LANES)
    ]
    return pieces + [tail]


def join(first, second):
    lane = lax.broadcasted_iota(jnp.int32, first[0].shape, 1)
    rolled = [pltpu.roll(piece, LANES // 2, 1) for piece in second]
    before = [first[-1], *rolled[:-1]]
    return first[:-1] + [
        jnp.where(lane < LANES // 2, a, b) for a, b in zip(before, rolled, strict=True)
    ]


def regroup(pieces, level, lane):
    piece_lanes = LANES // 8
    upper = lane // piece_lanes >= 4
    if level == 0:
        pieces = [
            jnp.where(upper, pltpu.roll(pieces[i + 4], 4 * piece_lanes, 1), pieces[i])
            for i in range(4)
        ]
    else:
        pieces = [
            jnp.where(upper, pieces[i + 4], pltpu.roll(pieces[i], 4 * piece_lanes, 1))
            for i in range(4)
        ]
    for bit in (1, 2):
        upper = (lane // piece_lanes & bit) != 0
        for one in range(4):
            if one & bit:
                continue
            a, b = pieces[one], pieces[one | bit]
            pieces[one] = jnp.where(upper, pltpu.roll(b, piece_lanes * bit, 1), a)
            pieces[one | bit] = jnp.where(
                upper, b, pltpu.roll(a, LANES - piece_lanes * bit, 1)
            )
    return pieces


def slot_matrix(level, lat_dev, piece_refs):
    ext = lat_dev + 2 * HALO
    ext_pad = pl.cdiv(ext, 8) * 8
    core = lax.axis_index("wave") % 2
    vectors = []
    order = chip_order(len(piece_refs))
    for ref in [piece_refs[order.index(step)] for step in range(len(piece_refs))]:
        source = ref[core]
        vectors += [
            source[start : start + ext_pad]
            for start in range(0, source.shape[0] - ext_pad + 1, ext)
        ]
    vectors += [jnp.zeros_like(vectors[0])] * (-len(vectors) % 8)
    lane = lax.broadcasted_iota(jnp.int32, vectors[0].shape, 1)
    columns = [[] for _ in range(4)]
    for start in range(0, len(vectors), 8):
        for kind, piece in enumerate(regroup(vectors[start : start + 8], level, lane)):
            columns[kind].append(piece)
    matrix = jnp.concatenate([jnp.concatenate(c, axis=1) for c in columns], axis=0)
    return matrix


def ordered_part(level, lat_dev, piece_refs, half, select_ref):
    matrix = slot_matrix(level, lat_dev, piece_refs)
    high, low = split(matrix)
    count = high.shape[0] // 2
    lanes = matrix.shape[1]
    return lax.dot_general(
        jnp.concatenate([high[:count], low[:count], high[count:], low[count:]], axis=0),
        select_ref[half * lanes : (half + 1) * lanes],
        NN,
        preferred_element_type=jnp.float32,
    )


def level_quarters(ordered, table_ref):
    count = ordered.shape[0] // 4
    half = ordered.shape[1]
    real = ordered[: 2 * count]
    imag = pltpu.roll(ordered[2 * count :], half // 2, 1)
    lane = lax.broadcasted_iota(jnp.int32, real.shape, 1)
    first_half = lane < half // 2
    outer = (lane < half // 4) | (lane >= half // 4 * 3)
    even = jnp.where(first_half, real, imag)
    odd = jnp.where(first_half, imag, real)
    turned = pltpu.roll(odd, half // 2, 1)
    even_turned = jnp.where(first_half == outer, even, -even)
    odd_turned = jnp.where(outer, turned, -turned)
    products = [
        lax.dot_general(
            jnp.concatenate(rows, axis=0).astype(jnp.bfloat16),
            table_ref[parity],
            NN,
            preferred_element_type=jnp.float32,
        )
        for parity, rows in enumerate(((even, even_turned), (odd, odd_turned)))
    ]
    near, far = [
        [add_halves(product, start, count) for product in products] for start in (0, 2 * count)
    ]
    return [
        [a + b for a, b in zip(*near, strict=True)],
        [a + b for a, b in zip(*far, strict=True)],
        [a - b for a, b in zip(*near, strict=True)],
        [a - b for a, b in zip(*far, strict=True)],
    ]


def level_rows(quarters):
    return join(quarters[0], quarters[1]) + join(quarters[2], quarters[3])


def late_quarters(matrix, turned_ref, turn_ref):
    count = matrix.shape[0] // 2
    cosine = jnp.broadcast_to(turn_ref[0:1], (count, matrix.shape[1]))
    sine = jnp.broadcast_to(turn_ref[1:2], (count, matrix.shape[1]))
    square = cosine * cosine - sine * sine
    parts = [
        (part[:count].astype(jnp.float32), part[count:].astype(jnp.float32))
        for part in split(matrix)
    ]
    rows = []
    rows += [(re, im) for re, im in parts]
    rows += [(cosine * re - sine * im, cosine * im + sine * re) for re, im in parts]
    rows += [(square * re, square * im) for re, im in parts]
    rows += [(cosine * re + sine * im, cosine * im - sine * re) for re, im in parts]
    product = lax.dot_general(
        jnp.concatenate([jnp.concatenate(row, axis=1) for row in rows], axis=0).astype(
            jnp.bfloat16
        ),
        turned_ref[...],
        NN,
        preferred_element_type=jnp.float32,
    )
    return [add_halves(product, 2 * count * quarter, count) for quarter in range(4)]


def store_rows(rows, field_ref, level, lat_dev, near_ref):
    blocks = len(rows)
    count = rows[0].shape[0]
    for at, value in enumerate(rows):
        there = slice(at * LANES, (at + 1) * LANES)
        for hemi in range(2):
            start = hemi * (count // 2) + HALO
            field_ref[level, hemi * lat_dev : (hemi + 1) * lat_dev, there] = value[
                start : start + lat_dev
            ]
        for side in range(3):
            place = (at + 1 - side) % blocks
            near_ref[side, pl.ds(place, count, stride=blocks), :] = value


def interpolate(lat_dev, row_step, step, f, g, near_ref):
    blocks = row_step.shape[0] // (2 * lat_dev)
    ext_pad = near_ref.shape[1] // (2 * blocks)
    points = 2 * lat_dev * blocks
    point = lax.broadcasted_iota(jnp.int32, (points, LANES), 1)

    def line(side, j):
        return jnp.concatenate(
            [
                near_ref[side, pl.ds((hemi * ext_pad + j) * blocks, lat_dev * blocks), :]
                for hemi in range(2)
            ],
            axis=0,
        )

    lines = [[line(side, j) for j in range(2 * HALO + 1)] for side in range(3)]
    values = []
    for upper in range(2):
        picked = []
        for side in range(3):
            choice = lines[side][upper]
            for j in range(1, 2 * HALO):
                choice = jnp.where(row_step == j, lines[side][j + upper], choice)
            picked.append(choice)
        left = jnp.where(point >= LANES - 28, picked[0], picked[1])
        right = jnp.where(point < 28, picked[2], picked[1])
        for shift in range(2):
            place = (step + shift) & (LANES - 1)
            values.append(
                jnp.where(
                    point < LANES // 2,
                    jnp.take_along_axis(left, place, axis=1),
                    jnp.take_along_axis(right, place, axis=1),
                )
            )
    lower = (1.0 - f) * values[0] + f * values[1]
    higher = (1.0 - f) * values[2] + f * values[3]
    return (1.0 - g) * lower + g * higher


def early_kernel(lat_dev, piece_count, *refs):
    piece_refs = refs[:piece_count]
    select_ref, table_ref, quarters_ref, later_ref = refs[piece_count:]
    ordered = ordered_part(0, lat_dev, piece_refs, 0, select_ref)
    pieces = sum(level_quarters(ordered, table_ref), [])
    for index, piece in enumerate(pieces):
        quarters_ref[index] = piece
    for level in range(later_ref.shape[0]):
        later_ref[level] = ordered_part(level + 1, lat_dev, piece_refs, 0, select_ref)


def first_kernel(lat_dev, piece_count, *refs):
    piece_refs, plan_refs = refs[:piece_count], refs[piece_count + 3 : -3]
    quarters_ref, turned_ref, turn_ref = refs[piece_count : piece_count + 3]
    field_ref, horizontal_ref, near_ref = refs[-3:]
    matrix = slot_matrix(0, lat_dev, piece_refs)
    quarters = late_quarters(matrix, turned_ref, turn_ref)
    size = len(quarters[0])
    quarters = [
        [piece + quarters_ref[size * i + j] for j, piece in enumerate(quarter)]
        for i, quarter in enumerate(quarters)
    ]
    store_rows(level_rows(quarters), field_ref, 0, lat_dev, near_ref)
    horizontal_ref[...] = interpolate(lat_dev, *[ref[...] for ref in plan_refs], near_ref)


def later_kernel(lat_dev, piece_count, *refs):
    piece_refs, plan_refs = refs[:piece_count], refs[piece_count + 3 : -9]
    early_ref, select_ref, table_ref = refs[piece_count : piece_count + 3]
    vertical_ref, below_ref, first_ref = refs[-9:-6]
    field_hbm, departed_ref, horizontal_ref, field_ref, near_ref, sems = refs[-6:]
    copies = [pltpu.make_async_copy(first_ref, field_hbm.at[pl.ds(0, 1)], sems.at[0])]
    copies[0].start()
    vertical = vertical_ref[...]
    below = below_ref[...]
    plans = [ref[...] for ref in plan_refs]
    for level in range(1, departed_ref.shape[0] + 1):
        ordered = early_ref[level - 1]
        ordered = ordered + ordered_part(level, lat_dev, piece_refs, 1, select_ref)
        rows = level_rows(level_quarters(ordered, table_ref))
        store_rows(rows, field_ref, level - 1, lat_dev, near_ref)
        copy = pltpu.make_async_copy(
            field_ref.at[pl.ds(level - 1, 1)], field_hbm.at[pl.ds(level, 1)], sems.at[level]
        )
        copy.start()
        copies.append(copy)
        horizontal = interpolate(lat_dev, *plans, near_ref)
        departed_ref[level - 1] = (1.0 - vertical) * below + vertical * horizontal
        below = horizontal
    horizontal_ref[...] = below
    for copy in copies:
        copy.wait()


def last_kernel(below_ref, *refs):
    *above_refs, vertical_ref, out_ref = refs
    lev = lax.axis_index("lev")
    is_last = lev == lax.axis_size("lev") - 1
    vertical = vertical_ref[...]
    below = below_ref[...]
    above = below
    for color, above_ref in enumerate(above_refs):
        above = jnp.where(lev % COLORS == color, above_ref[...], above)
    above = jnp.where(is_last, below, above)
    out_ref[...] = (1.0 - vertical) * below + vertical * above


def per_device(legendre, spectral, pair_low, dep_lat, dep_col, lon_steps, tilt_steps):
    pair_local, level_count, _, slot_count = spectral.shape
    wavenumber_count = slot_count - 1
    lon_count = 2 * wavenumber_count
    lat_all = legendre.shape[1]
    wave_size = lax.axis_size("wave")
    lat_dev = lat_all // wave_size
    slots = pl.cdiv(pair_local, GROUP) * GROUP
    extra = slots - pair_local
    if extra:
        spectral = jnp.pad(spectral, ((0, extra), (0, 0), (0, 0), (0, 0)))
        legendre = jnp.pad(legendre, ((0, extra), (0, 0), (0, 0)))
    tables = jnp.asarray(fourier_tables(wavenumber_count))
    parts, tables = legendre_sums(
        (pair_low, spectral, legendre, tables), pair_local, wave_size
    )
    received = [swap(part, 2 * step) if step else part for step, part in enumerate(parts)]
    select, turned, turn, *plans, vertical = plan(
        tables,
        pair_low,
        dep_lat,
        dep_col,
        lon_steps,
        tilt_steps,
        pair_local,
        lat_dev,
        2 * GROUP * half_vectors(wave_size // 2, slots // GROUP),
        wavenumber_count,
    )
    received[-1], select = lax.optimization_barrier((received[-1], select))
    blocks = lon_count // LANES
    points = 2 * lat_dev * blocks
    ext_pad = pl.cdiv(lat_dev + 2 * HALO, 8) * 8
    received = [received[step] for step in chip_order(len(received))]
    pieces = [swap(piece, 1) for piece in received]
    vmem = pl.BlockSpec(memory_space=pltpu.VMEM)
    params = pltpu.CompilerParams(vmem_limit_bytes=24 * MIB)
    quarter_pieces = 4 * pl.cdiv(lon_count // 4, LANES)
    quarters, early = pl.pallas_call(
        functools.partial(early_kernel, lat_dev, len(received)),
        in_specs=[vmem] * (len(received) + 2),
        out_specs=[vmem] * 2,
        out_shape=[
            jax.ShapeDtypeStruct((quarter_pieces, 2 * ext_pad, LANES), jnp.float32),
            jax.ShapeDtypeStruct(
                (level_count - 1, 8 * ext_pad, wavenumber_count), jnp.float32
            ),
        ],
        compiler_params=params,
        cost_estimate=pl.CostEstimate(
            flops=10**8, bytes_accessed=2 * 10**6, transcendentals=0
        ),
        name="early",
    )(*received, select, tables)
    first_operands = (*pieces, quarters, turned, turn, *plans)
    operands = (*pieces, early, select, tables, *plans)
    near = pltpu.VMEM((3, 2 * ext_pad * blocks, LANES), jnp.float32)
    flat = jax.ShapeDtypeStruct((points, LANES), jnp.float32)
    field_first, horizontal = pl.pallas_call(
        functools.partial(first_kernel, lat_dev, len(pieces)),
        in_specs=[vmem] * len(first_operands),
        out_specs=[vmem] * 2,
        out_shape=[jax.ShapeDtypeStruct((1, 2 * lat_dev, lon_count), jnp.float32), flat],
        scratch_shapes=[near],
        compiler_params=params,
        cost_estimate=pl.CostEstimate(
            flops=10**8, bytes_accessed=4 * 10**6, transcendentals=0
        ),
        name="first_level",
    )(*first_operands)
    above = [trade(horizontal, color) for color in range(COLORS)]
    levels = jax.ShapeDtypeStruct((level_count, 2 * lat_dev, lon_count), jnp.float32)
    grid_field, departed, top = pl.pallas_call(
        functools.partial(later_kernel, lat_dev, len(pieces)),
        in_specs=[vmem] * (len(operands) + 3),
        out_specs=[pl.BlockSpec(memory_space=pltpu.HBM), vmem, vmem],
        out_shape=[
            levels,
            jax.ShapeDtypeStruct((level_count - 1, points, LANES), jnp.float32),
            flat,
        ],
        scratch_shapes=[
            pltpu.VMEM((level_count - 1, 2 * lat_dev, lon_count), jnp.float32),
            near,
            pltpu.SemaphoreType.DMA((level_count,)),
        ],
        compiler_params=params,
        cost_estimate=pl.CostEstimate(
            flops=10**8, bytes_accessed=4 * 10**6, transcendentals=0
        ),
        name="later_levels",
    )(*operands, vertical, horizontal, field_first)
    final = pl.pallas_call(
        last_kernel,
        in_specs=[vmem] * (COLORS + 2),
        out_specs=vmem,
        out_shape=flat,
        compiler_params=params,
        name="top_level",
    )(top, *above, vertical)
    departed = jnp.concatenate([departed, final[None]], axis=0)
    return grid_field, departed.reshape(level_count, 2 * lat_dev, lon_count)


def solution(mesh):
    return jax.shard_map(
        per_device,
        mesh=mesh,
        in_specs=(
            P("wave", None, None),
            P("wave", "lev", None, None),
            P(),
            P("wave"),
            P("wave"),
            P("wave", None),
            P("wave", None),
        ),
        out_specs=(P("lev", "wave", None), P("lev", "wave", None)),
        check_vma=False,
    )
```

```python
import functools
import math

import jax
import jax.numpy as jnp
import ml_dtypes
import numpy as np
from jax import lax
from jax.experimental import pallas as pl
from jax.experimental.pallas import tpu as pltpu
from jax.sharding import PartitionSpec as P

LANES = 128
GROUP = 8
HALO = 2
MIB = 1024 * 1024
FAR = -(2**20)
COLORS = 3
ORDER = (0, 2, 1, 3)
NT = (((1,), (1,)), ((), ()))
NN = (((1,), (0,)), ((), ()))


def split(value):
    high = value.astype(jnp.bfloat16)
    low = (value - high.astype(jnp.float32)).astype(jnp.bfloat16)
    return high, low


def widen(value, width):
    lane = lax.broadcasted_iota(jnp.int32, (value.shape[0], LANES), 1)
    full = value.shape[1] // LANES * LANES
    parts = [value[:, :full]]
    for start in range(full, value.shape[1]):
        column = jnp.broadcast_to(value[:, start : start + 1], lane.shape)
        parts.append(jnp.where(lane == start - full, column, 0.0))
    assert len(parts) <= 2 and full + LANES * (len(parts) - 1) == width
    return jnp.concatenate(parts, axis=1)


def half_vectors(chips, groups):
    return pl.cdiv(chips * groups, 8) * 8


def wave_rows(low_ref, wave, pair_local, waves_ref):
    row = lax.broadcasted_iota(jnp.int32, (GROUP, LANES), 0)
    groups = pl.cdiv(pair_local, GROUP)
    chips = low_ref.shape[0] // pair_local // 2
    count = half_vectors(chips, groups)
    for index in range(2 * count):
        half, place = divmod(index, count)
        chip, group = divmod(place, groups)
        value = jnp.full((GROUP, LANES), FAR, jnp.int32)
        if chip < chips:
            base = (wave ^ (2 * chip + half)) * pair_local + group * GROUP
            for slot in range(min(GROUP, pair_local - group * GROUP)):
                value = jnp.where(row == slot, low_ref[base + slot], value)
        waves_ref[index * GROUP : (index + 1) * GROUP] = value


def departure(wave, lat_dev, half, lat_ref, col_ref, lon, tilt, out_refs):
    row_step_ref, place_ref, lon_frac_ref, lat_frac_ref, vertical_ref = out_refs
    points = lon.shape[0]
    blocks = points // (2 * lat_dev)
    row = lax.broadcasted_iota(jnp.int32, lon.shape, 0)
    point = lax.broadcasted_iota(jnp.int32, lon.shape, 1)
    row_step = jnp.zeros(lon.shape, jnp.int32)
    col_step = jnp.zeros(lon.shape, jnp.int32)
    for index in range(points):
        own = wave * lat_dev + index // blocks % lat_dev - HALO
        row_step = jnp.where(row == index, lat_ref[index] - own, row_step)
        first = LANES * (index % blocks)
        col_step = jnp.where(row == index, col_ref[index] - first, col_step)
    col_step = jnp.where(col_step >= half, col_step - 2 * half, col_step)
    col_step = jnp.where(col_step < -half, col_step + 2 * half, col_step)
    quarters = 4 * col_step + lon - 12
    row_step_ref[...] = row_step
    place_ref[...] = point + (quarters >> 2)
    lon_frac_ref[...] = (quarters & 3).astype(jnp.float32) * 0.25
    lat_frac_ref[...] = (tilt & 3).astype(jnp.float32) * 0.25
    vertical_ref[...] = (tilt >> 2).astype(jnp.float32) * 0.25


def legendre_kernel(pair_local, lat_dev, *refs):
    low_hbm, spec_hbm, leg_hbm, table_hbm = refs[:4]
    *chip_refs, table_ref = refs[4:-7]
    low_ref, spec_ref, leg_ref, sums_ref, small_sem, spec_sem, leg_sem = refs[-7:]
    slots, lat_all, slot_count = leg_ref.shape
    level_count = spec_ref.shape[1]
    pair_total = low_ref.shape[0]
    ext = lat_dev + 2 * HALO
    width = pl.cdiv(slot_count, LANES) * LANES
    low_copy = pltpu.make_async_copy(low_hbm, low_ref, small_sem.at[0])
    table_copy = pltpu.make_async_copy(table_hbm, table_ref, small_sem.at[1])
    low_copy.start()
    groups = slots // GROUP
    bounds = sorted({0, min(2, groups), groups})
    copies = []
    for index, (start, stop) in enumerate(zip(bounds[:-1], bounds[1:], strict=True)):
        part = pl.ds(start * GROUP, (stop - start) * GROUP)
        pair = (
            pltpu.make_async_copy(leg_hbm.at[part], leg_ref.at[part], leg_sem.at[index]),
            pltpu.make_async_copy(spec_hbm.at[part], spec_ref.at[part], spec_sem.at[index]),
        )
        for copy in pair:
            copy.start()
        copies.append((start, pair))
    table_copy.start()
    wave = lax.axis_index("wave")
    slot_of_row = lax.broadcasted_iota(jnp.int32, (GROUP, LANES), 0)
    slot_pos = lax.broadcasted_iota(jnp.int32, (GROUP, width), 1)
    low_copy.wait()
    for index in range(groups):
        for at, pair in copies:
            if at == index:
                for copy in pair:
                    copy.wait()
        start = index * GROUP
        base = wave * pair_local + start
        first = jnp.zeros((GROUP, LANES), jnp.int32)
        for slot in range(GROUP):
            low = low_ref[jnp.minimum(base + slot, pair_total - 1)]
            first = jnp.where(slot_of_row == slot, slot_count - 1 - low, first)
        first = jnp.concatenate([first] * (width // LANES), axis=1)
        second = slot_pos >= first
        sign = (1 - 2 * ((slot_pos - jnp.where(second, first, 0)) & 1)).astype(jnp.float32)
        member = [jnp.where(second, 0.0, 1.0), jnp.where(second, 1.0, 0.0)]
        masks = [
            jnp.concatenate(member, axis=0).astype(jnp.bfloat16),
            jnp.concatenate([m * sign for m in member], axis=0).astype(jnp.bfloat16),
        ]
        highs, lows = [], []
        for level in range(level_count):
            for part in range(2):
                row = widen(spec_ref[pl.ds(start, GROUP), level, part, :], width)
                high, low = split(jnp.concatenate([row, row], axis=0))
                highs += [high * mask for mask in masks]
                lows += [low * mask for mask in masks]
        columns = jnp.concatenate(highs + lows, axis=0)
        count = columns.shape[0] // 2
        half = GROUP * lat_all
        table = leg_ref[pl.ds(start, GROUP)].reshape(half, slot_count)
        rows = jnp.concatenate(split(widen(table, width)), axis=0)
        crossed = lax.dot_general(rows, columns, NT, preferred_element_type=jnp.float32)
        crossed = (crossed[:half, :count] + crossed[:half, count:]) + (
            crossed[half:, :count] + crossed[half:, count:]
        )
        slot_of_lane = lax.broadcasted_iota(jnp.int32, (lat_all, count), 1) % GROUP
        sums = crossed[:lat_all]
        for slot in range(1, GROUP):
            block = crossed[slot * lat_all : (slot + 1) * lat_all]
            sums = jnp.where(slot_of_lane == slot, block, sums)
        edge = jnp.zeros((HALO, count), jnp.float32)
        padded = jnp.concatenate([edge, sums, edge], axis=0)
        here = slice(index * ext, (index + 1) * ext)
        for dest in range(sums_ref.shape[0]):
            sums_ref[dest, here] = padded[dest * lat_dev : dest * lat_dev + ext]
    used = groups * ext
    sums_ref[:, used:] = jnp.zeros_like(sums_ref[:, used:])
    for step, chip_ref in enumerate(chip_refs):
        dest = (wave // 2 ^ step) * 2
        for core in range(2):
            chip_ref[core] = sums_ref[dest + core]
    table_copy.wait()


def legendre_sums(operands, pair_local, wave_size):
    pair_low, spectral, legendre, tables = operands
    slots, level_count = spectral.shape[:2]
    lat_all = legendre.shape[1]
    lat_dev = lat_all // wave_size
    lanes = 8 * level_count * GROUP
    ext = lat_dev + 2 * HALO
    rows = pl.cdiv((slots // GROUP - 1) * ext + pl.cdiv(ext, 8) * 8, 8) * 8
    chips = wave_size // 2
    out = jax.ShapeDtypeStruct((2, rows, lanes), jnp.float32)
    outs = [out] * chips + [jax.ShapeDtypeStruct(tables.shape, tables.dtype)]
    results = pl.pallas_call(
        functools.partial(legendre_kernel, pair_local, lat_dev),
        in_specs=[pl.BlockSpec(memory_space=pltpu.HBM)] * len(operands),
        out_specs=[pl.BlockSpec(memory_space=pltpu.VMEM)] * len(outs),
        out_shape=outs,
        scratch_shapes=[
            pltpu.SMEM(pair_low.shape, jnp.int32),
            pltpu.VMEM(spectral.shape, jnp.float32),
            pltpu.VMEM(legendre.shape, jnp.float32),
            pltpu.VMEM((wave_size, rows, lanes), jnp.float32),
            pltpu.SemaphoreType.DMA((2,)),
            pltpu.SemaphoreType.DMA((2,)),
            pltpu.SemaphoreType.DMA((2,)),
        ],
        compiler_params=pltpu.CompilerParams(vmem_limit_bytes=24 * MIB),
        name="legendre",
    )(*[pltpu.with_memory_space_constraint(x, pltpu.HBM) for x in operands])
    return results[:chips], results[chips]


def chip_order(count):
    return [0, *range(count - 1, 0, -1)]


def swap(value, by):
    wave_size = lax.axis_size("wave")
    return lax.ppermute(value, "wave", [(i, i ^ by) for i in range(wave_size)])


def trade(value, color):
    lev_size, wave_size = lax.axis_size("lev"), lax.axis_size("wave")
    pairs = []
    for lev in range(lev_size):
        other = lev
        if lev % COLORS == color and lev + 1 < lev_size:
            other = lev + 1
        if lev > 0 and (lev - 1) % COLORS == color:
            other = lev - 1
        for wave in range(wave_size):
            there = other * wave_size + (wave ^ 1 if other == lev else wave)
            pairs.append((lev * wave_size + wave, there))
    return lax.ppermute(value, ("lev", "wave"), pairs)


def plan_kernel(pair_local, lat_dev, table_ref, *refs):
    sources = refs[:5]
    select_ref, turned_ref, turn_ref, *plan_refs = refs[5:-7]
    low_ref, lat_ref, col_ref, lon_ref, tilt_ref, waves_ref, sems = refs[-7:]
    copies = [
        pltpu.make_async_copy(there, here, sems.at[i])
        for i, (there, here) in enumerate(zip(sources, refs[-7:-2], strict=True))
    ]
    for copy in copies:
        copy.start()
    half = select_ref.shape[1]
    quarter = half // 4
    lane = lax.broadcasted_iota(jnp.int32, (2 * GROUP, half), 1)
    kind = sum((lane >= quarter * i).astype(jnp.int32) for i in range(1, 4))
    order = 4 * (lane - quarter * kind)
    for i, first in enumerate(ORDER):
        order = jnp.where(kind == i, order + first, order)
    wave = lax.axis_index("wave")
    for copy in copies:
        copy.wait()
    departure(wave, lat_dev, half, lat_ref, col_ref, lon_ref[...], tilt_ref[...], plan_refs)
    wave_rows(low_ref, wave, pair_local, waves_ref)
    for start in range(0, waves_ref.shape[0], GROUP):
        waves = waves_ref[start : start + GROUP]
        waves = jnp.concatenate([waves, half - 1 - waves], axis=0)
        waves = jnp.concatenate([waves] * (half // LANES), axis=1)
        match = jnp.where(waves == order, 1.0, 0.0).astype(jnp.bfloat16)
        select_ref[2 * start : 2 * (start + GROUP)] = match
    row = lax.broadcasted_iota(jnp.int32, (2 * GROUP, half), 0)
    sign = jnp.where((kind == 0) | (kind == 2), 1.0, -1.0)
    turns = jnp.where((row == 0) == (kind < 2), sign, 0.0)
    turns = jnp.where(row < 2, turns, 0.0).astype(jnp.bfloat16)
    lanes = select_ref.shape[0] // 2
    groups = pl.cdiv(pair_local, GROUP)
    used = low_ref.shape[0] // pair_local // 2 * groups * 2 * GROUP
    late = select_ref[lanes:]
    turn_ref[...] = lax.dot_general(turns, late, NT, preferred_element_type=jnp.float32)
    even, odd = table_ref[0], table_ref[1]
    both = (
        jnp.concatenate([even[: half // 2], odd[half // 2 :]], axis=0),
        jnp.concatenate([even[half // 2 :], odd[: half // 2]], axis=0),
    )
    for part, table in enumerate(both):
        turned_ref[part * lanes : part * lanes + used] = lax.dot_general(
            late[:used], table, NN, preferred_element_type=jnp.float32
        ).astype(jnp.bfloat16)
        if used < lanes:
            turned_ref[part * lanes + used : (part + 1) * lanes] = jnp.zeros(
                (lanes - used, table.shape[1]), jnp.bfloat16
            )


def plan(tables, pair_low, dep_lat, dep_col, lon_steps, tilt_steps, pair_local, lat_dev, slots, half):
    operands = (pair_low, dep_lat, dep_col, lon_steps, tilt_steps)
    integer = jax.ShapeDtypeStruct(lon_steps.shape, jnp.int32)
    fraction = jax.ShapeDtypeStruct(lon_steps.shape, jnp.float32)
    outs = [
        jax.ShapeDtypeStruct((2 * slots, half), jnp.bfloat16),
        jax.ShapeDtypeStruct((2 * slots, tables.shape[2]), jnp.bfloat16),
        jax.ShapeDtypeStruct((2 * GROUP, slots), jnp.float32),
        integer,
        integer,
        fraction,
        fraction,
        fraction,
    ]
    return pl.pallas_call(
        functools.partial(plan_kernel, pair_local, lat_dev),
        in_specs=[pl.BlockSpec(memory_space=pltpu.VMEM)]
        + [pl.BlockSpec(memory_space=pltpu.HBM)] * len(operands),
        out_specs=[pl.BlockSpec(memory_space=pltpu.VMEM)] * len(outs),
        out_shape=outs,
        scratch_shapes=[
            pltpu.SMEM(pair_low.shape, jnp.int32),
            pltpu.SMEM(dep_lat.shape, jnp.int32),
            pltpu.SMEM(dep_col.shape, jnp.int32),
            pltpu.VMEM(lon_steps.shape, jnp.int32),
            pltpu.VMEM(tilt_steps.shape, jnp.int32),
            pltpu.VMEM((slots, LANES), jnp.int32),
            pltpu.SemaphoreType.DMA((len(operands),)),
        ],
        compiler_params=pltpu.CompilerParams(vmem_limit_bytes=24 * MIB),
        cost_estimate=pl.CostEstimate(
            flops=10**7, bytes_accessed=4 * 10**6, transcendentals=0
        ),
        name="plan",
    )(tables, *[pltpu.with_memory_space_constraint(x, pltpu.HBM) for x in operands])


def fourier_tables(wavenumber_count):
    lon_count = 2 * wavenumber_count
    quarter = lon_count // 4
    whole = quarter // LANES * LANES
    tables = []
    for parity in range(2):
        kinds = ORDER[2 * parity : 2 * parity + 2]
        wave = np.concatenate([np.arange(kind, wavenumber_count, 4) for kind in kinds])
        phase = wave[:, None] * np.arange(quarter)[None, :] % lon_count
        angle = phase * (2.0 * math.pi / lon_count)
        weight = np.where(wave == 0, 1.0, 2.0)[:, None]
        parts = [weight * np.cos(angle), -weight * np.sin(angle)]
        tables.append(np.concatenate(parts if parity == 0 else parts[::-1], axis=0))
    exact = np.stack(tables)
    high = exact.astype(ml_dtypes.bfloat16)
    low = (exact - high.astype(np.float64)).astype(ml_dtypes.bfloat16)
    return np.concatenate(
        [high[..., :whole], low[..., :whole], high[..., whole:], low[..., whole:]], axis=2
    )


def add_halves(product, start, count):
    high = product[start : start + count]
    low = product[start + count : start + 2 * count]
    whole = (product.shape[1] - LANES) // 2
    tail = high[:, 2 * whole :]
    tail = tail + (low[:, 2 * whole :] + pltpu.roll(tail, LANES // 2, 1))
    pieces = [
        high[:, at : at + LANES] + (low[:, at : at + LANES] + high[:, whole + at : whole + at + LANES])
        for at in range(0, whole, LANES)
    ]
    return pieces + [tail]


def join(first, second):
    lane = lax.broadcasted_iota(jnp.int32, first[0].shape, 1)
    rolled = [pltpu.roll(piece, LANES // 2, 1) for piece in second]
    before = [first[-1], *rolled[:-1]]
    return first[:-1] + [
        jnp.where(lane < LANES // 2, a, b) for a, b in zip(before, rolled, strict=True)
    ]


def regroup(pieces, level, lane):
    piece_lanes = LANES // 8
    upper = lane // piece_lanes >= 4
    if level == 0:
        pieces = [
            jnp.where(upper, pltpu.roll(pieces[i + 4], 4 * piece_lanes, 1), pieces[i])
            for i in range(4)
        ]
    else:
        pieces = [
            jnp.where(upper, pieces[i + 4], pltpu.roll(pieces[i], 4 * piece_lanes, 1))
            for i in range(4)
        ]
    for bit in (1, 2):
        upper = (lane // piece_lanes & bit) != 0
        for one in range(4):
            if one & bit:
                continue
            a, b = pieces[one], pieces[one | bit]
            pieces[one] = jnp.where(upper, pltpu.roll(b, piece_lanes * bit, 1), a)
            pieces[one | bit] = jnp.where(
                upper, b, pltpu.roll(a, LANES - piece_lanes * bit, 1)
            )
    return pieces


def slot_matrix(level, lat_dev, piece_refs):
    ext = lat_dev + 2 * HALO
    ext_pad = pl.cdiv(ext, 8) * 8
    core = lax.axis_index("wave") % 2
    vectors = []
    order = chip_order(len(piece_refs))
    for ref in [piece_refs[order.index(step)] for step in range(len(piece_refs))]:
        source = ref[core]
        vectors += [
            source[start : start + ext_pad]
            for start in range(0, source.shape[0] - ext_pad + 1, ext)
        ]
    vectors += [jnp.zeros_like(vectors[0])] * (-len(vectors) % 8)
    lane = lax.broadcasted_iota(jnp.int32, vectors[0].shape, 1)
    columns = [[] for _ in range(4)]
    for start in range(0, len(vectors), 8):
        for kind, piece in enumerate(regroup(vectors[start : start + 8], level, lane)):
            columns[kind].append(piece)
    matrix = jnp.concatenate([jnp.concatenate(c, axis=1) for c in columns], axis=0)
    return matrix


def ordered_part(level, lat_dev, piece_refs, half, select_ref):
    matrix = slot_matrix(level, lat_dev, piece_refs)
    high, low = split(matrix)
    count = high.shape[0] // 2
    lanes = matrix.shape[1]
    return lax.dot_general(
        jnp.concatenate([high[:count], low[:count], high[count:], low[count:]], axis=0),
        select_ref[half * lanes : (half + 1) * lanes],
        NN,
        preferred_element_type=jnp.float32,
    )


def level_quarters(ordered, table_ref):
    count = ordered.shape[0] // 4
    half = ordered.shape[1]
    real = ordered[: 2 * count]
    imag = pltpu.roll(ordered[2 * count :], half // 2, 1)
    lane = lax.broadcasted_iota(jnp.int32, real.shape, 1)
    first_half = lane < half // 2
    outer = (lane < half // 4) | (lane >= half // 4 * 3)
    even = jnp.where(first_half, real, imag)
    odd = jnp.where(first_half, imag, real)
    turned = pltpu.roll(odd, half // 2, 1)
    even_turned = jnp.where(first_half == outer, even, -even)
    odd_turned = jnp.where(outer, turned, -turned)
    products = [
        lax.dot_general(
            jnp.concatenate(rows, axis=0).astype(jnp.bfloat16),
            table_ref[parity],
            NN,
            preferred_element_type=jnp.float32,
        )
        for parity, rows in enumerate(((even, even_turned), (odd, odd_turned)))
    ]
    near, far = [
        [add_halves(product, start, count) for product in products] for start in (0, 2 * count)
    ]
    return [
        [a + b for a, b in zip(*near, strict=True)],
        [a + b for a, b in zip(*far, strict=True)],
        [a - b for a, b in zip(*near, strict=True)],
        [a - b for a, b in zip(*far, strict=True)],
    ]


def level_rows(quarters):
    return join(quarters[0], quarters[1]) + join(quarters[2], quarters[3])


def late_quarters(matrix, turned_ref, turn_ref):
    count = matrix.shape[0] // 2
    cosine = jnp.broadcast_to(turn_ref[0:1], (count, matrix.shape[1]))
    sine = jnp.broadcast_to(turn_ref[1:2], (count, matrix.shape[1]))
    square = cosine * cosine - sine * sine
    parts = [
        (part[:count].astype(jnp.float32), part[count:].astype(jnp.float32))
        for part in split(matrix)
    ]
    rows = []
    rows += [(re, im) for re, im in parts]
    rows += [(cosine * re - sine * im, cosine * im + sine * re) for re, im in parts]
    rows += [(square * re, square * im) for re, im in parts]
    rows += [(cosine * re + sine * im, cosine * im - sine * re) for re, im in parts]
    product = lax.dot_general(
        jnp.concatenate([jnp.concatenate(row, axis=1) for row in rows], axis=0).astype(
            jnp.bfloat16
        ),
        turned_ref[...],
        NN,
        preferred_element_type=jnp.float32,
    )
    return [add_halves(product, 2 * count * quarter, count) for quarter in range(4)]


def store_rows(rows, field_ref, level, lat_dev, near_ref):
    blocks = len(rows)
    count = rows[0].shape[0]
    for at, value in enumerate(rows):
        there = slice(at * LANES, (at + 1) * LANES)
        for hemi in range(2):
            start = hemi * (count // 2) + HALO
            field_ref[level, hemi * lat_dev : (hemi + 1) * lat_dev, there] = value[
                start : start + lat_dev
            ]
        for side in range(3):
            place = (at + 1 - side) % blocks
            near_ref[side, pl.ds(place, count, stride=blocks), :] = value


def interpolate(lat_dev, row_step, step, f, g, near_ref):
    blocks = row_step.shape[0] // (2 * lat_dev)
    ext_pad = near_ref.shape[1] // (2 * blocks)
    points = 2 * lat_dev * blocks
    point = lax.broadcasted_iota(jnp.int32, (points, LANES), 1)

    def line(side, j):
        return jnp.concatenate(
            [
                near_ref[side, pl.ds((hemi * ext_pad + j) * blocks, lat_dev * blocks), :]
                for hemi in range(2)
            ],
            axis=0,
        )

    lines = [[line(side, j) for j in range(2 * HALO + 1)] for side in range(3)]
    values = []
    for upper in range(2):
        picked = []
        for side in range(3):
            choice = lines[side][upper]
            for j in range(1, 2 * HALO):
                choice = jnp.where(row_step == j, lines[side][j + upper], choice)
            picked.append(choice)
        left = jnp.where(point >= LANES - 28, picked[0], picked[1])
        right = jnp.where(point < 28, picked[2], picked[1])
        for shift in range(2):
            place = (step + shift) & (LANES - 1)
            values.append(
                jnp.where(
                    point < LANES // 2,
                    jnp.take_along_axis(left, place, axis=1),
                    jnp.take_along_axis(right, place, axis=1),
                )
            )
    lower = (1.0 - f) * values[0] + f * values[1]
    higher = (1.0 - f) * values[2] + f * values[3]
    return (1.0 - g) * lower + g * higher


def early_kernel(lat_dev, piece_count, *refs):
    piece_refs = refs[:piece_count]
    select_ref, table_ref, quarters_ref, later_ref = refs[piece_count:]
    ordered = ordered_part(0, lat_dev, piece_refs, 0, select_ref)
    pieces = sum(level_quarters(ordered, table_ref), [])
    for index, piece in enumerate(pieces):
        quarters_ref[index] = piece
    for level in range(later_ref.shape[0]):
        later_ref[level] = ordered_part(level + 1, lat_dev, piece_refs, 0, select_ref)


def first_kernel(lat_dev, piece_count, *refs):
    piece_refs, plan_refs = refs[:piece_count], refs[piece_count + 3 : -3]
    quarters_ref, turned_ref, turn_ref = refs[piece_count : piece_count + 3]
    field_ref, horizontal_ref, near_ref = refs[-3:]
    matrix = slot_matrix(0, lat_dev, piece_refs)
    quarters = late_quarters(matrix, turned_ref, turn_ref)
    size = len(quarters[0])
    quarters = [
        [piece + quarters_ref[size * i + j] for j, piece in enumerate(quarter)]
        for i, quarter in enumerate(quarters)
    ]
    store_rows(level_rows(quarters), field_ref, 0, lat_dev, near_ref)
    horizontal_ref[...] = interpolate(lat_dev, *[ref[...] for ref in plan_refs], near_ref)


def later_kernel(lat_dev, piece_count, *refs):
    piece_refs, plan_refs = refs[:piece_count], refs[piece_count + 3 : -9]
    early_ref, select_ref, table_ref = refs[piece_count : piece_count + 3]
    vertical_ref, below_ref, first_ref = refs[-9:-6]
    field_hbm, departed_ref, horizontal_ref, field_ref, near_ref, sems = refs[-6:]
    copies = [pltpu.make_async_copy(first_ref, field_hbm.at[pl.ds(0, 1)], sems.at[0])]
    copies[0].start()
    vertical = vertical_ref[...]
    below = below_ref[...]
    plans = [ref[...] for ref in plan_refs]
    for level in range(1, departed_ref.shape[0] + 1):
        ordered = early_ref[level - 1]
        ordered = ordered + ordered_part(level, lat_dev, piece_refs, 1, select_ref)
        rows = level_rows(level_quarters(ordered, table_ref))
        store_rows(rows, field_ref, level - 1, lat_dev, near_ref)
        copy = pltpu.make_async_copy(
            field_ref.at[pl.ds(level - 1, 1)], field_hbm.at[pl.ds(level, 1)], sems.at[level]
        )
        copy.start()
        copies.append(copy)
        horizontal = interpolate(lat_dev, *plans, near_ref)
        departed_ref[level - 1] = (1.0 - vertical) * below + vertical * horizontal
        below = horizontal
    horizontal_ref[...] = below
    for copy in copies:
        copy.wait()


def last_kernel(below_ref, *refs):
    *above_refs, vertical_ref, out_ref = refs
    lev = lax.axis_index("lev")
    is_last = lev == lax.axis_size("lev") - 1
    vertical = vertical_ref[...]
    below = below_ref[...]
    above = below
    for color, above_ref in enumerate(above_refs):
        above = jnp.where(lev % COLORS == color, above_ref[...], above)
    above = jnp.where(is_last, below, above)
    out_ref[...] = (1.0 - vertical) * below + vertical * above


def per_device(legendre, spectral, pair_low, dep_lat, dep_col, lon_steps, tilt_steps):
    pair_local, level_count, _, slot_count = spectral.shape
    wavenumber_count = slot_count - 1
    lon_count = 2 * wavenumber_count
    lat_all = legendre.shape[1]
    wave_size = lax.axis_size("wave")
    lat_dev = lat_all // wave_size
    slots = pl.cdiv(pair_local, GROUP) * GROUP
    extra = slots - pair_local
    if extra:
        spectral = jnp.pad(spectral, ((0, extra), (0, 0), (0, 0), (0, 0)))
        legendre = jnp.pad(legendre, ((0, extra), (0, 0), (0, 0)))
    tables = jnp.asarray(fourier_tables(wavenumber_count))
    parts, tables = legendre_sums(
        (pair_low, spectral, legendre, tables), pair_local, wave_size
    )
    received = [swap(part, 2 * step) if step else part for step, part in enumerate(parts)]
    select, turned, turn, *plans, vertical = plan(
        tables,
        pair_low,
        dep_lat,
        dep_col,
        lon_steps,
        tilt_steps,
        pair_local,
        lat_dev,
        2 * GROUP * half_vectors(wave_size // 2, slots // GROUP),
        wavenumber_count,
    )
    received[-1], select = lax.optimization_barrier((received[-1], select))
    blocks = lon_count // LANES
    points = 2 * lat_dev * blocks
    ext_pad = pl.cdiv(lat_dev + 2 * HALO, 8) * 8
    received = [received[step] for step in chip_order(len(received))]
    pieces = [swap(piece, 1) for piece in received]
    vmem = pl.BlockSpec(memory_space=pltpu.VMEM)
    params = pltpu.CompilerParams(vmem_limit_bytes=24 * MIB)
    quarter_pieces = 4 * pl.cdiv(lon_count // 4, LANES)
    quarters, early = pl.pallas_call(
        functools.partial(early_kernel, lat_dev, len(received)),
        in_specs=[vmem] * (len(received) + 2),
        out_specs=[vmem] * 2,
        out_shape=[
            jax.ShapeDtypeStruct((quarter_pieces, 2 * ext_pad, LANES), jnp.float32),
            jax.ShapeDtypeStruct(
                (level_count - 1, 8 * ext_pad, wavenumber_count), jnp.float32
            ),
        ],
        compiler_params=params,
        cost_estimate=pl.CostEstimate(
            flops=10**8, bytes_accessed=2 * 10**6, transcendentals=0
        ),
        name="early",
    )(*received, select, tables)
    first_operands = (*pieces, quarters, turned, turn, *plans)
    operands = (*pieces, early, select, tables, *plans)
    near = pltpu.VMEM((3, 2 * ext_pad * blocks, LANES), jnp.float32)
    flat = jax.ShapeDtypeStruct((points, LANES), jnp.float32)
    field_first, horizontal = pl.pallas_call(
        functools.partial(first_kernel, lat_dev, len(pieces)),
        in_specs=[vmem] * len(first_operands),
        out_specs=[vmem] * 2,
        out_shape=[jax.ShapeDtypeStruct((1, 2 * lat_dev, lon_count), jnp.float32), flat],
        scratch_shapes=[near],
        compiler_params=params,
        cost_estimate=pl.CostEstimate(
            flops=10**8, bytes_accessed=4 * 10**6, transcendentals=0
        ),
        name="first_level",
    )(*first_operands)
    above = [trade(horizontal, color) for color in range(COLORS)]
    levels = jax.ShapeDtypeStruct((level_count, 2 * lat_dev, lon_count), jnp.float32)
    grid_field, departed, top = pl.pallas_call(
        functools.partial(later_kernel, lat_dev, len(pieces)),
        in_specs=[vmem] * (len(operands) + 3),
        out_specs=[pl.BlockSpec(memory_space=pltpu.HBM), vmem, vmem],
        out_shape=[
            levels,
            jax.ShapeDtypeStruct((level_count - 1, points, LANES), jnp.float32),
            flat,
        ],
        scratch_shapes=[
            pltpu.VMEM((level_count - 1, 2 * lat_dev, lon_count), jnp.float32),
            near,
            pltpu.SemaphoreType.DMA((level_count,)),
        ],
        compiler_params=params,
        cost_estimate=pl.CostEstimate(
            flops=10**8, bytes_accessed=4 * 10**6, transcendentals=0
        ),
        name="later_levels",
    )(*operands, vertical, horizontal, field_first)
    final = pl.pallas_call(
        last_kernel,
        in_specs=[vmem] * (COLORS + 2),
        out_specs=vmem,
        out_shape=flat,
        compiler_params=params,
        name="top_level",
    )(top, *above, vertical)
    departed = jnp.concatenate([departed, final[None]], axis=0)
    return grid_field, departed.reshape(level_count, 2 * lat_dev, lon_count)


def solution(mesh):
    return jax.shard_map(
        per_device,
        mesh=mesh,
        in_specs=(
            P("wave", None, None),
            P("wave", "lev", None, None),
            P(),
            P("wave"),
            P("wave"),
            P("wave", None),
            P("wave", None),
        ),
        out_specs=(P("lev", "wave", None), P("lev", "wave", None)),
        check_vma=False,
    )
```
